32 devices in a mesh: blk: 4 (over z), batch: 8 (over y, x, core).
Axes of the slice: x: 2, y: 2, z: 4, core: 2. Of those that a mesh axis runs over, the one named last changes fastest.
Arguments:
- hidden_in: bfloat16 [8, 1024, 1024], P('batch', 'blk'), may hold values from -6 to 6
- key_mask: int32 [8, 1024], P('batch'), may hold values 0 or 1
- lengths: int32 [8], P('batch'), may hold values from 769 to 1024, as said below
- first_gain: bfloat16 [1024], P(('blk', 'batch')), may hold values from 0.5 to 1.5
- first_shift: bfloat16 [1024], P(('blk', 'batch')), may hold values from -1.1953125 to 1.1953125
- input_weight: bfloat16 [1024, 3072], P(('blk', 'batch')), may hold values from -0.1875 to 0.1875
- query_bias: bfloat16 [1024], P(('blk', 'batch')), may hold values from -1.1953125 to 1.1953125
- value_bias: bfloat16 [1024], P(('blk', 'batch')), may hold values from -1.1953125 to 1.1953125
- output_weight: bfloat16 [1024, 1024], P(('blk', 'batch')), may hold values from -0.75 to 0.75
- output_bias: bfloat16 [1024], P(('blk', 'batch')), may hold values from -1.1953125 to 1.1953125
- second_gain: bfloat16 [1024], P(('blk', 'batch')), may hold values from 0.5 to 1.5
- second_shift: bfloat16 [1024], P(('blk', 'batch')), may hold values from -1.1953125 to 1.1953125
- up_weight: bfloat16 [1024, 4096], P(('blk', 'batch')), may hold values from -0.1875 to 0.1875
- up_bias: bfloat16 [4096], P(('blk', 'batch')), may hold values from -1.1953125 to 1.1953125
- down_weight: bfloat16 [4096, 1024], P(('blk', 'batch')), may hold values from -0.09375 to 0.09375
- down_bias: bfloat16 [1024], P(('blk', 'batch')), may hold values from -1.1953125 to 1.1953125
- cotangent: bfloat16 [8, 1024, 1024], P('batch', 'blk'), may hold values from -6 to 6
Outputs:
- layer_out: bfloat16 [8, 1024, 1024], P('batch', 'blk')
- input_gradient: bfloat16 [8, 1024, 1024], P('batch', 'blk')
- first_gain_gradient: float32 [1024], P(('blk', 'batch'))
- first_shift_gradient: float32 [1024], P(('blk', 'batch'))
- input_weight_gradient: float32 [1024, 3072], P(('blk', 'batch'))
- query_bias_gradient: float32 [1024], P(('blk', 'batch'))
- value_bias_gradient: float32 [1024], P(('blk', 'batch'))
- output_weight_gradient: float32 [1024, 1024], P(('blk', 'batch'))
- output_bias_gradient: float32 [1024], P(('blk', 'batch'))
- second_gain_gradient: float32 [1024], P(('blk', 'batch'))
- second_shift_gradient: float32 [1024], P(('blk', 'batch'))
- up_weight_gradient: float32 [1024, 4096], P(('blk', 'batch'))
- up_bias_gradient: float32 [4096], P(('blk', 'batch'))
- down_weight_gradient: float32 [4096, 1024], P(('blk', 'batch'))
- down_bias_gradient: float32 [1024], P(('blk', 'batch'))
The draws below stay inside these ranges and needn't reach their ends.
Inputs may be any that keep to these rules, and one draw needn't show every extreme that they name: `lengths`: every sequence ends within its last 256 positions.
All inputs are finite; a program needn't handle non-finite values. No bound on the sum of `key_mask` on one device may be relied on, other than what follows from the above.
Results may differ from the reference program's by a relative error of at most 0.03.
Values may be sent and summed in bfloat16 or wider, within the bound.
No kernel may reach another device: no remote copies, remote signals or barrier semaphores. Data moves between devices by JAX's collectives and lax.ppermute only.
A program may use at most 96 MiB of HBM per device.

```python
import jax
import jax.numpy as jnp
from jax import lax

D = 1024
HEADS = 16
FF = 4096
SEQ_DEV = 256
LEN = 1024
BATCH = 8


def draw_lengths(key, part):
    key = jax.random.fold_in(key, 11)
    first_key, second_key = jax.random.split(key)
    shortest = LEN - SEQ_DEV + 1
    drawn = jax.random.randint(first_key, (BATCH,), shortest, LEN + 1)
    order = jax.random.permutation(second_key, BATCH)
    drawn = jnp.where(order == 0, LEN, drawn)
    drawn = jnp.where(order == 1, shortest, drawn)
    return drawn.astype(jnp.int32)


def place_ends(entries, own_key, low, top_value):
    shape = entries.shape
    place = [jax.random.randint(jax.random.fold_in(own_key, axis), (), 0, shape[axis]) for axis in range(len(shape))]
    entries = entries.at[tuple(place)].set(low)
    longest = shape.index(max(shape))
    place[longest] = (place[longest] + 1) % shape[longest]
    return entries.at[tuple(place)].set(top_value)


def shard_levels(rng, extent, cuts, smallest, top_value):
    factor_of = 1.0
    for axis_at, shards_of in cuts:
        heights = jax.random.uniform(jax.random.fold_in(jax.random.fold_in(rng, 6), axis_at), (shards_of,), jnp.float32, smallest / len(cuts), top_value / len(cuts))
        factor_of = factor_of * jnp.repeat(jnp.exp(heights), extent[axis_at] // shards_of).reshape((-1,) + (1,) * (len(extent) - 1 - axis_at))
    return factor_of


def noise(own_key, dims, deviation, limit, cuts=(), kind=jnp.bfloat16):
    array = deviation * jax.random.normal(own_key, dims, jnp.float32)
    if cuts:
        array = array * shard_levels(own_key, dims, cuts, -0.22, 0.18)
    return jnp.clip(array, -limit, limit).astype(kind)


def setup_inputs(seed: int = 0) -> dict:
    streams_of = jax.random.split(jax.random.key(seed), 18)
    hidden_in = noise(streams_of[0], (BATCH, LEN, D), 1.0, 6.0, ((0, 8), (1, 4)))
    key_mask = place_ends((jax.random.randint(streams_of[1], (BATCH, LEN), 0, 8) < 7).astype(jnp.int32), jax.random.fold_in(streams_of[1], 1), 0, 1)
    lengths = draw_lengths(jax.random.fold_in(streams_of[17], 71), 0)
    first_gain = jnp.clip(1.0 + 0.1 * jax.random.normal(streams_of[3], (D,), jnp.float32), 0.5, 1.5).astype(jnp.bfloat16)
    first_shift = noise(streams_of[4], (D,), 0.2, 1.1953125, ((0, 32),))
    input_weight = noise(streams_of[5], (D, 3 * D), D ** -0.5, 0.1875, ((0, 32),))
    query_bias = noise(streams_of[6], (D,), 0.2, 1.1953125, ((0, 32),))
    value_bias = noise(streams_of[7], (D,), 0.2, 1.1953125, ((0, 32),))
    output_weight = noise(streams_of[8], (D, D), (D // 16) ** -0.5, 0.75, ((0, 32),))
    output_bias = noise(streams_of[9], (D,), 0.2, 1.1953125, ((0, 32),))
    second_gain = jnp.clip(1.0 + 0.1 * jax.random.normal(streams_of[10], (D,), jnp.float32), 0.5, 1.5).astype(jnp.bfloat16)
    second_shift = noise(streams_of[11], (D,), 0.2, 1.1953125, ((0, 32),))
    up_weight = noise(streams_of[12], (D, FF), D ** -0.5, 0.1875, ((0, 32),))
    up_bias = noise(streams_of[13], (FF,), 0.2, 1.1953125, ((0, 32),))
    down_weight = noise(streams_of[14], (FF, D), FF ** -0.5, 0.09375, ((0, 32),))
    down_bias = noise(streams_of[15], (D,), 0.2, 1.1953125, ((0, 32),))
    cotangent = noise(streams_of[16], (BATCH, LEN, D), 1.0, 6.0, ((0, 8), (1, 4)))
    return dict(hidden_in=hidden_in, key_mask=key_mask, lengths=lengths, first_gain=first_gain, first_shift=first_shift, input_weight=input_weight, query_bias=query_bias, value_bias=value_bias, output_weight=output_weight, output_bias=output_bias, second_gain=second_gain, second_shift=second_shift, up_weight=up_weight, up_bias=up_bias, down_weight=down_weight, down_bias=down_bias, cotangent=cotangent)


EPSILON = 1e-05
SCORE_SCALE = 0.125
MASKED = -1e+30
HIGHEST = lax.Precision.HIGHEST

@jax.custom_vjp
def low(v):
    return lax.optimization_barrier(v.astype(jnp.bfloat16)).astype(jnp.float32)

@jax.custom_vjp
def low_back(v):
    return v

def low_keep(v):
    return (low(v), None)

def low_pass(kept, grad):
    return (grad,)

def back_keep(v):
    return (v, None)

def back_low(kept, grad):
    return (low(grad),)
low.defvjp(low_keep, low_pass)
low_back.defvjp(back_keep, back_low)

def normalize(values, gain, shift):
    average = lax.optimization_barrier(jnp.mean(values, axis=-1, keepdims=True))
    centred = values - average
    variance = lax.optimization_barrier(jnp.mean(centred * centred, axis=-1, keepdims=True))
    return centred * lax.rsqrt(variance + EPSILON) * gain + shift

def residual_layer(inputs, marks, length, params):
    gain_one, shift_one, joint_weight, bias_query, bias_value, out_weight, bias_out, gain_two, shift_two, weight_up, bias_up, weight_down, bias_down = params
    positions, model_width = inputs.shape
    head_size = model_width // HEADS
    normed_one = low(normalize(inputs, gain_one, shift_one))
    joint = jnp.dot(normed_one, joint_weight, precision=HIGHEST)
    joint = joint + jnp.concatenate([bias_query, jnp.zeros_like(bias_query), bias_value])
    joint = low(low_back(joint))
    queries = joint[:, :model_width].reshape(positions, HEADS, head_size)
    keys_all = joint[:, model_width:2 * model_width].reshape(positions, HEADS, head_size)
    values_all = joint[:, 2 * model_width:].reshape(positions, HEADS, head_size)
    scores = jnp.einsum('qhe,khe->hqk', queries, keys_all, precision=HIGHEST) * SCORE_SCALE
    scores = low_back(scores)
    places = jnp.arange(positions, dtype=jnp.int32)
    causal = places[None, :] <= places[:, None]
    itself = places[None, :] == places[:, None]
    valid = (marks > 0) & (places < length)
    keep = causal & (itself | valid[None, :])
    scores = jnp.where(keep[None], scores, MASKED)
    shifted = scores - lax.optimization_barrier(jnp.max(scores, axis=-1, keepdims=True))
    raised = jnp.exp(shifted)
    chances = low(raised / lax.optimization_barrier(jnp.sum(raised, axis=-1, keepdims=True)))
    attended = jnp.einsum('hqk,khe->qhe', chances, values_all, precision=HIGHEST).reshape(positions, model_width)
    attended = low(low_back(attended))
    branch = low_back(jnp.dot(attended, out_weight, precision=HIGHEST) + bias_out)
    middle = inputs + branch
    normed_two = low(normalize(middle, gain_two, shift_two))
    hidden_pre = low_back(jnp.dot(normed_two, weight_up, precision=HIGHEST) + bias_up)
    activated = low(jax.nn.gelu(hidden_pre, approximate=True))
    return middle + low_back(jnp.dot(activated, weight_down, precision=HIGHEST) + bias_down)

def reference(hidden_in, key_mask, lengths, first_gain, first_shift, input_weight, query_bias, value_bias, output_weight, output_bias, second_gain, second_shift, up_weight, up_bias, down_weight, down_bias, cotangent):
    params = tuple((p.astype(jnp.float32) for p in (first_gain, first_shift, input_weight, query_bias, value_bias, output_weight, output_bias, second_gain, second_shift, up_weight, up_bias, down_weight, down_bias)))
    inputs = hidden_in.astype(jnp.float32)
    checked = jax.checkpoint(residual_layer)

    def forward(values_in, weights):
        return lax.map(lambda item: checked(item[0], item[1], item[2], weights), (values_in, key_mask, lengths))
    outputs, pullback = jax.vjp(forward, inputs, params)
    places = jnp.arange(LEN, dtype=jnp.int32)
    row_live = (places[None, :] < lengths[:, None]).astype(jnp.float32)
    input_grads, grads = pullback(cotangent.astype(jnp.float32) * row_live[:, :, None])
    return (outputs.astype(jnp.bfloat16), input_grads.astype(jnp.bfloat16), grads[0], grads[1], grads[2], grads[3], grads[4], grads[5], grads[6], grads[7], grads[8], grads[9], grads[10], grads[11], grads[12])
```

```python
import functools

import jax
import jax.numpy as jnp
from jax import lax
from jax.experimental import pallas as pl
from jax.experimental.pallas import tpu as pltpu
from jax.sharding import PartitionSpec as P

HEADS = 16
EPSILON = 1e-05
SCORE_SCALE = 0.125
MASKED = -1e30
LANES = 128
AXES = ("blk", "batch")
F32 = jnp.float32
BF16 = jnp.bfloat16

NT = (((1,), (1,)), ((), ()))
NN = (((1,), (0,)), ((), ()))
TN = (((0,), (0,)), ((), ()))


def dot(a, b, dims=NN):
    return lax.dot_general(a, b, dims, preferred_element_type=F32)


def bits_of(size):
    return size.bit_length() - 1


def key_mask_terms(rows):
    key = lax.broadcasted_iota(jnp.int32, (rows, rows), 0)
    query = lax.broadcasted_iota(jnp.int32, (rows, rows), 1)
    return key < query, key == query


def attend_kernel(head, rows, q_ref, k_ref, v_ref, bias_ref, att_ref, wide_ref, lse_ref):
    length, width = q_ref.shape
    earlier, same = key_mask_terms(rows)
    lane = lax.broadcasted_iota(jnp.int32, (rows, width), 1)
    value_t = v_ref[...].astype(F32).T.astype(BF16)
    for j in range(length // rows):
        here = slice(j * rows, (j + 1) * rows)
        bias_here = bias_ref[here, :]
        for h in range(width // head):
            mine = (lane >= h * head) & (lane < (h + 1) * head)
            query = jnp.where(mine, q_ref[here, :].astype(F32) * SCORE_SCALE, 0.0).astype(BF16)
            inner = dot(k_ref[here, :], query, NT)
            inner = jnp.where(same, inner, jnp.where(earlier, inner + bias_here, MASKED))
            top = jnp.max(inner, axis=0, keepdims=True)
            if j:
                outer = dot(k_ref[: j * rows, :], query, NT) + bias_ref[: j * rows, :]
                top = jnp.maximum(top, jnp.max(outer, axis=0, keepdims=True))
            inner = jnp.exp(inner - top)
            total = jnp.sum(inner, axis=0, keepdims=True)
            if j:
                outer = jnp.exp(outer - top)
                total = total + jnp.sum(outer, axis=0, keepdims=True)
            share = 1.0 / total
            value_h = value_t[h * head : (h + 1) * head]
            out = dot(value_h[:, here], (inner * share).astype(BF16))
            if j:
                out = out + dot(value_h[:, : j * rows], (outer * share).astype(BF16))
            wide_ref[h * head : (h + 1) * head, here] = out
            lse_ref[0, h : h + 1, here] = top + jnp.log(total)
    att_ref[...] = wide_ref[...].T.astype(BF16)


def attend(joint, key_bias, head, rows):
    length, width = joint.shape
    width = width // 3
    pairs = width // LANES
    column = lambda part: pl.BlockSpec((length, LANES), lambda p: (0, part * pairs + p))
    return pl.pallas_call(
        functools.partial(attend_kernel, head, rows),
        grid=(pairs,),
        in_specs=[column(0), column(1), column(2), pl.BlockSpec((length, 1), lambda p: (0, 0))],
        out_specs=[
            pl.BlockSpec((length, LANES), lambda p: (0, p)),
            pl.BlockSpec((LANES, length), lambda p: (p, 0)),
            pl.BlockSpec((1, 8, length), lambda p: (p, 0, 0)),
        ],
        out_shape=[
            jax.ShapeDtypeStruct((length, width), BF16),
            jax.ShapeDtypeStruct((width, length), F32),
            jax.ShapeDtypeStruct((pairs, 8, length), F32),
        ],
        compiler_params=pltpu.CompilerParams(vmem_limit_bytes=40 * 2**20),
        name="attend",
    )(joint, joint, joint, key_bias)


def attend_back_kernel(
    head,
    rows,
    q_ref,
    k_ref,
    v_ref,
    slope_ref,
    wide_ref,
    lse_ref,
    bias_ref,
    dq_ref,
    dk_ref,
    dv_ref,
    key_sum,
    value_sum,
    query_t,
):
    length, width = q_ref.shape
    earlier, same = key_mask_terms(rows)
    lane = lax.broadcasted_iota(jnp.int32, (rows, width), 1)
    key_t = k_ref[...].astype(F32).T.astype(BF16)
    product = slope_ref[...].astype(F32).T * wide_ref[...]
    key_sum[...] = jnp.zeros_like(key_sum)
    value_sum[...] = jnp.zeros_like(value_sum)
    for j in range(length // rows):
        here = slice(j * rows, (j + 1) * rows)
        for h in range(width // head):
            mine = (lane >= h * head) & (lane < (h + 1) * head)
            query = jnp.where(mine, q_ref[here, :].astype(F32) * SCORE_SCALE, 0.0).astype(BF16)
            slope = jnp.where(mine, slope_ref[here, :].astype(F32), 0.0).astype(BF16)
            top = lse_ref[0, h : h + 1, here]
            delta = jnp.sum(product[h * head : (h + 1) * head, here], axis=0, keepdims=True)
            key_h = key_t[h * head : (h + 1) * head]
            back = None
            for part in (slice(0, j * rows), here) if j else (here,):
                scores = dot(k_ref[part, :], query, NT)
                if part is here:
                    scores = jnp.where(
                        same, scores, jnp.where(earlier, scores + bias_ref[part, :], MASKED)
                    )
                else:
                    scores = scores + bias_ref[part, :]
                chances = jnp.exp(scores - top)
                slopes = dot(v_ref[part, :], slope, NT)
                grads = (chances * (slopes - delta)).astype(BF16)
                value_sum[part, :] += dot(chances.astype(BF16), slope)
                key_sum[part, :] += dot(grads, query)
                term = dot(key_h[:, part], grads)
                back = term if back is None else back + term
            query_t[h * head : (h + 1) * head, here] = back * SCORE_SCALE
    dq_ref[...] = query_t[...].T.astype(BF16)
    dk_ref[...] = key_sum[...].astype(BF16)
    dv_ref[...] = value_sum[...].astype(BF16)


def attend_back(joint, slope, wide, lse, key_bias, head, rows):
    length, width = slope.shape
    pairs = width // LANES
    column = lambda part: pl.BlockSpec((length, LANES), lambda p: (0, part * pairs + p))
    return pl.pallas_call(
        functools.partial(attend_back_kernel, head, rows),
        grid=(pairs,),
        in_specs=[
            column(0),
            column(1),
            column(2),
            column(0),
            pl.BlockSpec((LANES, length), lambda p: (p, 0)),
            pl.BlockSpec((1, 8, length), lambda p: (p, 0, 0)),
            pl.BlockSpec((length, 1), lambda p: (0, 0)),
        ],
        out_specs=[column(0)] * 3,
        out_shape=[jax.ShapeDtypeStruct((length, width), BF16)] * 3,
        scratch_shapes=[
            pltpu.VMEM((length, LANES), F32),
            pltpu.VMEM((length, LANES), F32),
            pltpu.VMEM((LANES, length), F32),
        ],
        compiler_params=pltpu.CompilerParams(vmem_limit_bytes=40 * 2**20),
        name="attend_back",
    )(joint, joint, joint, slope, wide, lse, key_bias)


def centre(values):
    average = jnp.mean(values, axis=-1, keepdims=True)
    centred = values - average
    variance = jnp.mean(centred * centred, axis=-1, keepdims=True)
    scale = lax.rsqrt(variance + EPSILON)
    return centred * scale, scale


def norm_back(slope, normal, scale, gain):
    weighted = slope * gain
    return scale * (
        weighted
        - jnp.mean(weighted, axis=-1, keepdims=True)
        - normal * jnp.mean(weighted * normal, axis=-1, keepdims=True)
    )


GELU_A = 0.7978845608028654
GELU_B = 0.044715


def gelu_terms(pre):
    square = pre * pre
    bend = jnp.tanh(GELU_A * pre * (1.0 + GELU_B * square))
    half = 0.5 * (1.0 + bend)
    slope = half + 0.5 * pre * (1.0 - bend * bend) * (GELU_A * (1.0 + 3.0 * GELU_B * square))
    return pre * half, slope


def solution(mesh):
    nb, nt = mesh.shape["blk"], mesh.shape["batch"]
    devices = nb * nt
    group_size = nb // 2
    total_bits = bits_of(devices)
    plane_bits = list(range(1, bits_of(nt)))
    group_bits = list(range(bits_of(nt), bits_of(nt) + bits_of(group_size)))
    top_bit = total_bits - 1
    members = 2 * group_size

    def at_home(i):
        return (i // nt) // group_size == i % 2

    def send(value, route):
        return lax.ppermute(value, AXES, route)

    def flip(value, bit, who=None):
        return send(value, [(i, i ^ (1 << bit)) for i in range(devices) if who is None or who(i)])

    def mirror(i):
        return (nb - 1 - i // nt) * nt + i % nt

    def local(
        hidden_in,
        key_mask,
        lengths,
        first_gain,
        first_shift,
        input_weight,
        query_bias,
        value_bias,
        output_weight,
        output_bias,
        second_gain,
        second_shift,
        up_weight,
        up_bias,
        down_weight,
        down_bias,
        cotangent,
    ):
        rows, width = hidden_in.shape[1:]
        length = key_mask.shape[1]
        head = width // HEADS
        blk, lane_id = lax.axis_index("blk"), lax.axis_index("batch")
        index = blk * nt + lane_id
        core = lane_id % 2
        group, place = blk // group_size, blk % group_size
        member = place * 2 + core
        home = group == core
        share = width // members
        ff = up_weight.shape[1]
        piece = ff // devices

        def bit(b):
            return (index >> b) & 1

        def ordered(mine, theirs, side, axis):
            return jnp.where(
                side == 0,
                jnp.concatenate([mine, theirs], axis),
                jnp.concatenate([theirs, mine], axis),
            )

        def side_of(value, side, axis):
            lo, hi = jnp.split(value, 2, axis)
            return jnp.where(side == 0, lo, hi)

        def spread(value):
            return value.reshape((1,) * total_bits + value.shape)

        def join(value, b):
            return ordered(value, flip(value, b), bit(b), total_bits - 1 - b)

        def trade(value, b, a):
            lead, columns = value.shape[:-1], value.shape[-1]
            view = value.reshape(lead + (a, 2, columns // (2 * a)))
            keep = side_of(view, bit(b), -2).reshape(lead + (columns // 2,))
            give = side_of(view, 1 - bit(b), -2).reshape(lead + (columns // 2,))
            return ordered(keep, flip(give, b), bit(b), total_bits - 1 - b)

        def halve(value, b):
            axis = total_bits - 1 - b
            keep = side_of(value, bit(b), axis).astype(F32)
            give = side_of(value, 1 - bit(b), axis).astype(BF16)
            return keep + flip(give, b).astype(F32)

        def untrade(value, b, a):
            axis = total_bits - 1 - b
            keep = side_of(value, bit(b), axis).astype(BF16)
            give = side_of(value, 1 - bit(b), axis).astype(BF16)
            lead, columns = keep.shape[:-1], keep.shape[-1]
            keep = keep.reshape(lead + (a, 1, columns // a))
            theirs = flip(give, b).reshape(lead + (a, 1, columns // a))
            return ordered(keep, theirs, bit(b), -2).reshape(lead + (2 * columns,))

        own = hidden_in[0]

        def first_route(i):
            return i ^ (1 << group_bits[0]) if at_home(i) else mirror(i) ^ 1

        came = send(own, [(i, first_route(i)) for i in range(devices)])
        near = ordered(own, came, bit(group_bits[0]), 0)
        for b in group_bits[1:]:
            near = ordered(near, flip(near, b, at_home), bit(b), 0)
        far = came
        away = lambda i: not at_home(i)
        for b in group_bits:
            far = ordered(far, flip(far, b, away), 1 - bit(b), 0)
        swapped = flip(jnp.where(home, near, far), 0)
        near_full = jnp.where(home, near, swapped)
        far_full = jnp.where(home, swapped, far)
        inputs = ordered(near_full, far_full, group, 0)

        small = jnp.concatenate(
            [
                first_gain,
                first_shift,
                query_bias,
                value_bias,
                output_bias,
                second_gain,
                second_shift,
                down_bias,
                up_bias,
            ]
        ).reshape(1, -1)
        small = spread(small)
        for b in range(total_bits):
            small = join(small, b)
        small = small.reshape(devices, -1).astype(F32)
        each = width // devices
        gain_one, shift_one, bias_q, bias_v, bias_out, gain_two, shift_two, bias_down = (
            small[:, v * each : (v + 1) * each].reshape(width) for v in range(8)
        )
        bias_up = small[:, 8 * each :].reshape(2, group_size, nt // 2, 2, piece)
        bias_up = lax.dynamic_index_in_dim(bias_up, place, 1, False)
        bias_up = lax.dynamic_index_in_dim(bias_up, core, 2, False).reshape(-1)
        bias_q = lax.dynamic_index_in_dim(bias_q.reshape(members, share), member, 0, False)
        bias_v = lax.dynamic_index_in_dim(bias_v.reshape(members, share), member, 0, False)

        w_in = trade(spread(input_weight), 0, 3 * group_size)
        for b in reversed(group_bits):
            w_in = trade(w_in, b, 3)
        w_in = join(w_in, top_bit)
        for b in plane_bits:
            w_in = join(w_in, b)
        w_in = w_in.reshape(width, 3 * share)

        w_up = trade(spread(up_weight), 0, 2 * group_size * (nt // 2))
        for b in reversed(group_bits):
            w_up = trade(w_up, b, 2)
        w_up = join(w_up, top_bit)
        for b in plane_bits:
            w_up = join(w_up, b)
        w_up = w_up.reshape(width, ff // members)

        w_down = join(spread(down_weight), top_bit)
        for b in reversed(plane_bits):
            w_down = join(w_down, b)
        w_down = w_down.reshape(ff // members, width)

        w_out = spread(output_weight)
        for b in group_bits + [top_bit] + plane_bits[::-1] + [0]:
            w_out = join(w_out, b)
        w_out = w_out.reshape(width, width)

        places = jnp.arange(length, dtype=jnp.int32)
        valid = ((key_mask[0] > 0) & (places < lengths[0])).astype(F32).reshape(1, length)
        valid = jnp.where(home, valid, flip(valid, 0))
        key_bias = jnp.where(valid > 0.5, 0.0, MASKED).reshape(length, 1)
        normal_one, _ = centre(inputs.astype(F32))
        normed_one = (normal_one * gain_one + shift_one).astype(BF16)
        joint = dot(normed_one, w_in)
        joint = joint + jnp.concatenate([bias_q, jnp.zeros_like(bias_q), bias_v])
        joint = joint.astype(BF16)
        att, wide, lse = attend(joint, key_bias, head, rows)

        other = own
        for b in group_bits:
            other = ordered(other, flip(other, b, away), bit(b), 0)
        other = jnp.where(home, send(other, [(i, i ^ 1) for i in range(devices) if away(i)]), other)
        base = ordered(near_full, other, group, 0).astype(F32)
        live = first_live = (
            blk * rows + jnp.arange(rows, dtype=jnp.int32) < lengths[0]
        ).astype(F32)[:, None]
        grad_out = cotangent[0].astype(F32) * live
        grad_low = grad_out.astype(BF16)
        grad_down = grad_low
        for b in group_bits:
            grad_down = ordered(grad_down, flip(grad_down, b), bit(b), 0)
        grad_down = ordered(grad_down, flip(grad_down, 0), core, 0)

        att_halves = att.reshape(2, group_size * rows, share)
        near_att = side_of(att_halves, group, 0)[0]
        far_att = side_of(att_halves, 1 - group, 0)[0]
        far_att = send(far_att, [(i, mirror(i)) for i in range(devices)])
        near_att = near_att.reshape(-1, 1, 1, share)
        far_att = far_att.reshape(-1, 1, 1, share)
        for k, b in enumerate(group_bits):
            near_att = ordered(near_att, flip(near_att, b), bit(b), 1)
            far_att = ordered(far_att, flip(far_att, b), 1 - bit(b), 1)
        att_all = ordered(near_att, far_att, group, 0)
        att_all = ordered(att_all, flip(att_all, 0), core, 2).reshape(-1, width)

        middle = base + dot(att_all, w_out) + bias_out
        normal_two, _ = centre(middle)
        normed_two = (normal_two * gain_two + shift_two).astype(BF16)
        pre = dot(normed_two, w_up) + bias_up
        act, act_slope = gelu_terms(pre)
        act = act.astype(BF16)
        out_part = dot(act, w_down).astype(BF16)
        grad_act = dot(grad_down, w_down, NT)
        grad_pre = (grad_act * act_slope).astype(BF16)
        normed_two_part = dot(grad_pre, w_up, NT).astype(BF16)
        d_down = dot(act, grad_down, TN).astype(BF16)
        d_up = dot(normed_two, grad_pre, TN).astype(BF16)
        d_bias_up = jnp.sum(grad_pre.astype(F32), axis=0)

        def own_rows(value):
            value = value.reshape(2, group_size, rows, value.shape[-1])
            value = lax.dynamic_index_in_dim(value, core, 0, False)
            return lax.dynamic_index_in_dim(value, place, 0, False)

        def reduce_rows(value):
            value = value.reshape(2, group_size * rows, width)
            total = side_of(value, core, 0)[0].astype(F32)
            total = total + flip(side_of(value, 1 - core, 0)[0], 0).astype(F32)
            for b in reversed(group_bits):
                give = side_of(total, 1 - bit(b), 0).astype(BF16)
                total = side_of(total, bit(b), 0) + flip(give, b).astype(F32)
            return total

        grad_normed_two = reduce_rows(normed_two_part)
        middle_own = own_rows(middle)
        normal_own, scale_own = centre(middle_own)
        grad_middle = grad_out + norm_back(grad_normed_two, normal_own, scale_own, gain_two)
        d_gain_two = jnp.sum(grad_normed_two * normal_own, axis=0)
        d_shift_two = jnp.sum(grad_normed_two, axis=0)
        grad_branch = grad_middle.astype(BF16)
        grad_att = dot(grad_branch, w_out, NT).astype(BF16)

        slices = grad_att.reshape(rows, members, share)
        parts = []
        for r in range(members):
            part = lax.dynamic_index_in_dim(slices, blk ^ r, 1, False)

            def route(i):
                m = (i // nt) ^ r
                return ((i % 2) * group_size + m // 2) * nt + (i % nt) - i % 2 + m % 2

            parts.append(send(part, [(i, route(i)) for i in range(devices)]))
        slope = jnp.stack(parts)
        order = [slope]
        for b in range(bits_of(members)):
            view = slope.reshape((members >> (b + 1), 2, 1 << b) + slope.shape[1:])
            flipped = view[:, ::-1].reshape(slope.shape)
            slope = jnp.where((member >> b) & 1 == 0, slope, flipped)
        slope = slope.reshape(length, share)
        dq, dk, dv = attend_back(joint, slope, wide, lse, key_bias, head, rows)
        grad_joint = jnp.concatenate([dq, dk, dv], axis=1)
        d_in = dot(normed_one, grad_joint, TN).astype(BF16)
        joint_sum = jnp.sum(grad_joint.astype(F32), axis=0)
        normed_one_part = dot(grad_joint, w_in, NT)
        d_gain_one = jnp.sum(normed_one_part * normal_one, axis=0)
        d_shift_one = jnp.sum(normed_one_part, axis=0)
        halves = normed_one_part.reshape(2, group_size * rows, width)
        keep_side = jnp.where(home, group, 1 - group)
        total = side_of(halves, keep_side, 0)[0]
        total = total + flip(side_of(halves, 1 - keep_side, 0)[0].astype(BF16), 0).astype(F32)
        for b in reversed(group_bits):
            side = jnp.where(home, bit(b), 1 - bit(b))
            give = side_of(total, 1 - side, 0).astype(BF16)
            total = side_of(total, side, 0) + flip(give, b).astype(F32)
        came = send(
            total.astype(BF16), [(i, mirror(i) ^ 1) for i in range(devices) if away(i)]
        )
        grad_normed_one = jnp.where(home, total, came.astype(F32))
        normal_in, scale_in = centre(own.astype(F32))
        input_gradient = grad_middle + norm_back(grad_normed_one, normal_in, scale_in, gain_one)

        layer_out = middle_own + reduce_rows(out_part) + bias_down

        d_up = d_up.reshape((2,) * total_bits + (each, -1))
        for b in reversed(plane_bits):
            d_up = halve(d_up, b)
        d_up = halve(d_up, top_bit)
        for b in group_bits:
            d_up = untrade(d_up, b, 2)
        d_up = untrade(d_up, 0, 2 * group_size * (nt // 2)).reshape(each, ff)

        d_down = d_down.reshape(
            tuple(2 if b in plane_bits + [top_bit] else 1 for b in reversed(range(total_bits)))
            + (piece, width)
        )
        for b in plane_bits:
            d_down = halve(d_down, b)
        d_down = halve(d_down, top_bit).reshape(piece, width)

        d_out = dot(own_rows(att_all), grad_branch, TN).astype(BF16)
        d_out = d_out.reshape((2,) * total_bits + (each, width))
        for b in [0] + plane_bits + [top_bit] + group_bits:
            d_out = halve(d_out, b)
        d_out = d_out.reshape(each, width)

        d_in = d_in.reshape((2,) * total_bits + (each, -1))
        for b in reversed(plane_bits):
            d_in = halve(d_in, b)
        d_in = halve(d_in, top_bit)
        for b in group_bits:
            d_in = untrade(d_in, b, 3)
        d_in = untrade(d_in, 0, 3 * group_size).reshape(each, 3 * width)

        def at_member(value):
            empty = jnp.zeros((members, share), F32)
            return lax.dynamic_update_slice(empty, value[None], (member, 0)).reshape(width)

        d_up_bias = jnp.zeros((2, group_size, nt // 2, 2, piece), F32)
        d_up_bias = lax.dynamic_update_slice(
            d_up_bias,
            d_bias_up.reshape(2, 1, nt // 2, 1, piece),
            (0, place, 0, core, 0),
        )
        sums = jnp.concatenate(
            [
                value.reshape(devices, -1)
                for value in (
                    d_gain_one,
                    d_shift_one,
                    at_member(joint_sum[:share]),
                    at_member(joint_sum[2 * share :]),
                    jnp.sum(grad_branch.astype(F32), axis=0),
                    d_gain_two,
                    d_shift_two,
                    jnp.sum(grad_low.astype(F32), axis=0),
                    d_up_bias,
                )
            ],
            axis=1,
        )
        sums = sums.reshape((2,) * total_bits + (1, -1))
        for b in reversed(range(total_bits)):
            axis = total_bits - 1 - b
            sums = side_of(sums, bit(b), axis) + flip(side_of(sums, 1 - bit(b), axis), b)
        sums = sums.reshape(-1)
        vectors = [sums[v * each : (v + 1) * each] for v in range(8)]
        return (
            layer_out.astype(BF16)[None],
            input_gradient.astype(BF16)[None],
            vectors[0],
            vectors[1],
            d_in.astype(F32),
            vectors[2],
            vectors[3],
            d_out.astype(F32),
            vectors[4],
            vectors[5],
            vectors[6],
            d_up.astype(F32),
            sums[8 * each :],
            d_down.astype(F32),
            vectors[7],
        )

    vector, matrix = P(AXES), P(AXES, None)
    tokens = P("batch", "blk", None)
    return jax.shard_map(
        local,
        mesh=mesh,
        in_specs=(
            tokens,
            P("batch", None),
            P("batch"),
            vector,
            vector,
            matrix,
            vector,
            vector,
            matrix,
            vector,
            vector,
            vector,
            matrix,
            vector,
            matrix,
            vector,
            tokens,
        ),
        out_specs=(
            tokens,
            tokens,
            vector,
            vector,
            matrix,
            vector,
            vector,
            matrix,
            vector,
            vector,
            vector,
            matrix,
            vector,
            matrix,
            vector,
        ),
        check_vma=False,
    )
```

```python
import functools

import jax
import jax.numpy as jnp
from jax import lax
from jax.experimental import pallas as pl
from jax.experimental.pallas import tpu as pltpu
from jax.sharding import PartitionSpec as P

HEADS = 16
EPSILON = 1e-05
SCORE_SCALE = 0.125
MASKED = -1e30
LANES = 128
AXES = ("blk", "batch")
F32 = jnp.float32
BF16 = jnp.bfloat16

NT = (((1,), (1,)), ((), ()))
NN = (((1,), (0,)), ((), ()))
TN = (((0,), (0,)), ((), ()))


def dot(a, b, dims=NN):
    return lax.dot_general(a, b, dims, preferred_element_type=F32)


def bits_of(size):
    return size.bit_length() - 1


def key_mask_terms(rows):
    key = lax.broadcasted_iota(jnp.int32, (rows, rows), 0)
    query = lax.broadcasted_iota(jnp.int32, (rows, rows), 1)
    return key < query, key == query


def centre(values):
    average = jnp.mean(values, axis=-1, keepdims=True)
    centred = values - average
    variance = jnp.mean(centred * centred, axis=-1, keepdims=True)
    scale = lax.rsqrt(variance + EPSILON)
    return centred * scale, scale


def norm_back(slope, normal, scale, gain):
    weighted = slope * gain
    return scale * (
        weighted
        - jnp.mean(weighted, axis=-1, keepdims=True)
        - normal * jnp.mean(weighted * normal, axis=-1, keepdims=True)
    )


GELU_A = 0.7978845608028654
GELU_B = 0.044715


def gelu_terms(pre):
    square = pre * pre
    bend = jnp.tanh(GELU_A * pre * (1.0 + GELU_B * square))
    half = 0.5 * (1.0 + bend)
    slope = half + 0.5 * pre * (1.0 - bend * bend) * (GELU_A * (1.0 + 3.0 * GELU_B * square))
    return pre * half, slope


EXTRA = 16


def shaped(shape, kind):
    return jax.ShapeDtypeStruct(shape, kind)


def token(value):
    corner = tuple(slice(0, 1) for _ in value.shape[:-2]) + (slice(0, 8), slice(0, LANES))
    return value[corner].reshape(8, LANES)


def kernel_call(
    body, outs, *args, name, smem=(), away=(), scratch=(), vmem=8, flops=0, after=()
):
    count = len(args)
    if after:
        inner = body
        body = lambda *refs: inner(*refs[:count], *refs[count + len(after) :])
    args = args + tuple(token(v) for v in after)

    def spec(i, places):
        if i in places:
            return pl.BlockSpec(memory_space=pl.ANY)
        return pl.BlockSpec(memory_space=pltpu.VMEM)

    ins = [
        pl.BlockSpec(memory_space=pltpu.SMEM) if i in smem else spec(i, away)
        for i in range(len(args))
    ]
    moved = sum(v.size * v.dtype.itemsize for v in args + tuple(outs))
    return pl.pallas_call(
        body,
        in_specs=ins,
        out_specs=[spec(i, ()) for i in range(len(outs))],
        out_shape=list(outs),
        scratch_shapes=list(scratch),
        compiler_params=pltpu.CompilerParams(vmem_limit_bytes=vmem * 2**20),
        cost_estimate=pl.CostEstimate(flops=flops, bytes_accessed=moved if flops else 0, transcendentals=0),
        name=name,
    )(*args)


def iota(shape, dim):
    return lax.broadcasted_iota(jnp.int32, shape, dim)


class Layout:
    def __init__(self, nb, nt, rows, width, ff, length):
        self.nb, self.nt, self.rows, self.width, self.ff, self.length = nb, nt, rows, width, ff, length
        self.devices = nb * nt
        self.size = nb // 2
        self.planes = nt // 2
        self.members = 2 * self.size
        self.each = width // self.devices
        self.piece = ff // self.devices
        self.share = width // self.members
        self.ff_share = ff // self.members
        self.small = 8 * self.each + self.piece
        self.valid_at = -(-self.small // 512) * 512
        self.head = width // HEADS


def each_way(flag, write):
    pl.when(flag == 0)(lambda: write(0))
    pl.when(flag == 1)(lambda: write(1))


def write_half(lay, side, count, in_from, up_from, in_start, up_start, give, keep, n):
    hw, pc = lay.share, lay.piece
    tail = lay.planes * pc if count > 0 else pc
    spans = []
    if count == 0:
        for q in range(3 * lay.size):
            spans.append((in_from, in_start + 2 * q * hw, hw))
        for q in range(2 * lay.size * lay.planes):
            spans.append((up_from, up_start + 2 * q * pc, pc))
    else:
        for q in range(3 * count // 2):
            spans.append((in_from, in_start + 2 * q * hw, hw))
        for q in range(count):
            spans.append((up_from, up_start + 2 * q * tail, tail))
    at = 0
    for source, start, span in spans:
        mine = source[0:n, start + side * span : start + (side + 1) * span]
        other = source[0:n, start + (1 - side) * span : start + (2 - side) * span]
        keep[0:n, at : at + span] = mine
        give[0:n, at : at + span] = other
        at += span


def load_all(pairs, sems):
    copies = [pltpu.make_async_copy(a, b, sems.at[i]) for i, (a, b) in enumerate(pairs)]
    for copy in copies:
        copy.start()
    return copies


def wait_all(copies):
    for copy in copies:
        copy.wait()


def pack_kernel(lay, spot, lengths, *refs):
    sources, (give, keep), targets, sems = refs[:12], refs[12:14], refs[14:26], refs[26]
    wait_all(load_all(list(zip(sources, targets, strict=True)), sems))
    w_in, w_up, mask = targets[:3]
    smalls = targets[3:]
    n = lay.each
    base = max(n, 16)
    if base > n:
        for ref in (give, keep):
            ref[0:base, :] = jnp.zeros((base, ref.shape[1]), BF16)
    each_way(spot[2], lambda side: write_half(lay, side, 0, w_in, w_up, 0, 0, give, keep, n))
    line = jnp.zeros((1, lay.small), F32)
    at = 0
    for ref in smalls:
        span = ref.shape[1]
        where = iota((span, lay.small), 1) == iota((span, lay.small), 0) + at
        line = line + dot(ref[...], where.astype(F32).astype(BF16))
        at += span
    row = iota((EXTRA, lay.small), 0) == spot[5]
    extra = jnp.where(row, line, 0.0).astype(BF16)
    live = (mask[...] > 0) & (iota(mask.shape, 1) < lengths[0])
    valid = jnp.where(live, 1.0, 0.0) * jnp.ones((EXTRA, 1), F32)
    for ref in (give, keep):
        ref[base : base + EXTRA, :] = jnp.zeros((EXTRA, ref.shape[1]), BF16)
        ref[base : base + EXTRA, 0 : lay.small] = extra
        ref[base : base + EXTRA, lay.valid_at : lay.valid_at + lay.length] = valid.astype(BF16)


def merge_rows(keep, came, side, n, out):
    if n < 16:
        mine, theirs = keep[0:16, :].astype(F32)[0:n], came[0:16, :].astype(F32)[0:n]
        first = jnp.where(side == 0, mine, theirs)
        second = jnp.where(side == 0, theirs, mine)
        out[...] = jnp.concatenate([first, second], axis=0).astype(BF16)
        return
    out[pl.ds(pl.multiple_of(side * n, n), n), :] = keep[0:n, :]
    out[pl.ds(pl.multiple_of((1 - side) * n, n), n), :] = came[0:n, :]


def merge_extra(lay, keep, came, n):
    n = max(n, 16)
    total = keep[n : n + EXTRA, 0 : lay.small].astype(F32) + came[n : n + EXTRA, 0 : lay.small].astype(F32)
    return total.astype(BF16)


def trade_kernel(lay, step, count, spot, keep, came, give, hold, valid, both):
    n = (1 << step) * lay.each
    merge_rows(keep, came, spot[2] if step == 0 else (spot[4] >> (step - 1)) & 1, n, both)
    start = 3 * count * lay.share
    each_way(
        (spot[4] >> step) & 1,
        lambda side: write_half(lay, side, count, both, both, 0, start, give, hold, 2 * n),
    )
    extra = merge_extra(lay, keep, came, n)
    for ref in (give, hold):
        ref[2 * n : 2 * n + EXTRA, :] = jnp.zeros((EXTRA, ref.shape[1]), BF16)
        ref[2 * n : 2 * n + EXTRA, 0 : lay.small] = extra
    if step == 0:
        place = slice(lay.valid_at, lay.valid_at + lay.length)
        base = max(n, 16)
        mine, theirs = (ref[base : base + 16, place].astype(F32)[0:8] for ref in (keep, came))
        valid[...] = jnp.where(spot[6] == 1, mine, theirs)
    else:
        valid[...] = jnp.zeros_like(valid)


def settle_kernel(lay, step, spot, keep, came, far, in_block, up_block, far_out, both):
    far_out[...] = far[...]
    n = (1 << step) * lay.each
    merge_rows(keep, came, (spot[4] >> (step - 1)) & 1, n, both)
    cut = 3 * lay.share
    in_block[0 : 2 * n, :] = both[:, 0:cut]
    up_block[...] = both[:, cut:]
    in_block[2 * n : 2 * n + EXTRA, :] = jnp.zeros((EXTRA, cut), BF16)
    in_block[2 * n : 2 * n + EXTRA, 0 : lay.small] = merge_extra(lay, keep, came, n)


def split_kernel(cut, mine, came, up, down, own, left, right, up_out, down_out, own_out):
    left[0], left[1] = mine[:, 0:cut], came[:, 0:cut]
    right[0], right[1] = mine[:, cut:], came[:, cut:]
    own_out[...] = own[...]
    if up_out.shape[0] == 2:
        up_out[0], up_out[1] = up[...], down[...]
    else:
        up_out[0] = up[...]
    down_out[...] = jnp.zeros_like(down_out) if up_out.shape[0] == 2 else down[...]


def stack_kernel(one, one_came, two, two_came, one_out, two_out):
    n = one.shape[0]
    one_out[0:n], one_out[n : 2 * n] = one[...], one_came[...]
    two_out[0:n], two_out[n : 2 * n] = two[...], two_came[...]


def stack(one, one_came, two, two_came, *after):
    outs = [shaped((2 * v.shape[0],) + v.shape[1:], BF16) for v in (one, two)]
    return kernel_call(
        stack_kernel, outs, one, one_came, two, two_came, name="stack", after=after
    )


def unpair_kernel(pair, came, ups, downs):
    ups[0], ups[1] = pair[0], came[0]
    downs[0], downs[1] = pair[1], came[1]


def block_spot(lay, spot, k, flipped):
    bits = bits_of(lay.planes)
    top = (spot[3] ^ k) & 1
    order = range(bits - 1, -1, -1) if flipped else range(bits)
    plane = spot[1] >> 1
    for position, b in enumerate(order):
        plane = plane ^ (((k >> (position + 1)) & 1) << b)
    return top, plane


def vector_kernel(lay, spot, first, second, out, rows, sems):
    n, count, wide = lay.members * lay.each, 2 * lay.planes, rows.shape[1]
    copies = []
    for k in range(count):
        source = first if k < count // 2 else second
        copy = pltpu.make_async_copy(
            source.at[k % (count // 2), n : n + EXTRA, 0:wide],
            rows.at[k * EXTRA : (k + 1) * EXTRA, :],
            sems.at[k],
        )
        copy.start()
        copies.append(copy)
    for copy in copies:
        copy.wait()
    out[...] = jnp.zeros_like(out)
    tall = count * EXTRA
    line, lane = iota((tall, lay.width), 0), iota((tall, lay.width), 1)
    holder, block = jnp.zeros_like(line), jnp.zeros_like(line)
    for k in range(count):
        top, plane = block_spot(lay, spot, k, False)
        inside = line - k * EXTRA
        here = (inside >= 0) & (inside < EXTRA)
        lead = (top * lay.size + inside // 2) * lay.nt + plane * 2 + inside % 2
        holder = jnp.where(here, jnp.where(inside < lay.members, lead, -1), holder)
        block = jnp.where(here & (inside == spot[5]), top * lay.planes + plane, jnp.where(here, -1, block))
    values = rows[...]
    source, target = iota((wide, lay.width), 0), iota((wide, lay.width), 1)
    for v in range(8):
        spread = (source == v * lay.each + target % lay.each).astype(F32).astype(BF16)
        tiled = jnp.where(lane // lay.each == holder, dot(values, spread), 0.0)
        out[v : v + 1, :] = jnp.sum(tiled, axis=0, keepdims=True)
    spread = (source == 8 * lay.each + target % lay.piece).astype(F32).astype(BF16)
    tiled = jnp.where(lane // lay.piece == block, dot(values, spread), 0.0)
    out[8:9, :] = jnp.sum(tiled, axis=0, keepdims=True)
    hw = lay.share
    mine = pl.ds(pl.multiple_of(spot[5] * hw, hw), hw)
    out[9:10, 0:hw] = out[2:3, mine]
    out[9:10, 2 * hw : 3 * hw] = out[3:4, mine]


def attend_kernel(lay, spot, bias, vecs, *refs):
    g, rows, hw, length, head = lay.size, lay.rows, lay.share, lay.length, lay.head
    near, far, near_c, far_c = (refs[i * g : (i + 1) * g] for i in range(4))
    weights = refs[4 * g : 4 * g + 4]
    near_att, far_att, joint, wide, lse, normed, x, w, x_sems, w_sems = refs[4 * g + 4 :]
    group, place = spot[3], spot[4]
    pending = []
    for e in range(g):
        for side, (at_home, at_away) in enumerate(((near[e], near_c[e]), (far_c[e], far[e]))):
            spot_here = (place if side == 0 else g - 1 - place) ^ e
            spot_here = (group if side == 0 else 1 - group) * g + spot_here
            target = x.at[pl.ds(pl.multiple_of(spot_here * rows, rows), rows), :]
            sem = x_sems.at[side * g + e]
            home = pltpu.make_async_copy(at_home, target, sem)
            visit = pltpu.make_async_copy(at_away, target, sem)
            pl.when(spot[6] == 1)(home.start)
            pl.when(spot[6] == 0)(visit.start)
            pending.append(home)
    count = 2 * lay.planes
    span = 2 * lay.each
    cut = weights[0].shape[-1]
    loads = []
    for k in range(count):
        for side in range(2):
            source = weights[2 * side + (k >= count // 2)]
            top, plane = block_spot(lay, spot, k, side == 1)
            for q in range(g):
                start = ((top * g + q) * lay.planes + plane) * span
                copy = pltpu.make_async_copy(
                    source.at[k % (count // 2), q * span : (q + 1) * span, :],
                    w.at[pl.ds(pl.multiple_of(start, span), span), 0:cut]
                    if side == 0
                    else w.at[pl.ds(pl.multiple_of(start, span), span), cut:],
                    w_sems.at[(k * 2 + side) * g + q],
                )
                copy.start()
                loads.append(copy)
    for copy in pending:
        copy.wait()
    for j in range(length // rows):
        here = slice(j * rows, (j + 1) * rows)
        normal, _ = centre(x[here, :].astype(F32))
        normed[here, :] = (normal * vecs[0:1, :] + vecs[1:2, :]).astype(BF16)
    for copy in loads:
        copy.wait()
    for j in range(length // rows):
        here = slice(j * rows, (j + 1) * rows)
        joint[here, :] = (dot(normed[here, :], w[...]) + vecs[9:10, 0 : 3 * hw]).astype(BF16)
    earlier, same = key_mask_terms(rows)
    lane = iota((rows, LANES), 1)
    for p in range(hw // LANES):
        q_at, k_at, v_at = (slice(i * hw + p * LANES, i * hw + (p + 1) * LANES) for i in range(3))
        value_t = joint[:, v_at].astype(F32).T.astype(BF16)
        for j in range(length // rows):
            here, past = slice(j * rows, (j + 1) * rows), slice(0, j * rows)
            bias_here = bias[here, :]
            for h in range(LANES // head):
                mine = (lane >= h * head) & (lane < (h + 1) * head)
                query = jnp.where(mine, joint[here, q_at].astype(F32) * SCORE_SCALE, 0.0).astype(BF16)
                inner = dot(joint[here, k_at], query, NT)
                inner = jnp.where(same, inner, jnp.where(earlier, inner + bias_here, MASKED))
                top = jnp.max(inner, axis=0, keepdims=True)
                if j:
                    outer = dot(joint[past, k_at], query, NT) + bias[past, :]
                    top = jnp.maximum(top, jnp.max(outer, axis=0, keepdims=True))
                inner = jnp.exp(inner - top)
                total = jnp.sum(inner, axis=0, keepdims=True)
                if j:
                    outer = jnp.exp(outer - top)
                    total = total + jnp.sum(outer, axis=0, keepdims=True)
                share = 1.0 / total
                value_h = value_t[h * head : (h + 1) * head]
                out = dot(value_h[:, here], (inner * share).astype(BF16))
                if j:
                    out = out + dot(value_h[:, past], (outer * share).astype(BF16))
                at = p * LANES + h * head
                wide[at : at + head, here] = out
                lse[p, h : h + 1, here] = top + jnp.log(total)
    for i in range(g):
        here = slice(i * rows, (i + 1) * rows)
        for out_ref, first in ((near_att, group * g + i), (far_att, (1 - group) * g + i)):
            part = wide[:, pl.ds(pl.multiple_of(first * rows, rows), rows)]
            out_ref[here, :] = part.T.astype(BF16)


def attend(lay, spot, bias, vecs, hidden, weights, later):
    d, hw, length, g = lay.width, lay.share, lay.length, lay.size
    outs = [
        shaped((g * lay.rows, hw), BF16),
        shaped((g * lay.rows, hw), BF16),
        shaped((length, 3 * hw), BF16),
        shaped((hw, length), F32),
        shaped((hw // LANES, 8, length), F32),
        shaped((length, d), BF16),
        shaped((length, d), BF16),
        shaped((d, 3 * hw), BF16),
    ]
    copies = 2 * lay.planes * 2 * g
    args = (spot, bias, vecs) + tuple(hidden) + tuple(weights)
    return kernel_call(
        functools.partial(attend_kernel, lay),
        outs,
        *args,
        name="attend",
        smem=(0,),
        away=tuple(range(3, len(args))),
        scratch=[
            pltpu.SemaphoreType.DMA((2 * g,)),
            pltpu.SemaphoreType.DMA((copies,)),
        ],
        vmem=60,
        flops=2 * length * d * 3 * hw + 3 * length * length * d // 2,
        after=(later,),
    )


def fold_kernel(slot, shift, a, b, spot, keep, came, hold, give):
    total = keep[...].astype(F32) + came[...].astype(F32)
    side = (spot[slot] >> shift) & 1
    view = total.reshape(a, 2, b, total.shape[-1])

    def write(s):
        hold[...] = view[:, s].reshape(a * b, -1).astype(BF16)
        give[...] = view[:, 1 - s].reshape(a * b, -1).astype(BF16)

    each_way(side, write)


def fold(spot, slot, shift, a, keep, came):
    count, columns = keep.shape
    b = count // (2 * a)
    return kernel_call(
        functools.partial(fold_kernel, slot, shift, a, b),
        [shaped((a * b, columns), BF16)] * 2,
        spot,
        keep,
        came,
        name="fold",
        smem=(0,),
    )


def mask_kernel(spot, lengths, cotangent, out):
    rows = out.shape[0]
    live = spot[0] * rows + iota((rows, 1), 0) < lengths[0]
    out[...] = jnp.where(live, cotangent[...].astype(F32), 0.0).astype(BF16)


def place_rows(lay, spot, e):
    return spot[4] ^ e


def weight_loads(lay, spot, ups, ups_came, downs, downs_came, w_up, w_down):
    pairs = []
    count, span, g = 2 * lay.planes, 2 * lay.each, lay.size
    for k in range(count):
        source = ups if k < count // 2 else ups_came
        top, plane = block_spot(lay, spot, k, False)
        for q in range(g):
            start = ((top * g + q) * lay.planes + plane) * span
            pairs.append(
                (
                    source.at[k % (count // 2), q * span : (q + 1) * span, :],
                    w_up.at[pl.ds(pl.multiple_of(start, span), span), :],
                )
            )
        source = downs if k < count // 2 else downs_came
        top, plane = block_spot(lay, spot, k, True)
        start = (top * lay.planes + plane) * lay.piece
        pairs.append(
            (
                source.at[k % (count // 2)],
                w_down.at[pl.ds(pl.multiple_of(start, lay.piece), lay.piece), :],
            )
        )
    return pairs


def row_loads(lay, spot, mine, swapped, target):
    pairs = []
    g, rows = lay.size, lay.rows
    for e in range(g):
        for source, sequence in ((mine[e], spot[2]), (swapped[e], 1 - spot[2])):
            start = (sequence * g + (spot[4] ^ e)) * rows
            pairs.append((source, target.at[pl.ds(pl.multiple_of(start, rows), rows), :]))
    return pairs


def forward_kernel(lay, spot, vecs, w_out, *refs):
    g, rows, hw, d = lay.size, lay.rows, lay.share, lay.width
    lists = [refs[i * g : (i + 1) * g] for i in range(8)]
    near, far, near_c, far_c, base_m, base_c, down_m, down_c = lists
    blocks = refs[8 * g : 8 * g + 4]
    (
        dn_keep,
        dn_give,
        middle_own,
        att_own,
        normed,
        act,
        grad_pre,
        bias_sum,
        att,
        wo,
        base,
        gd,
        w_up,
        w_down,
        sems,
    ) = refs[8 * g + 4 :]
    core, group, place = spot[2], spot[3], spot[4]
    span = g * rows
    pairs = [(w_out, wo)]
    for e in range(g):
        for source, sequence, at, side in (
            (near[e], group, place ^ e, core),
            (near_c[e], group, place ^ e, 1 - core),
            (far[e], 1 - group, (g - 1 - place) ^ e, core),
            (far_c[e], 1 - group, (g - 1 - place) ^ e, 1 - core),
        ):
            row = pl.multiple_of(sequence * span, span)
            column = pl.multiple_of((at * 2 + side) * hw, hw)
            pairs.append((source, att.at[pl.ds(row, span), pl.ds(column, hw)]))
    pairs += row_loads(lay, spot, base_m, base_c, base)
    first = len(pairs)
    pairs += weight_loads(lay, spot, *blocks, w_up, w_down)
    pairs += row_loads(lay, spot, down_m, down_c, gd)
    copies = load_all(pairs, sems)
    wait_all(copies[:first])
    bias_out, gain, shift = vecs[4:5, :], vecs[5:6, :], vecs[6:7, :]
    bias_up = vecs[8:9, 0 : lay.ff_share]
    total = jnp.zeros((1, lay.ff_share), F32)
    for i in range(2 * g):
        here = slice(i * rows, (i + 1) * rows)
        middle = base[here, :].astype(F32) + (dot(att[here, :], wo[...]) + bias_out)
        normal, _ = centre(middle)
        normed[here, :] = (normal * gain + shift).astype(BF16)

        @pl.when((core == i // g) & (place == i % g))
        def _():
            middle_own[...] = middle
            att_own[...] = att[here, :]

    wait_all(copies[first:])
    for i in range(2 * g):
        here = slice(i * rows, (i + 1) * rows)
        pre = dot(normed[here, :], w_up[...]) + bias_up
        value, slope = gelu_terms(pre)
        act[here, :] = value.astype(BF16)
        grad = (dot(gd[here, :], w_down[...], NT) * slope).astype(BF16)
        grad_pre[here, :] = grad
        total = total + jnp.sum(grad.astype(F32), axis=0, keepdims=True)
        back = dot(grad, w_up[...], NT).astype(BF16)
        at = slice((i % g) * rows, (i % g + 1) * rows)

        @pl.when(core == i // g)
        def _():
            dn_keep[at, :] = back

        @pl.when(core != i // g)
        def _():
            dn_give[at, :] = back

    bias_sum[...] = total


def forward_call(lay, spot, vecs, w_out, lists, blocks):
    d, f, rows, g = lay.width, lay.ff_share, lay.rows, lay.size
    tokens = 2 * g * rows
    outs = [
        shaped((g * rows, d), BF16),
        shaped((g * rows, d), BF16),
        shaped((rows, d), F32),
        shaped((rows, d), BF16),
        shaped((tokens, d), BF16),
        shaped((tokens, f), BF16),
        shaped((tokens, f), BF16),
        shaped((1, f), F32),
    ]
    args = (spot, vecs, w_out) + tuple(lists) + tuple(blocks)
    copies = 1 + 8 * g + 2 * lay.planes * (g + 1)
    return kernel_call(
        functools.partial(forward_kernel, lay),
        outs,
        *args,
        name="feed_forward",
        smem=(0,),
        away=tuple(range(2, len(args))),
        scratch=[
            pltpu.VMEM((tokens, d), BF16),
            pltpu.VMEM((d, d), BF16),
            pltpu.VMEM((tokens, d), BF16),
            pltpu.VMEM((tokens, d), BF16),
            pltpu.VMEM((d, f), BF16),
            pltpu.VMEM((f, d), BF16),
            pltpu.SemaphoreType.DMA((copies,)),
        ],
        vmem=60,
        flops=2 * tokens * d * (d + 3 * f),
    )


def cut_rows(value, side, a, b, keep, give):
    for i in range(a):
        for ref, s in ((keep, side), (give, 1 - side)):
            start = pl.multiple_of((2 * i + s) * b, b)
            ref[i * b : (i + 1) * b, :] = value[pl.ds(start, b), :]


def gradient_kernel(lay, spot, normed, act, grad_pre, *refs):
    g, rows, d, f = lay.size, lay.rows, lay.width, lay.ff_share
    down_m, down_c, blocks = refs[:g], refs[g : 2 * g], refs[2 * g : 2 * g + 2]
    up_keep, up_give, down_keep, down_give, out_keep, out_give, gd, w_down, full, sems = refs[
        2 * g + 2 :
    ]
    pairs = row_loads(lay, spot, down_m, down_c, gd)
    count = 2 * lay.planes
    for k in range(count):
        source = blocks[k >= count // 2]
        top, plane = block_spot(lay, spot, k, True)
        start = (top * lay.planes + plane) * lay.piece
        pairs.append(
            (
                source.at[k % (count // 2)],
                w_down.at[pl.ds(pl.multiple_of(start, lay.piece), lay.piece), :],
            )
        )
    copies = load_all(pairs, sems)
    tile = 256
    for i in range(d // tile):
        here = slice(i * tile, (i + 1) * tile)
        full[here, 0:f] = dot(normed[:, here], grad_pre[...], TN).astype(BF16)
    plane_bits = bits_of(lay.planes)
    side = (spot[1] >> plane_bits) & 1
    cut_rows(full.at[0:d, 0:f], side, 2 * g, d // (4 * g), up_keep, up_give)
    wait_all(copies)
    tile = min(256, f)
    for i in range(f // tile):
        here = slice(i * tile, (i + 1) * tile)
        full[here, 0:d] = dot(act[:, here], gd[...], TN).astype(BF16)
    side = (spot[1] >> 1) & 1
    cut_rows(full.at[0:f, 0:d], side, lay.planes, lay.piece, down_keep, down_give)
    for i in range(2 * g):
        here = slice(i * rows, (i + 1) * rows)
        at = slice((i % g) * rows, (i % g + 1) * rows)
        part = dot(act[here, :], w_down[...]).astype(BF16)

        @pl.when(spot[2] == i // g)
        def _():
            out_keep[at, :] = part

        @pl.when(spot[2] != i // g)
        def _():
            out_give[at, :] = part


def gradient_call(lay, spot, normed, act, grad_pre, down_m, down_c, blocks):
    d, f, rows, g = lay.width, lay.ff_share, lay.rows, lay.size
    tokens = 2 * g * rows
    outs = [shaped((d // 2, f), BF16)] * 2 + [shaped((f // 2, d), BF16)] * 2
    outs += [shaped((g * rows, d), BF16)] * 2
    args = (spot, normed, act, grad_pre) + tuple(down_m) + tuple(down_c) + tuple(blocks)
    return kernel_call(
        functools.partial(gradient_kernel, lay),
        outs,
        *args,
        name="gradients",
        smem=(0,),
        away=tuple(range(4, len(args))),
        scratch=[
            pltpu.VMEM((tokens, d), BF16),
            pltpu.VMEM((f, d), BF16),
            pltpu.VMEM((d, d), BF16),
            pltpu.SemaphoreType.DMA((2 * g + 2 * lay.planes,)),
        ],
        vmem=60,
        flops=2 * tokens * d * 3 * f,
    )


def turn_kernel(lay, spot, vecs, keep, came, middle, grad_low, w_out, *refs):
    pieces = refs[: lay.members]
    grad_middle, grad_branch, sums, wo, att_grad, sems = refs[lay.members :]
    copies = load_all([(w_out, wo)], sems)
    normal, scale = centre(middle[...])
    slope = keep[...].astype(F32) + came[...].astype(F32)
    total = grad_low[...].astype(F32) + norm_back(slope, normal, scale, vecs[5:6, :])
    grad_middle[...] = total
    branch = total.astype(BF16)
    grad_branch[...] = branch
    sums[...] = jnp.zeros_like(sums)
    add = lambda value: jnp.sum(value, axis=0, keepdims=True)
    sums[0:1, :] = add(branch.astype(F32))
    sums[1:2, :] = add(slope * normal)
    sums[2:3, :] = add(slope)
    sums[3:4, :] = add(grad_low[...].astype(F32))
    wait_all(copies)
    att_grad[...] = dot(branch, wo[...], NT).astype(BF16)
    for r in range(lay.members):
        start = pl.multiple_of((spot[0] ^ r) * lay.share, lay.share)
        pieces[r][...] = att_grad[:, pl.ds(start, lay.share)]


def turn_call(lay, spot, vecs, keep, came, middle, grad_low, w_out, later):
    d, rows = lay.width, lay.rows
    outs = [shaped((rows, lay.share), BF16)] * lay.members
    outs += [shaped((rows, d), F32), shaped((rows, d), BF16), shaped((8, d), F32)]
    return kernel_call(
        functools.partial(turn_kernel, lay),
        outs,
        spot,
        vecs,
        keep,
        came,
        middle,
        grad_low,
        w_out,
        name="turn",
        smem=(0,),
        away=(6,),
        scratch=[
            pltpu.VMEM((d, d), BF16),
            pltpu.VMEM((rows, d), BF16),
            pltpu.SemaphoreType.DMA((1,)),
        ],
        vmem=60,
        flops=2 * rows * d * d,
        after=(later,),
    )


def attend_back_kernel(lay, spot, bias, joint, wide, lse, normed, *refs):
    m, rows, hw, length, head, d = lay.members, lay.rows, lay.share, lay.length, lay.head, lay.width
    parts = refs[:m]
    (
        grads_out,
        left_keep,
        left_give,
        right_keep,
        right_give,
        sums,
        slope_all,
        key_sum,
        value_sum,
        query_t,
        full,
    ) = refs[m:]
    for r in range(m):
        start = pl.multiple_of((spot[5] ^ r) * rows, rows)
        slope_all[pl.ds(start, rows), :] = parts[r][...]
    earlier, same = key_mask_terms(rows)
    lane = iota((rows, LANES), 1)
    for p in range(hw // LANES):
        q_at, k_at, v_at = (slice(i * hw + p * LANES, i * hw + (p + 1) * LANES) for i in range(3))
        s_at = slice(p * LANES, (p + 1) * LANES)
        key_t = joint[:, k_at].astype(F32).T.astype(BF16)
        product = slope_all[:, s_at].astype(F32).T * wide[s_at, :]
        key_sum[...] = jnp.zeros_like(key_sum)
        value_sum[...] = jnp.zeros_like(value_sum)
        for j in range(length // rows):
            here = slice(j * rows, (j + 1) * rows)
            for h in range(LANES // head):
                mine = (lane >= h * head) & (lane < (h + 1) * head)
                query = jnp.where(mine, joint[here, q_at].astype(F32) * SCORE_SCALE, 0.0).astype(BF16)
                slope = jnp.where(mine, slope_all[here, s_at].astype(F32), 0.0).astype(BF16)
                top = lse[p, h : h + 1, here]
                delta = jnp.sum(product[h * head : (h + 1) * head, here], axis=0, keepdims=True)
                key_h = key_t[h * head : (h + 1) * head]
                back = None
                for part in (slice(0, j * rows), here) if j else (here,):
                    scores = dot(joint[part, k_at], query, NT)
                    if part is here:
                        scores = jnp.where(
                            same, scores, jnp.where(earlier, scores + bias[part, :], MASKED)
                        )
                    else:
                        scores = scores + bias[part, :]
                    chances = jnp.exp(scores - top)
                    slopes = dot(joint[part, v_at], slope, NT)
                    grads = (chances * (slopes - delta)).astype(BF16)
                    value_sum[part, :] += dot(chances.astype(BF16), slope)
                    key_sum[part, :] += dot(grads, query)
                    term = dot(key_h[:, part], grads)
                    back = term if back is None else back + term
                query_t[h * head : (h + 1) * head, here] = back * SCORE_SCALE
        grads_out[:, q_at] = query_t[...].T.astype(BF16)
        grads_out[:, k_at] = key_sum[...].astype(BF16)
        grads_out[:, v_at] = value_sum[...].astype(BF16)
    sums[...] = jnp.sum(grads_out[...].astype(F32), axis=0, keepdims=True)
    tile = 256
    for i in range(d // tile):
        here = slice(i * tile, (i + 1) * tile)
        full[here, :] = dot(normed[:, here], grads_out[...], TN).astype(BF16)
    cut = left_keep.shape[1]
    g = lay.size
    side = (spot[1] >> bits_of(lay.planes)) & 1
    cut_rows(full.at[:, 0:cut], side, 2 * g, d // (4 * g), left_keep, left_give)
    side = (spot[1] >> 1) & 1
    cut_rows(full.at[:, cut:], side, g * lay.planes, 2 * lay.each, right_keep, right_give)


def attend_back(lay, spot, bias, joint, wide, lse, normed, parts, cut):
    d, hw, length = lay.width, lay.share, lay.length
    outs = [shaped((length, 3 * hw), BF16)]
    outs += [shaped((d // 2, cut), BF16)] * 2 + [shaped((d // 2, 3 * hw - cut), BF16)] * 2
    outs += [shaped((1, 3 * hw), F32)]
    return kernel_call(
        functools.partial(attend_back_kernel, lay),
        outs,
        spot,
        bias,
        joint,
        wide,
        lse,
        normed,
        *parts,
        name="attend_back",
        smem=(0,),
        scratch=[
            pltpu.VMEM((length, hw), BF16),
            pltpu.VMEM((length, LANES), F32),
            pltpu.VMEM((length, LANES), F32),
            pltpu.VMEM((LANES, length), F32),
            pltpu.VMEM((d, 3 * hw), BF16),
        ],
        vmem=60,
        flops=2 * length * d * 3 * hw + 4 * length * length * d,
    )


def input_kernel(
    lay, spot, grads, w, x, sums_two, joint_sum, bias_up_sum, keep, give, sums, sums_low, vectors
):
    rows, g, hw = lay.rows, lay.size, lay.share
    gain = jnp.zeros((1, lay.width), F32)
    shift = jnp.zeros((1, lay.width), F32)
    for i in range(2 * g):
        here = slice(i * rows, (i + 1) * rows)
        part = dot(grads[here, :], w[...], NT)
        normal, _ = centre(x[here, :].astype(F32))
        gain = gain + jnp.sum(part * normal, axis=0, keepdims=True)
        shift = shift + jnp.sum(part, axis=0, keepdims=True)
        low = part.astype(BF16)
        at = slice((i % g) * rows, (i % g + 1) * rows)

        @pl.when(spot[8] == i // g)
        def _():
            keep[at, :] = low

        @pl.when(spot[8] != i // g)
        def _():
            give[at, :] = low

    vectors[...] = jnp.zeros_like(vectors)
    vectors[0:1, :] = gain
    vectors[1:2, :] = shift
    mine = pl.ds(pl.multiple_of(spot[5] * hw, hw), hw)
    vectors[2:3, mine] = joint_sum[:, 0:hw]
    vectors[3:4, mine] = joint_sum[:, 2 * hw :]
    vectors[4:8, :] = sums_two[0:4, :]
    each, piece, small = lay.each, lay.piece, lay.small
    device, lane = iota((lay.devices, lay.width), 0), iota((lay.devices, lay.width), 1)
    total = jnp.zeros((lay.devices, small), F32)
    source, target = iota((lay.width, small), 0), iota((lay.width, small), 1)
    for v in range(8):
        value = jnp.where(lane // each == device, vectors[v : v + 1, :], 0.0)
        move = (target == v * each + source % each).astype(F32)
        total = total + jnp.dot(value, move, precision=lax.Precision.HIGHEST)
    shape = (lay.devices, lay.ff_share)
    device, lane = iota(shape, 0), iota(shape, 1)
    plane, chip = device % lay.nt // 2, device // lay.nt
    block = chip // lay.size * lay.planes + plane
    here = (lane // piece == block) & (chip % lay.size == spot[4]) & (device % 2 == spot[2])
    source, target = iota((lay.ff_share, small), 0), iota((lay.ff_share, small), 1)
    move = (target == 8 * each + source % piece).astype(F32)
    value = jnp.where(here, bias_up_sum[...], 0.0)
    total = total + jnp.dot(value, move, precision=lax.Precision.HIGHEST)
    sums[...] = total
    sums_low[...] = total.astype(BF16)


def input_call(lay, spot, grads, w, x, sums_two, joint_sum, bias_up_sum):
    d, rows, g = lay.width, lay.rows, lay.size
    small = (lay.devices, lay.small)
    return kernel_call(
        functools.partial(input_kernel, lay),
        [shaped((g * rows, d), BF16)] * 2 + [shaped(small, F32), shaped(small, BF16)],
        spot,
        grads,
        w,
        x,
        sums_two,
        joint_sum,
        bias_up_sum,
        name="input_slope",
        smem=(0,),
        scratch=[pltpu.VMEM((8, d), F32)],
        vmem=60,
        flops=2 * lay.length * d * 3 * lay.share,
    )


def fold_into(spot, cut, keep, came, hold, give, rows=None):
    slot, shift, a = cut
    count = keep.shape[0]
    b = count // (2 * a)
    side = (spot[slot] >> shift) & 1
    half = a * b

    def write(s):
        for i in range(a):
            for ref, t in ((hold, s), (give, 1 - s)):
                at = slice((2 * i + t) * b, (2 * i + t + 1) * b)
                value = keep[at, :].astype(F32) + came[at, :].astype(F32)
                ref[i * b : (i + 1) * b, :] = value.astype(BF16)

    each_way(side, write)


def two_fold_kernel(cuts, spot, one, one_came, two, two_came, one_keep, one_give, two_keep, two_give):
    fold_into(spot, cuts[0], one, one_came, one_keep, one_give)
    fold_into(spot, cuts[1], two, two_came, two_keep, two_give)


def two_fold(spot, cuts, one, one_came, two, two_came):
    outs = []
    for v in (one, two):
        outs += [shaped((v.shape[0] // 2, v.shape[1]), BF16)] * 2
    return kernel_call(
        functools.partial(two_fold_kernel, cuts),
        outs,
        spot,
        one,
        one_came,
        two,
        two_came,
        name="two_fold",
        smem=(0,),
    )


def sums_fold_kernel(
    cuts, spot, one, one_came, two, two_came, sums, sums_came, one_keep, one_give, two_keep, two_give, sums_out
):
    n, half = one.shape[0], one_keep.shape[0]
    tall, small = sums.shape
    came = one_came[n : n + tall, 0:small] if one_came.shape[0] > n else sums_came[...]
    total = sums[...] + came.astype(F32)
    sums_out[...] = total
    fold_into(spot, cuts[0], one, one_came, one_keep, one_give)
    one_give[half : half + tall, :] = jnp.zeros((tall, one_give.shape[1]), BF16)
    one_give[half : half + tall, 0:small] = total.astype(BF16)
    fold_into(spot, cuts[1], two, two_came, two_keep, two_give)


def sums_fold(spot, cuts, one, one_came, two, two_came, sums, sums_came):
    half, other = one.shape[0] // 2, two.shape[0] // 2
    outs = [
        shaped((half, one.shape[1]), BF16),
        shaped((half + sums.shape[0], one.shape[1]), BF16),
        shaped((other, two.shape[1]), BF16),
        shaped((other, two.shape[1]), BF16),
        shaped(sums.shape, F32),
    ]
    args = (spot, one, one_came, two, two_came, sums, sums_came)
    return kernel_call(
        functools.partial(sums_fold_kernel, cuts), outs, *args, name="sums_fold", smem=(0,)
    )


def top_fold_kernel(shift, spot, one, one_came, two, two_came, sums, keep, give, sums_out):
    n, cut = one.shape
    half = n // 2
    tall, small = sums.shape
    total = sums[...] + one_came[n : n + tall, 0:small].astype(F32)
    sums_out[...] = total
    give[half : half + tall, :] = jnp.zeros((tall, give.shape[1]), BF16)
    give[half : half + tall, 0:small] = total.astype(BF16)

    def write(s):
        for here, x, y in ((slice(0, cut), one, one_came), (slice(cut, None), two, two_came)):
            for ref, t in ((keep, s), (give, 1 - s)):
                at = slice(t * half, (t + 1) * half)
                value = x[at, :].astype(F32) + y[at, :].astype(F32)
                ref[0:half, here] = value.astype(BF16)

    each_way((spot[0] >> shift) & 1, write)


def top_pair_kernel(shift, spot, one, one_came, two, two_came, one_keep, two_keep, give):
    half = one_keep.shape[0]

    def write(s):
        for i, (x, y, keep) in enumerate(((one, one_came, one_keep), (two, two_came, two_keep))):
            for ref, t in ((keep, s), (give.at[i], 1 - s)):
                at = slice(t * half, (t + 1) * half)
                ref[...] = (x[at, :].astype(F32) + y[at, :].astype(F32)).astype(BF16)

    each_way((spot[0] >> shift) & 1, write)


def home_first_kernel(slot, shift, spot, w_in, w_in_came, w_up, w_up_came, sums, keep, give, sums_out):
    n, cut = w_in.shape
    half = n // 2
    tall, small = sums.shape
    total = sums[...] + w_in_came[n : n + tall, 0:small].astype(F32)
    sums_out[...] = total
    give[half : half + tall, :] = jnp.zeros((tall, give.shape[1]), BF16)
    give[half : half + tall, 0:small] = total.astype(BF16)

    def write(s):
        for here, x, y in ((slice(0, cut), w_in, w_in_came), (slice(cut, None), w_up, w_up_came)):
            for ref, t in ((keep, s), (give, 1 - s)):
                at = slice(t * half, (t + 1) * half)
                value = x[at, :].astype(F32) + y[at, :].astype(F32)
                ref[0:half, here] = value.astype(BF16)

    each_way((spot[slot] >> shift) & 1, write)


def home_next_kernel(slot, shift, spot, mine, came, sums, keep, give, sums_out):
    n, columns = mine.shape
    half = n // 2
    tall, small = sums.shape
    total = sums[...] + came[n : n + tall, 0:small].astype(F32)
    sums_out[...] = total
    base = give.shape[0] - tall
    give[base : base + tall, :] = jnp.zeros((tall, give.shape[1]), BF16)
    give[base : base + tall, 0:small] = total.astype(BF16)

    def write(s):
        for here, x in ((slice(0, columns), mine), (slice(columns, None), came)):
            for ref, t in ((keep, s), (give, 1 - s)):
                ref[0:half, here] = x[t * half : (t + 1) * half, :]

    each_way((spot[slot] >> shift) & 1, write)


def home_last_kernel(lay, spot, mine, came, sums, w_in, w_up, *vectors):
    n = lay.each
    tall = lay.devices
    base = came.shape[0] - tall
    hw, piece, cut = lay.share, lay.piece, 3 * lay.share
    span = cut + lay.ff_share
    for f, ref in enumerate((mine, came)):
        for e in range(lay.size):
            place = 0
            for k in range(bits_of(lay.size)):
                place |= ((e >> k) & 1) << (bits_of(lay.size) - 1 - k)
            member = (spot[4] ^ place) * 2 + (spot[2] ^ f)

            def write(m, ref=ref, e=e):
                for i in range(3):
                    at = i * lay.width + m * hw
                    start = e * span + i * hw
                    w_in[:, at : at + hw] = ref[0:n, start : start + hw].astype(F32)
                for b in range(2 * lay.planes):
                    top, plane = b // lay.planes, b % lay.planes
                    at = (((top * lay.size + m // 2) * lay.planes + plane) * 2 + m % 2) * piece
                    start = e * span + cut + b * piece
                    w_up[:, at : at + piece] = ref[0:n, start : start + piece].astype(F32)

            for m in range(lay.members):
                pl.when(member == m)(functools.partial(write, m))
    total = sums[...] + came[base : base + tall, 0 : lay.small].astype(F32)
    own = jnp.where(iota(total.shape, 0) == spot[7], total, 0.0)
    own = jnp.sum(own, axis=0, keepdims=True)
    at = 0
    for ref in vectors:
        ref[...] = own[:, at : at + ref.shape[1]]
        at += ref.shape[1]


def add_kernel(one, two, out):
    out[...] = (one[...].astype(F32) + two[...].astype(F32)).astype(out.dtype)


def last_kernel(spot, vecs, keep, came, sent, own, grad_middle, out):
    total = keep[...].astype(F32) + came[...].astype(F32)
    slope = jnp.where(spot[6] == 1, total, sent[...].astype(F32))
    normal, scale = centre(own[...].astype(F32))
    out[...] = (grad_middle[...] + norm_back(slope, normal, scale, vecs[0:1, :])).astype(BF16)


def out_kernel(vecs, middle, keep, came, out):
    total = keep[...].astype(F32) + came[...].astype(F32)
    out[...] = (middle[...] + (total + vecs[7:8, :])).astype(BF16)


def solution(mesh):
    nb, nt = mesh.shape["blk"], mesh.shape["batch"]
    devices = nb * nt
    group_size = nb // 2
    total_bits = bits_of(devices)
    plane_bits = list(range(1, bits_of(nt)))
    group_bits = list(range(bits_of(nt), bits_of(nt) + bits_of(group_size)))
    top_bit = total_bits - 1
    members = 2 * group_size

    def at_home(i):
        return (i // nt) // group_size == i % 2

    def send(value, route):
        return lax.ppermute(value, AXES, route)

    def flip(value, bit, who=None):
        return send(value, [(i, i ^ (1 << bit)) for i in range(devices) if who is None or who(i)])

    def mirror(i):
        return (nb - 1 - i // nt) * nt + i % nt

    def local(
        hidden_in,
        key_mask,
        lengths,
        first_gain,
        first_shift,
        input_weight,
        query_bias,
        value_bias,
        output_weight,
        output_bias,
        second_gain,
        second_shift,
        up_weight,
        up_bias,
        down_weight,
        down_bias,
        cotangent,
    ):
        rows, width = hidden_in.shape[1:]
        length = key_mask.shape[1]
        head = width // HEADS
        blk, lane_id = lax.axis_index("blk"), lax.axis_index("batch")
        index = blk * nt + lane_id
        core = lane_id % 2
        group, place = blk // group_size, blk % group_size
        member = place * 2 + core
        home = group == core
        share = width // members
        ff = up_weight.shape[1]
        piece = ff // devices

        def bit(b):
            return (index >> b) & 1

        def ordered(mine, theirs, side, axis):
            return jnp.where(
                side == 0,
                jnp.concatenate([mine, theirs], axis),
                jnp.concatenate([theirs, mine], axis),
            )

        def side_of(value, side, axis):
            lo, hi = jnp.split(value, 2, axis)
            return jnp.where(side == 0, lo, hi)

        lay = Layout(nb, nt, rows, width, ff, length)
        each = lay.each
        own = hidden_in[0]
        kept_group = jnp.where(home, group, 1 - group)
        kept_place = jnp.where(home, place, group_size - 1 - place)
        spot = jnp.stack(
            [blk, lane_id, core, group, place, member, home.astype(jnp.int32), index]
            + [kept_group, kept_place]
        )
        away = lambda i: not at_home(i)
        from_away = [(i, i ^ 1) for i in range(devices) if away(i)]
        across = [(i, mirror(i) ^ 1) for i in range(devices) if away(i)]
        mirrored = [(i, mirror(i)) for i in range(devices)]

        wide_in = 3 * group_size * share + 2 * group_size * lay.planes * piece
        row = lambda value: value.reshape(1, -1)
        vectors = [
            row(v)
            for v in (
                first_gain,
                first_shift,
                query_bias,
                value_bias,
                output_bias,
                second_gain,
                second_shift,
                down_bias,
                up_bias,
            )
        ]
        start = [input_weight, up_weight, key_mask] + vectors
        base = max(each, 16)
        give, keep = kernel_call(
            functools.partial(pack_kernel, lay),
            [shaped((base + EXTRA, wide_in), BF16)] * 2,
            spot,
            lengths,
            *start,
            name="pack",
            smem=(0, 1),
            away=tuple(range(2, 14)),
            vmem=60,
            scratch=[pltpu.VMEM(v.shape, v.dtype) for v in start] + [pltpu.SemaphoreType.DMA((12,))],
        )
        came_w = flip(give, 0)
        far = [send(own, across)]
        count = group_size
        for step, b in enumerate(group_bits):
            tall = (2 << step) * each
            columns = wide_in >> (step + 1)
            give, keep, ready = kernel_call(
                functools.partial(trade_kernel, lay, step, count),
                [shaped((tall + EXTRA, columns), BF16)] * 2 + [shaped((8, length), F32)],
                spot,
                keep,
                came_w,
                name="trade",
                smem=(0,),
                scratch=[pltpu.VMEM((tall, 2 * columns), BF16)],
            )
            valid = ready if step == 0 else valid
            came_w = flip(give, b)
            count //= 2
        tall = members * each
        in_block, up_block, far_later = kernel_call(
            functools.partial(settle_kernel, lay, len(group_bits)),
            [
                shaped((tall + EXTRA, 3 * share), BF16),
                shaped((tall, ff // members), BF16),
                shaped(own.shape, BF16),
            ],
            spot,
            keep,
            came_w,
            far[0],
            name="settle",
            smem=(0,),
            scratch=[pltpu.VMEM((tall, 3 * share + ff // members), BF16)],
        )
        cut = max(LANES, 3 * share // 2 // LANES * LANES)
        paired = up_block.shape == down_weight.shape

        def spread_group(values, who=None):
            for b in group_bits:
                values = values + [flip(v, b, who) for v in values]
            return values

        left, right, up_block, down_block, own_later = kernel_call(
            functools.partial(split_kernel, cut),
            [
                shaped((2, tall + EXTRA, cut), BF16),
                shaped((2, tall + EXTRA, 3 * share - cut), BF16),
                shaped((2 if paired else 1,) + up_block.shape, BF16),
                shaped((8, LANES) if paired else down_weight.shape, BF16),
                shaped(own.shape, BF16),
            ],
            in_block,
            flip(in_block, top_bit),
            up_block,
            down_weight,
            own,
            name="split",
        )
        far = far + spread_group([far_later], away)[1:]
        far_c = [send(v, from_away) for v in far]
        for k, (b, c) in enumerate(zip(plane_bits, reversed(plane_bits), strict=True)):
            left_came, right_came = flip(left, b), flip(right, c)
            if k + 1 < len(plane_bits):
                left, right = stack(left, left_came, right, right_came, *far[1:2])
        in_pieces = (left, left_came, right, right_came)
        vecs = kernel_call(
            functools.partial(vector_kernel, lay),
            [shaped((16, width), F32)],
            spot,
            left,
            left_came,
            name="vectors",
            smem=(0,),
            away=(1, 2),
            scratch=[
                pltpu.VMEM((2 * lay.planes * EXTRA, -(-lay.small // LANES) * LANES), BF16),
                pltpu.SemaphoreType.DMA((2 * lay.planes,)),
            ],
        )[0]

        near = [own] + spread_group([own_later])[1:]
        near_c = [flip(v, 0) for v in near]

        if paired:
            ups, downs = kernel_call(
                unpair_kernel,
                [shaped((2,) + v.shape, BF16) for v in up_block[:2]],
                up_block,
                flip(up_block, top_bit),
                name="unpair",
                after=(left, right),
            )
        else:
            ups, downs = up_block, down_block[None]
            ups, downs = stack(
                ups, flip(ups, top_bit), downs, flip(downs, top_bit), left, right
            )
        ups_first = ups
        for k, (b, c) in enumerate(zip(plane_bits, reversed(plane_bits), strict=True)):
            ups_came, downs_came = flip(ups, b), flip(downs, c)
            if k + 1 < len(plane_bits):
                ups, downs = stack(ups, ups_came, downs, downs_came)
        w_out = lax.all_gather(output_weight, AXES, axis=0, tiled=True)

        grad_low = kernel_call(
            mask_kernel,
            [shaped((rows, width), BF16)],
            spot,
            lengths,
            cotangent[0],
            name="mask",
            smem=(0, 1),
            after=(near[1],),
        )[0]
        down_m = spread_group([grad_low])
        down_c = [flip(v, 0) for v in down_m]

        key_bias = jnp.where(valid[0] > 0.5, 0.0, MASKED).astype(F32).reshape(length, 1)
        near_att, far_att, joint, wide, lse, normed_one, x_all, w_in = attend(
            lay, spot, key_bias, vecs, near + far + near_c + far_c, in_pieces, ups_first
        )
        far_att = spread_group([send(far_att, mirrored)])
        near_att = spread_group([near_att])
        att_c = [flip(v, 0) for v in near_att + far_att]

        (
            dn_keep,
            dn_give,
            middle,
            att_own,
            normed_two,
            act,
            grad_pre,
            d_bias_up,
        ) = forward_call(
            lay,
            spot,
            vecs,
            w_out,
            near_att + far_att + att_c + near + near_c + down_m + down_c,
            (ups, ups_came, downs, downs_came),
        )

        def reduce_group(keep, give, slot):
            came = flip(give, 0)
            for k in reversed(range(len(group_bits))):
                keep, give = fold(spot, slot, k, 1, keep, came)
                came = flip(give, group_bits[k])
            return keep, came

        dn_keep, dn_came = reduce_group(dn_keep, dn_give, 4)
        up_keep, up_give, down_keep, down_give, out_keep, out_give = gradient_call(
            lay, spot, normed_two, act, grad_pre, down_m, down_c, (downs, downs_came)
        )
        *slopes, grad_middle, grad_branch, sums_two = turn_call(
            lay, spot, vecs, dn_keep, dn_came, middle, grad_low, w_out, up_give
        )

        parts = []
        for r in range(members):

            def route(i):
                m = (i // nt) ^ r
                return ((i % 2) * group_size + m // 2) * nt + (i % nt) - i % 2 + m % 2

            parts.append(send(slopes[r], [(i, route(i)) for i in range(devices)]))
        grad_joint, left_keep, left_give, right_keep, right_give, joint_sum = attend_back(
            lay, spot, key_bias, joint, wide, lse, normed_one, parts, cut
        )
        in_keep, in_give, sums, sums_give = input_call(
            lay, spot, grad_joint, w_in, x_all, sums_two, joint_sum, d_bias_up
        )
        in_keep, in_came = reduce_group(in_keep, in_give, 9)
        in_sum = kernel_call(
            add_kernel, [shaped((rows, width), BF16)], in_keep, in_came, name="add"
        )[0]
        input_gradient = kernel_call(
            last_kernel,
            [shaped((rows, width), BF16)],
            spot,
            vecs,
            in_keep,
            in_came,
            send(in_sum, across),
            own,
            grad_middle,
            name="input_gradient",
            smem=(0,),
        )[0]

        planes_down = list(reversed(plane_bits))
        top_shift = bits_of(group_size)

        def cuts_of(lead, order):
            here, cuts = list(planes_down), []
            for b in order:
                cuts.append((1, b, lead << here.index(b)))
                here.remove(b)
            return cuts

        up_cuts, down_cuts = cuts_of(members, planes_down), cuts_of(2, plane_bits)
        for k, (b, c) in enumerate(zip(planes_down, plane_bits, strict=True)):
            up_came, down_came = flip(up_give, b), flip(down_give, c)
            if k + 1 < len(plane_bits):
                up_keep, up_give, down_keep, down_give = two_fold(
                    spot,
                    (up_cuts[k + 1], down_cuts[k + 1]),
                    up_keep,
                    up_came,
                    down_keep,
                    down_came,
                )
        if paired:
            half = (up_keep.shape[0] // 2, up_keep.shape[1])
            up_keep, down_keep, give = kernel_call(
                functools.partial(top_pair_kernel, top_shift),
                [shaped(half, BF16), shaped(half, BF16), shaped((2,) + half, BF16)],
                spot,
                up_keep,
                up_came,
                down_keep,
                down_came,
                name="top_pair",
                smem=(0,),
            )
            came = flip(give, top_bit)
            up_came, down_came = came[0], came[1]
        else:
            up_keep, up_give, down_keep, down_give = two_fold(
                spot, ((0, top_shift, 1),) * 2, up_keep, up_came, down_keep, down_came
            )
            up_came, down_came = flip(up_give, top_bit), flip(down_give, top_bit)
        d_down = kernel_call(
            add_kernel, [shaped((piece, width), F32)], down_keep, down_came, name="add"
        )[0]

        left_cuts, right_cuts = cuts_of(members, planes_down), cuts_of(members, plane_bits)
        sums_came = flip(sums_give, planes_down[0])
        for k, (b, c) in enumerate(zip(planes_down, plane_bits, strict=True)):
            left_came, right_came = flip(left_give, b), flip(right_give, c)
            if k + 1 < len(plane_bits):
                left_keep, left_give, right_keep, right_give, sums = sums_fold(
                    spot,
                    (left_cuts[k + 1], right_cuts[k + 1]),
                    left_keep,
                    left_came,
                    right_keep,
                    right_came,
                    sums,
                    sums_came,
                )
        tall = left_keep.shape[0] // 2
        small = (devices, lay.small)
        w_keep, w_give, sums = kernel_call(
            functools.partial(top_fold_kernel, top_shift),
            [
                shaped((tall, 3 * share), BF16),
                shaped((tall + devices, 3 * share), BF16),
                shaped(small, F32),
            ],
            spot,
            left_keep,
            left_came,
            right_keep,
            right_came,
            sums,
            name="top_fold",
            smem=(0,),
        )
        came = flip(w_give, top_bit)
        columns = 3 * share + ff // members
        steps = [(4, k, b) for k, b in reversed(list(enumerate(group_bits)))] + [(2, 0, 0)]
        for step, (slot, shift, b) in enumerate(steps):
            tall //= 2
            outs = [
                shaped((tall, columns), BF16),
                shaped((max(tall, 16) + devices, columns), BF16),
                shaped(small, F32),
            ]
            if step == 0:
                w_keep, w_give, sums = kernel_call(
                    functools.partial(home_first_kernel, slot, shift),
                    outs,
                    spot,
                    w_keep,
                    came,
                    up_keep,
                    up_came,
                    sums,
                    name="home_first",
                    smem=(0,),
                )
            else:
                w_keep, w_give, sums = kernel_call(
                    functools.partial(home_next_kernel, slot, shift),
                    outs,
                    spot,
                    w_keep,
                    came,
                    sums,
                    name="home_next",
                    smem=(0,),
                )
            came = flip(w_give, b)
            columns *= 2
        d_in, d_up, *vectors = kernel_call(
            functools.partial(home_last_kernel, lay),
            [shaped((each, 3 * width), F32), shaped((each, ff), F32)]
            + [shaped((1, each), F32)] * 8
            + [shaped((1, piece), F32)],
            spot,
            w_keep,
            came,
            sums,
            name="home_last",
            smem=(0,),
        )
        vectors = [v.reshape(-1) for v in vectors]

        d_out = dot(att_own, grad_branch, TN).astype(BF16)
        d_out = lax.psum_scatter(d_out, AXES, scatter_dimension=0, tiled=True).astype(F32)

        out_keep, out_came = reduce_group(out_keep, out_give, 4)
        layer_out = kernel_call(
            out_kernel,
            [shaped((rows, width), BF16)],
            vecs,
            middle,
            out_keep,
            out_came,
            name="layer_out",
        )[0]

        return (
            layer_out[None],
            input_gradient[None],
            vectors[0],
            vectors[1],
            d_in,
            vectors[2],
            vectors[3],
            d_out,
            vectors[4],
            vectors[5],
            vectors[6],
            d_up,
            vectors[8],
            d_down,
            vectors[7],
        )

    vector, matrix = P(AXES), P(AXES, None)
    tokens = P("batch", "blk", None)
    return jax.shard_map(
        local,
        mesh=mesh,
        in_specs=(
            tokens,
            P("batch", None),
            P("batch"),
            vector,
            vector,
            matrix,
            vector,
            vector,
            matrix,
            vector,
            vector,
            vector,
            matrix,
            vector,
            matrix,
            vector,
            tokens,
        ),
        out_specs=(
            tokens,
            tokens,
            vector,
            vector,
            matrix,
            vector,
            vector,
            matrix,
            vector,
            vector,
            vector,
            matrix,
            vector,
            matrix,
            vector,
        ),
        check_vma=False,
    )
```

```python
import functools

import jax
import jax.numpy as jnp
from jax import lax
from jax.experimental import pallas as pl
from jax.experimental.pallas import tpu as pltpu
from jax.sharding import PartitionSpec as P

HEADS = 16
EPSILON = 1e-05
SCORE_SCALE = 0.125
MASKED = -1e30
LANES = 128
AXES = ("blk", "batch")
F32 = jnp.float32
BF16 = jnp.bfloat16

NT = (((1,), (1,)), ((), ()))
NN = (((1,), (0,)), ((), ()))
TN = (((0,), (0,)), ((), ()))


def dot(a, b, dims=NN):
    return lax.dot_general(a, b, dims, preferred_element_type=F32)


def bits_of(size):
    return size.bit_length() - 1


def key_mask_terms(rows):
    key = lax.broadcasted_iota(jnp.int32, (rows, rows), 0)
    query = lax.broadcasted_iota(jnp.int32, (rows, rows), 1)
    return key < query, key == query


def centre(values):
    average = jnp.mean(values, axis=-1, keepdims=True)
    centred = values - average
    variance = jnp.mean(centred * centred, axis=-1, keepdims=True)
    scale = lax.rsqrt(variance + EPSILON)
    return centred * scale, scale


def norm_back(slope, normal, scale, gain):
    weighted = slope * gain
    return scale * (
        weighted
        - jnp.mean(weighted, axis=-1, keepdims=True)
        - normal * jnp.mean(weighted * normal, axis=-1, keepdims=True)
    )


GELU_A = 0.7978845608028654
GELU_B = 0.044715


def gelu_terms(pre):
    square = pre * pre
    bend = jnp.tanh(GELU_A * pre * (1.0 + GELU_B * square))
    half = 0.5 * (1.0 + bend)
    slope = half + 0.5 * pre * (1.0 - bend * bend) * (GELU_A * (1.0 + 3.0 * GELU_B * square))
    return pre * half, slope


EXTRA = 16


COST = lambda flops: 10**11


def shaped(shape, kind):
    return jax.ShapeDtypeStruct(shape, kind)


class Order:
    def __init__(self):
        self.ticket = jnp.zeros((8, LANES), F32)


def kernel_call(order, body, outs, *args, name, smem=(), away=(), scratch=(), vmem=8, flops=0, after=()):
    count, given = len(args), len(outs)
    inner = body

    def body(*refs):
        ins, rest = refs[:count], refs[count + len(after) :]
        before, results, ticket = rest[0], rest[1 : 1 + given], rest[1 + given]
        ticket[...] = before[...]
        inner(*ins, *results, *rest[2 + given :])

    away = tuple(away) + tuple(range(count, count + len(after)))
    args = args + tuple(after) + (order.ticket,)
    outs = list(outs) + [shaped((8, LANES), F32)]

    def spec(i, places):
        if i in places:
            return pl.BlockSpec(memory_space=pl.ANY)
        return pl.BlockSpec(memory_space=pltpu.VMEM)

    ins = [
        pl.BlockSpec(memory_space=pltpu.SMEM) if i in smem else spec(i, away)
        for i in range(len(args))
    ]
    moved = sum(v.size * v.dtype.itemsize for v in args + tuple(outs))
    *results, order.ticket = pl.pallas_call(
        body,
        in_specs=ins,
        out_specs=[spec(i, ()) for i in range(len(outs))],
        out_shape=list(outs),
        scratch_shapes=list(scratch),
        compiler_params=pltpu.CompilerParams(vmem_limit_bytes=vmem * 2**20),
        cost_estimate=pl.CostEstimate(flops=COST(flops), bytes_accessed=1, transcendentals=0),
        name=name,
    )(*args)
    return results


def iota(shape, dim):
    return lax.broadcasted_iota(jnp.int32, shape, dim)


class Layout:
    def __init__(self, nb, nt, rows, width, ff, length):
        self.nb, self.nt, self.rows, self.width, self.ff, self.length = nb, nt, rows, width, ff, length
        self.devices = nb * nt
        self.size = nb // 2
        self.planes = nt // 2
        self.members = 2 * self.size
        self.each = width // self.devices
        self.piece = ff // self.devices
        self.share = width // self.members
        self.ff_share = ff // self.members
        self.small = 8 * self.each + self.piece
        self.valid_at = -(-self.small // 512) * 512
        self.head = width // HEADS
        self.order = Order()


def each_way(flag, write):
    pl.when(flag == 0)(lambda: write(0))
    pl.when(flag == 1)(lambda: write(1))


def write_half(lay, side, count, in_from, up_from, in_start, up_start, give, keep, n):
    hw, pc = lay.share, lay.piece
    tail = lay.planes * pc if count > 0 else pc
    spans = []
    if count == 0:
        for q in range(3 * lay.size):
            spans.append((in_from, in_start + 2 * q * hw, hw))
        for q in range(2 * lay.size * lay.planes):
            spans.append((up_from, up_start + 2 * q * pc, pc))
    else:
        for q in range(3 * count // 2):
            spans.append((in_from, in_start + 2 * q * hw, hw))
        for q in range(count):
            spans.append((up_from, up_start + 2 * q * tail, tail))
    at = 0
    for source, start, span in spans:
        mine = source[0:n, start + side * span : start + (side + 1) * span]
        other = source[0:n, start + (1 - side) * span : start + (2 - side) * span]
        keep[0:n, at : at + span] = mine
        give[0:n, at : at + span] = other
        at += span


def load_all(pairs, sems):
    copies = [pltpu.make_async_copy(a, b, sems.at[i]) for i, (a, b) in enumerate(pairs)]
    for copy in copies:
        copy.start()
    return copies


def wait_all(copies):
    for copy in copies:
        copy.wait()


def pack_kernel(lay, spot, lengths, *refs):
    sources, (give, keep), targets, sems = refs[:13], refs[13:15], refs[15:28], refs[28]
    wait_all(load_all(list(zip(sources, targets, strict=True)), sems))
    w_in, w_up, mask, w_out = targets[:4]
    smalls = targets[4:]
    n = lay.each
    base = max(n, 16)
    if base > n:
        for ref in (give, keep):
            ref[0:base, :] = jnp.zeros((base, ref.shape[1]), BF16)
    each_way(spot[2], lambda side: write_half(lay, side, 0, w_in, w_up, 0, 0, give, keep, n))
    half = lay.width // 2
    last = give.shape[1] - half

    def write_out(side):
        keep[0:n, last:] = w_out[:, side * half : (side + 1) * half]
        give[0:n, last:] = w_out[:, (1 - side) * half : (2 - side) * half]

    each_way(spot[2], write_out)
    line = jnp.zeros((1, lay.small), F32)
    at = 0
    for ref in smalls:
        span = ref.shape[1]
        where = iota((span, lay.small), 1) == iota((span, lay.small), 0) + at
        line = line + dot(ref[...], where.astype(F32).astype(BF16))
        at += span
    row = iota((EXTRA, lay.small), 0) == spot[5]
    extra = jnp.where(row, line, 0.0).astype(BF16)
    live = (mask[...] > 0) & (iota(mask.shape, 1) < lengths[0])
    valid = jnp.where(live, 1.0, 0.0) * jnp.ones((EXTRA, 1), F32)
    for ref in (give, keep):
        ref[base : base + EXTRA, :] = jnp.zeros((EXTRA, ref.shape[1]), BF16)
        ref[base : base + EXTRA, 0 : lay.small] = extra
        ref[base : base + EXTRA, lay.valid_at : lay.valid_at + lay.length] = valid.astype(BF16)


def merge_rows(keep, came, side, n, out):
    if n < 16:
        mine, theirs = keep[0:16, :].astype(F32)[0:n], came[0:16, :].astype(F32)[0:n]
        first = jnp.where(side == 0, mine, theirs)
        second = jnp.where(side == 0, theirs, mine)
        out[...] = jnp.concatenate([first, second], axis=0).astype(BF16)
        return
    out[pl.ds(pl.multiple_of(side * n, n), n), :] = keep[0:n, :]
    out[pl.ds(pl.multiple_of((1 - side) * n, n), n), :] = came[0:n, :]


def merge_extra(lay, keep, came, n):
    n = max(n, 16)
    total = keep[n : n + EXTRA, 0 : lay.small].astype(F32) + came[n : n + EXTRA, 0 : lay.small].astype(F32)
    return total.astype(BF16)


def trade_kernel(lay, step, count, spot, keep, came, give, hold, valid, both):
    n = (1 << step) * lay.each
    merge_rows(keep, came, spot[2] if step == 0 else (spot[4] >> (step - 1)) & 1, n, both)
    start = 3 * count * lay.share
    each_way(
        (spot[4] >> step) & 1,
        lambda side: write_half(lay, side, count, both, both, 0, start, give, hold, 2 * n),
    )
    half = lay.width // 2
    for ref in (give, hold):
        ref[0 : 2 * n, ref.shape[1] - half :] = both[:, both.shape[1] - half :]
    extra = merge_extra(lay, keep, came, n)
    for ref in (give, hold):
        ref[2 * n : 2 * n + EXTRA, :] = jnp.zeros((EXTRA, ref.shape[1]), BF16)
        ref[2 * n : 2 * n + EXTRA, 0 : lay.small] = extra
    if step == 0:
        place = slice(lay.valid_at, lay.valid_at + lay.length)
        base = max(n, 16)
        mine, theirs = (ref[base : base + 16, place].astype(F32)[0:8] for ref in (keep, came))
        valid[...] = jnp.where(spot[6] == 1, mine, theirs)
    else:
        valid[...] = jnp.zeros_like(valid)


def settle_kernel(
    lay, step, spot, keep, came, far, down, in_block, up_block, far_out, pair, both
):
    far_out[...] = far[...]
    n = (1 << step) * lay.each
    merge_rows(keep, came, (spot[4] >> (step - 1)) & 1, n, both)
    cut = 3 * lay.share
    in_block[0 : 2 * n, :] = both[:, 0:cut]
    last = cut + lay.ff_share
    tall, half = 2 * n, lay.width // 2
    chunks = lay.ff_share // half
    part = tall // chunks
    targets = [up_block.at[0]] + ([pair] if pair.shape[0] > 8 else [])
    for ref in targets:
        ref[0:tall, :] = both[:, cut:last]
        for i in range(chunks):
            rows = both[i * part : (i + 1) * part, last:]
            ref[tall : tall + part, i * half : (i + 1) * half] = rows
    if pair.shape[0] > 8:
        pair[tall + part :, :] = down[...]
    in_block[2 * n : 2 * n + EXTRA, :] = jnp.zeros((EXTRA, cut), BF16)
    in_block[2 * n : 2 * n + EXTRA, 0 : lay.small] = merge_extra(lay, keep, came, n)


def split_kernel(cut, mine, came, pair, grad, left, right, pair_out, grad_out):
    pair_out[...] = pair[...]
    grad_out[...] = grad[...]
    left[0], left[1] = mine[:, 0:cut], came[:, 0:cut]
    right[0], right[1] = mine[:, cut:], came[:, cut:]


def stack_kernel(one, one_came, two, two_came, one_out, two_out):
    n = one.shape[0]
    one_out[0:n], one_out[n : 2 * n] = one[...], one_came[...]
    two_out[0:n], two_out[n : 2 * n] = two[...], two_came[...]


def stack(lay, one, one_came, two, two_came, *after):
    outs = [shaped((2 * v.shape[0],) + v.shape[1:], BF16) for v in (one, two)]
    return kernel_call(
        lay.order, stack_kernel, outs, one, one_came, two, two_came, name="stack", after=after
    )


def unpair_kernel(pair, up, down):
    n = up.shape[1]
    up[0], down[0] = pair[0:n, :], pair[n:, :]


def bundle_kernel(g, spot, *refs):
    near, far, out = refs[:g], refs[g : 2 * g], refs[2 * g]
    rows = near[0].shape[0]

    def write(home):
        parts = list(near) if home else list(far) + list(near)
        for i, ref in enumerate(parts):
            out[i * rows : (i + 1) * rows, :] = ref[...]

    each_way(spot[6], write)


def out_kernel_rows(mine, came, out):
    count, tall, half = out.shape
    chunks = mine.shape[2] // half
    part = tall // chunks
    for k in range(count):
        source = (mine if k < count // 2 else came).at[k % (count // 2)]
        for i in range(chunks):
            rows = source[tall : tall + part, i * half : (i + 1) * half]
            out[k, i * part : (i + 1) * part, :] = rows


def join_kernel(one, one_came, out):
    n = one.shape[0]
    out[0:n], out[n : 2 * n] = one[...], one_came[...]


def join(lay, one, one_came, *after):
    out = shaped((2 * one.shape[0],) + one.shape[1:], BF16)
    return kernel_call(lay.order, join_kernel, [out], one, one_came, name="join", after=after)[0]


def block_spot(lay, spot, k, flipped):
    bits = bits_of(lay.planes)
    top = (spot[3] ^ k) & 1
    order = range(bits - 1, -1, -1) if flipped else range(bits)
    plane = spot[1] >> 1
    for position, b in enumerate(order):
        plane = plane ^ (((k >> (position + 1)) & 1) << b)
    return top, plane


def vector_kernel(lay, spot, first, second, out, rows, sems):
    n, count, wide = lay.members * lay.each, 2 * lay.planes, rows.shape[1]
    copies = []
    for k in range(count):
        source = first if k < count // 2 else second
        copy = pltpu.make_async_copy(
            source.at[k % (count // 2), n : n + EXTRA, 0:wide],
            rows.at[k * EXTRA : (k + 1) * EXTRA, :],
            sems.at[k],
        )
        copy.start()
        copies.append(copy)
    for copy in copies:
        copy.wait()
    out[...] = jnp.zeros_like(out)
    tall = count * EXTRA
    line, lane = iota((tall, lay.width), 0), iota((tall, lay.width), 1)
    holder, block = jnp.zeros_like(line), jnp.zeros_like(line)
    for k in range(count):
        top, plane = block_spot(lay, spot, k, False)
        inside = line - k * EXTRA
        here = (inside >= 0) & (inside < EXTRA)
        lead = (top * lay.size + inside // 2) * lay.nt + plane * 2 + inside % 2
        holder = jnp.where(here, jnp.where(inside < lay.members, lead, -1), holder)
        block = jnp.where(here & (inside == spot[5]), top * lay.planes + plane, jnp.where(here, -1, block))
    values = rows[...]
    source, target = iota((wide, lay.width), 0), iota((wide, lay.width), 1)
    for v in range(8):
        spread = (source == v * lay.each + target % lay.each).astype(F32).astype(BF16)
        tiled = jnp.where(lane // lay.each == holder, dot(values, spread), 0.0)
        out[v : v + 1, :] = jnp.sum(tiled, axis=0, keepdims=True)
    spread = (source == 8 * lay.each + target % lay.piece).astype(F32).astype(BF16)
    tiled = jnp.where(lane // lay.piece == block, dot(values, spread), 0.0)
    out[8:9, :] = jnp.sum(tiled, axis=0, keepdims=True)
    hw = lay.share
    mine = pl.ds(pl.multiple_of(spot[5] * hw, hw), hw)
    out[9:10, 0:hw] = out[2:3, mine]
    out[9:10, 2 * hw : 3 * hw] = out[3:4, mine]


def attend_kernel(lay, spot, bias, vecs, *refs):
    g, rows, hw, length, head = lay.size, lay.rows, lay.share, lay.length, lay.head
    near, far, came = refs[:g], refs[g : 2 * g], refs[2 * g]
    near_c = far_c = [came.at[e * rows : (e + 1) * rows, :] for e in range(g)]
    weights = refs[2 * g + 1 : 2 * g + 5]
    near_att, far_att, joint, wide, lse, normed, x, w, x_sems, w_sems = refs[2 * g + 5 :]
    group, place = spot[3], spot[4]
    pending = []
    for e in range(g):
        for side, (at_home, at_away) in enumerate(((near[e], near_c[e]), (far_c[e], far[e]))):
            spot_here = (place if side == 0 else g - 1 - place) ^ e
            spot_here = (group if side == 0 else 1 - group) * g + spot_here
            target = x.at[pl.ds(pl.multiple_of(spot_here * rows, rows), rows), :]
            sem = x_sems.at[side * g + e]
            home = pltpu.make_async_copy(at_home, target, sem)
            visit = pltpu.make_async_copy(at_away, target, sem)
            pl.when(spot[6] == 1)(home.start)
            pl.when(spot[6] == 0)(visit.start)
            pending.append(home)
    count = 2 * lay.planes
    span = 2 * lay.each
    cut = weights[0].shape[-1]
    loads = []
    for k in range(count):
        for side in range(2):
            source = weights[2 * side + (k >= count // 2)]
            top, plane = block_spot(lay, spot, k, side == 1)
            for q in range(g):
                start = ((top * g + q) * lay.planes + plane) * span
                copy = pltpu.make_async_copy(
                    source.at[k % (count // 2), q * span : (q + 1) * span, :],
                    w.at[pl.ds(pl.multiple_of(start, span), span), 0:cut]
                    if side == 0
                    else w.at[pl.ds(pl.multiple_of(start, span), span), cut:],
                    w_sems.at[(k * 2 + side) * g + q],
                )
                copy.start()
                loads.append(copy)
    for copy in pending:
        copy.wait()
    for j in range(length // rows):
        here = slice(j * rows, (j + 1) * rows)
        normal, _ = centre(x[here, :].astype(F32))
        normed[here, :] = (normal * vecs[0:1, :] + vecs[1:2, :]).astype(BF16)
    for copy in loads:
        copy.wait()
    for j in range(length // rows):
        here = slice(j * rows, (j + 1) * rows)
        joint[here, :] = (dot(normed[here, :], w[...]) + vecs[9:10, 0 : 3 * hw]).astype(BF16)
    earlier, same = key_mask_terms(rows)
    lane = iota((rows, LANES), 1)
    for p in range(hw // LANES):
        q_at, k_at, v_at = (slice(i * hw + p * LANES, i * hw + (p + 1) * LANES) for i in range(3))
        value_t = joint[:, v_at].astype(F32).T.astype(BF16)
        for j in range(length // rows):
            here, past = slice(j * rows, (j + 1) * rows), slice(0, j * rows)
            bias_here = bias[here, :]
            for h in range(LANES // head):
                mine = (lane >= h * head) & (lane < (h + 1) * head)
                query = jnp.where(mine, joint[here, q_at].astype(F32) * SCORE_SCALE, 0.0).astype(BF16)
                inner = dot(joint[here, k_at], query, NT)
                inner = jnp.where(same, inner, jnp.where(earlier, inner + bias_here, MASKED))
                top = jnp.max(inner, axis=0, keepdims=True)
                if j:
                    outer = dot(joint[past, k_at], query, NT) + bias[past, :]
                    top = jnp.maximum(top, jnp.max(outer, axis=0, keepdims=True))
                inner = jnp.exp(inner - top)
                total = jnp.sum(inner, axis=0, keepdims=True)
                if j:
                    outer = jnp.exp(outer - top)
                    total = total + jnp.sum(outer, axis=0, keepdims=True)
                share = 1.0 / total
                value_h = value_t[h * head : (h + 1) * head]
                out = dot(value_h[:, here], (inner * share).astype(BF16))
                if j:
                    out = out + dot(value_h[:, past], (outer * share).astype(BF16))
                at = p * LANES + h * head
                wide[at : at + head, here] = out
                lse[p, h : h + 1, here] = top + jnp.log(total)
    for i in range(g):
        here = slice(i * rows, (i + 1) * rows)
        for out_ref, first in ((near_att, group * g + i), (far_att, (1 - group) * g + i)):
            part = wide[:, pl.ds(pl.multiple_of(first * rows, rows), rows)]
            out_ref[here, :] = part.T.astype(BF16)


def attend(lay, spot, bias, vecs, hidden, weights):
    d, hw, length, g = lay.width, lay.share, lay.length, lay.size
    outs = [
        shaped((g * lay.rows, hw), BF16),
        shaped((g * lay.rows, hw), BF16),
        shaped((length, 3 * hw), BF16),
        shaped((hw, length), F32),
        shaped((hw // LANES, 8, length), F32),
        shaped((length, d), BF16),
        shaped((length, d), BF16),
        shaped((d, 3 * hw), BF16),
    ]
    copies = 2 * lay.planes * 2 * g
    args = (spot, bias, vecs) + tuple(hidden) + tuple(weights)
    return kernel_call(
        lay.order,
        functools.partial(attend_kernel, lay),
        outs,
        *args,
        name="attend",
        smem=(0,),
        away=tuple(range(3, len(args))),
        scratch=[
            pltpu.SemaphoreType.DMA((2 * g,)),
            pltpu.SemaphoreType.DMA((copies,)),
        ],
        vmem=24,
        flops=2 * length * d * 3 * hw + 3 * length * length * d // 2,
    )


def fold_kernel(slot, shift, a, b, spot, keep, came, hold, give):
    total = keep[...].astype(F32) + came[...].astype(F32)
    side = (spot[slot] >> shift) & 1
    view = total.reshape(a, 2, b, total.shape[-1])

    def write(s):
        hold[...] = view[:, s].reshape(a * b, -1).astype(BF16)
        give[...] = view[:, 1 - s].reshape(a * b, -1).astype(BF16)

    each_way(side, write)


def fold(lay, spot, slot, shift, a, keep, came):
    count, columns = keep.shape
    b = count // (2 * a)
    return kernel_call(
        lay.order,
        functools.partial(fold_kernel, slot, shift, a, b),
        [shaped((a * b, columns), BF16)] * 2,
        spot,
        keep,
        came,
        name="fold",
        smem=(0,),
    )


def mask_kernel(spot, lengths, cotangent, out):
    rows = out.shape[0]
    live = spot[0] * rows + iota((rows, 1), 0) < lengths[0]
    out[...] = jnp.where(live, cotangent[...].astype(F32), 0.0).astype(BF16)


def place_rows(lay, spot, e):
    return spot[4] ^ e


def block_of(lay, blocks, k):
    mine, came = blocks[2 * (k & 1)], blocks[2 * (k & 1) + 1]
    half = lay.planes // 2
    return (mine if k >> 1 < half else came).at[(k >> 1) % half]


def up_loads(lay, spot, blocks, w_up):
    pairs = []
    span, g = 2 * lay.each, lay.size
    for k in range(2 * lay.planes):
        source = block_of(lay, blocks, k)
        top, plane = block_spot(lay, spot, k, False)
        for q in range(g):
            start = ((top * g + q) * lay.planes + plane) * span
            pairs.append(
                (
                    source.at[q * span : (q + 1) * span, :],
                    w_up.at[pl.ds(pl.multiple_of(start, span), span), :],
                )
            )
    return pairs


def down_loads(lay, spot, blocks, w_down):
    pairs = []
    for k in range(2 * lay.planes):
        top, plane = block_spot(lay, spot, k, True)
        start = (top * lay.planes + plane) * lay.piece
        target = w_down.at[pl.ds(pl.multiple_of(start, lay.piece), lay.piece), :]
        pairs.append((block_of(lay, blocks, k), target))
    return pairs


def row_loads(lay, spot, mine, swapped, target):
    pairs = []
    g, rows = lay.size, lay.rows
    for e in range(g):
        for source, sequence in ((mine[e], spot[2]), (swapped[e], 1 - spot[2])):
            start = (sequence * g + (spot[4] ^ e)) * rows
            pairs.append((source, target.at[pl.ds(pl.multiple_of(start, rows), rows), :]))
    return pairs


def out_loads(lay, spot, blocks, target):
    pairs = []
    half, span, g = lay.width // 2, 2 * lay.each, lay.size
    for i, block in enumerate(blocks):
        column = pl.multiple_of((spot[2] ^ (i // 2)) * half, half)
        for k in range(lay.planes):
            top, plane = block_spot(lay, spot, 2 * k + i % 2, False)
            for q in range(g):
                row = pl.multiple_of(((top * g + q) * lay.planes + plane) * span, span)
                source = block.at[k, q * span : (q + 1) * span, :]
                pairs.append((source, target.at[pl.ds(row, span), pl.ds(column, half)]))
    return pairs


def forward_kernel(lay, spot, vecs, *refs):
    outs, refs = refs[:4], refs[4:]
    g, rows, hw, d = lay.size, lay.rows, lay.share, lay.width
    lists = [refs[i * g : (i + 1) * g] for i in range(7)]
    near, far, near_c, far_c, base_m, down_m, down_c = lists
    refs = refs[7 * g :]
    bundle, ups, downs = refs[0], refs[1:5], refs[5:9]
    (
        dn_keep,
        dn_give,
        middle_own,
        att_own,
        normed,
        act,
        grad_pre,
        bias_sum,
        wo,
        att,
        base,
        gd,
        w_up,
        w_down,
        sems,
    ) = refs[9:]
    core, group, place = spot[2], spot[3], spot[4]
    span = g * rows
    pairs = out_loads(lay, spot, outs, wo)
    for e in range(g):
        for source, sequence, at, side in (
            (near[e], group, place ^ e, core),
            (near_c[e], group, place ^ e, 1 - core),
            (far[e], 1 - group, (g - 1 - place) ^ e, core),
            (far_c[e], 1 - group, (g - 1 - place) ^ e, 1 - core),
        ):
            row = pl.multiple_of(sequence * span, span)
            column = pl.multiple_of((at * 2 + side) * hw, hw)
            pairs.append((source, att.at[pl.ds(row, span), pl.ds(column, hw)]))
    first_row = jnp.where(spot[6] == 1, span, 0)
    base_c = [
        bundle.at[pl.ds(pl.multiple_of(first_row + e * rows, rows), rows), :] for e in range(g)
    ]
    pairs += row_loads(lay, spot, base_m, base_c, base)
    first = len(pairs)
    pairs += up_loads(lay, spot, ups, w_up) + down_loads(lay, spot, downs, w_down)
    pairs += row_loads(lay, spot, down_m, down_c, gd)
    copies = load_all(pairs, sems)
    wait_all(copies[:first])
    bias_out, gain, shift = vecs[4:5, :], vecs[5:6, :], vecs[6:7, :]
    bias_up = vecs[8:9, 0 : lay.ff_share]
    total = jnp.zeros((1, lay.ff_share), F32)
    for i in range(2 * g):
        here = slice(i * rows, (i + 1) * rows)
        middle = base[here, :].astype(F32) + (dot(att[here, :], wo[...]) + bias_out)
        normal, _ = centre(middle)
        normed[here, :] = (normal * gain + shift).astype(BF16)

        @pl.when((core == i // g) & (place == i % g))
        def _():
            middle_own[...] = middle
            att_own[...] = att[here, :]

    wait_all(copies[first:])
    for i in range(2 * g):
        here = slice(i * rows, (i + 1) * rows)
        pre = dot(normed[here, :], w_up[...]) + bias_up
        value, slope = gelu_terms(pre)
        act[here, :] = value.astype(BF16)
        grad = (dot(gd[here, :], w_down[...], NT) * slope).astype(BF16)
        grad_pre[here, :] = grad
        total = total + jnp.sum(grad.astype(F32), axis=0, keepdims=True)
        back = dot(grad, w_up[...], NT).astype(BF16)
        at = slice((i % g) * rows, (i % g + 1) * rows)

        @pl.when(core == i // g)
        def _():
            dn_keep[at, :] = back

        @pl.when(core != i // g)
        def _():
            dn_give[at, :] = back

    bias_sum[...] = total


def forward_call(lay, spot, vecs, outs_w, lists, blocks):
    d, f, rows, g = lay.width, lay.ff_share, lay.rows, lay.size
    tokens = 2 * g * rows
    outs = [
        shaped((g * rows, d), BF16),
        shaped((g * rows, d), BF16),
        shaped((rows, d), F32),
        shaped((rows, d), BF16),
        shaped((tokens, d), BF16),
        shaped((tokens, f), BF16),
        shaped((tokens, f), BF16),
        shaped((1, f), F32),
        shaped((d, d), BF16),
    ]
    args = (spot, vecs) + tuple(outs_w) + tuple(lists) + tuple(blocks)
    copies = 4 * lay.planes * g + 8 * g + 2 * lay.planes * (g + 1)
    return kernel_call(
        lay.order,
        functools.partial(forward_kernel, lay),
        outs,
        *args,
        name="feed_forward",
        smem=(0,),
        away=tuple(range(2, len(args))),
        scratch=[
            pltpu.VMEM((tokens, d), BF16),
            pltpu.VMEM((tokens, d), BF16),
            pltpu.VMEM((tokens, d), BF16),
            pltpu.VMEM((d, f), BF16),
            pltpu.VMEM((f, d), BF16),
            pltpu.SemaphoreType.DMA((copies,)),
        ],
        vmem=24,
        flops=2 * tokens * d * (d + 3 * f),
    )


def cut_rows(value, side, a, b, keep, give):
    for i in range(a):
        for ref, s in ((keep, side), (give, 1 - side)):
            start = pl.multiple_of((2 * i + s) * b, b)
            ref[i * b : (i + 1) * b, :] = value[pl.ds(start, b), :]


def gradient_kernel(lay, spot, normed, act, grad_pre, *refs):
    g, rows, d, f = lay.size, lay.rows, lay.width, lay.ff_share
    down_m, down_c, blocks = refs[:g], refs[g : 2 * g], refs[2 * g : 2 * g + 4]
    up_keep, up_give, down_keep, down_give, out_keep, out_give, gd, w_down, full, sems = refs[
        2 * g + 4 :
    ]
    pairs = row_loads(lay, spot, down_m, down_c, gd)
    pairs += down_loads(lay, spot, blocks, w_down)
    copies = load_all(pairs, sems)
    tile = 256
    for i in range(d // tile):
        here = slice(i * tile, (i + 1) * tile)
        full[here, 0:f] = dot(normed[:, here], grad_pre[...], TN).astype(BF16)
    plane_bits = bits_of(lay.planes)
    side = (spot[1] >> plane_bits) & 1
    cut_rows(full.at[0:d, 0:f], side, 2 * g, d // (4 * g), up_keep, up_give)
    wait_all(copies)
    tile = min(256, f)
    for i in range(f // tile):
        here = slice(i * tile, (i + 1) * tile)
        full[here, 0:d] = dot(act[:, here], gd[...], TN).astype(BF16)
    side = (spot[1] >> 1) & 1
    cut_rows(full.at[0:f, 0:d], side, lay.planes, lay.piece, down_keep, down_give)
    for i in range(2 * g):
        here = slice(i * rows, (i + 1) * rows)
        at = slice((i % g) * rows, (i % g + 1) * rows)
        part = dot(act[here, :], w_down[...]).astype(BF16)

        @pl.when(spot[2] == i // g)
        def _():
            out_keep[at, :] = part

        @pl.when(spot[2] != i // g)
        def _():
            out_give[at, :] = part


def gradient_call(lay, spot, normed, act, grad_pre, down_m, down_c, blocks):
    d, f, rows, g = lay.width, lay.ff_share, lay.rows, lay.size
    tokens = 2 * g * rows
    outs = [shaped((d // 2, f), BF16)] * 2 + [shaped((f // 2, d), BF16)] * 2
    outs += [shaped((g * rows, d), BF16)] * 2
    args = (spot, normed, act, grad_pre) + tuple(down_m) + tuple(down_c) + tuple(blocks)
    return kernel_call(
        lay.order,
        functools.partial(gradient_kernel, lay),
        outs,
        *args,
        name="gradients",
        smem=(0,),
        away=tuple(range(4, len(args))),
        scratch=[
            pltpu.VMEM((tokens, d), BF16),
            pltpu.VMEM((f, d), BF16),
            pltpu.VMEM((d, d), BF16),
            pltpu.SemaphoreType.DMA((2 * g + 2 * lay.planes,)),
        ],
        vmem=24,
        flops=2 * tokens * d * 3 * f,
    )


def turn_kernel(lay, spot, vecs, keep, came, middle, grad_low, w_out, *refs):
    keep_out, give_out, grad_middle, grad_branch, sums, wo, att_grad, sems = refs
    copies = load_all([(w_out, wo)], sems)
    normal, scale = centre(middle[...])
    slope = keep[...].astype(F32) + came[...].astype(F32)
    total = grad_low[...].astype(F32) + norm_back(slope, normal, scale, vecs[5:6, :])
    grad_middle[...] = total
    branch = total.astype(BF16)
    grad_branch[...] = branch
    sums[...] = jnp.zeros_like(sums)
    add = lambda value: jnp.sum(value, axis=0, keepdims=True)
    sums[0:1, :] = add(branch.astype(F32))
    sums[1:2, :] = add(slope * normal)
    sums[2:3, :] = add(slope)
    sums[3:4, :] = add(grad_low[...].astype(F32))
    wait_all(copies)
    att_grad[...] = dot(branch, wo[...], NT).astype(BF16)
    hw = lay.share
    for i in range(lay.size):
        for ref, side in ((keep_out, spot[2]), (give_out, 1 - spot[2])):
            start = pl.multiple_of((2 * i + side) * hw, hw)
            ref[:, i * hw : (i + 1) * hw] = att_grad[:, pl.ds(start, hw)]


def outer_kernel(spot, att, branch, keep, give):
    tile, half = 256, keep.shape[1]

    def write(side):
        for i in range(keep.shape[0] // tile):
            here = slice(i * tile, (i + 1) * tile)
            value = dot(att[:, here], branch[...], TN).astype(BF16)
            keep[here, :] = value[:, side * half : (side + 1) * half]
            give[here, :] = value[:, (1 - side) * half : (2 - side) * half]

    each_way(spot[2], write)


def pick_kernel(lay, spot, mine, came, *pieces):
    hw = lay.share
    for r in range(lay.members):
        chip = spot[0] ^ r
        column = pl.ds(pl.multiple_of(chip % lay.size * hw, hw), hw)
        own = chip // lay.size == spot[2]

        @pl.when(own)
        def _(r=r, column=column):
            pieces[r][...] = mine[:, column]

        @pl.when(jnp.logical_not(own))
        def _(r=r, column=column):
            pieces[r][...] = came[:, column]


def turn_call(lay, spot, vecs, keep, came, middle, grad_low, w_out):
    d, rows = lay.width, lay.rows
    outs = [shaped((rows, d // 2), BF16)] * 2
    outs += [shaped((rows, d), F32), shaped((rows, d), BF16), shaped((8, d), F32)]
    return kernel_call(
        lay.order,
        functools.partial(turn_kernel, lay),
        outs,
        spot,
        vecs,
        keep,
        came,
        middle,
        grad_low,
        w_out,
        name="turn",
        smem=(0,),
        away=(6,),
        scratch=[
            pltpu.VMEM((d, d), BF16),
            pltpu.VMEM((rows, d), BF16),
            pltpu.SemaphoreType.DMA((1,)),
        ],
        vmem=24,
        flops=2 * rows * d * d,
    )


def assemble_kernel(lay, spot, *refs):
    out = refs[-1]
    for r in range(lay.members):
        start = pl.multiple_of((spot[0] ^ r) * lay.rows, lay.rows)
        out[pl.ds(start, lay.rows), :] = refs[r][...]


def attend_back_kernel(lay, spot, bias, joint, wide, lse, normed, slope_all, *refs):
    rows, hw, length, head, d = lay.rows, lay.share, lay.length, lay.head, lay.width
    (
        grads_out,
        left_keep,
        left_give,
        right_keep,
        right_give,
        sums,
        key_sum,
        value_sum,
        query_t,
        full,
    ) = refs
    earlier, same = key_mask_terms(rows)
    lane = iota((rows, LANES), 1)
    for p in range(hw // LANES):
        q_at, k_at, v_at = (slice(i * hw + p * LANES, i * hw + (p + 1) * LANES) for i in range(3))
        s_at = slice(p * LANES, (p + 1) * LANES)
        key_t = joint[:, k_at].astype(F32).T.astype(BF16)
        product = slope_all[:, s_at].astype(F32).T * wide[s_at, :]
        key_sum[...] = jnp.zeros_like(key_sum)
        value_sum[...] = jnp.zeros_like(value_sum)
        for j in range(length // rows):
            here = slice(j * rows, (j + 1) * rows)
            for h in range(LANES // head):
                mine = (lane >= h * head) & (lane < (h + 1) * head)
                query = jnp.where(mine, joint[here, q_at].astype(F32) * SCORE_SCALE, 0.0).astype(BF16)
                slope = jnp.where(mine, slope_all[here, s_at].astype(F32), 0.0).astype(BF16)
                top = lse[p, h : h + 1, here]
                delta = jnp.sum(product[h * head : (h + 1) * head, here], axis=0, keepdims=True)
                key_h = key_t[h * head : (h + 1) * head]
                back = None
                for part in (slice(0, j * rows), here) if j else (here,):
                    scores = dot(joint[part, k_at], query, NT)
                    if part is here:
                        scores = jnp.where(
                            same, scores, jnp.where(earlier, scores + bias[part, :], MASKED)
                        )
                    else:
                        scores = scores + bias[part, :]
                    chances = jnp.exp(scores - top)
                    slopes = dot(joint[part, v_at], slope, NT)
                    grads = (chances * (slopes - delta)).astype(BF16)
                    value_sum[part, :] += dot(chances.astype(BF16), slope)
                    key_sum[part, :] += dot(grads, query)
                    term = dot(key_h[:, part], grads)
                    back = term if back is None else back + term
                query_t[h * head : (h + 1) * head, here] = back * SCORE_SCALE
        grads_out[:, q_at] = query_t[...].T.astype(BF16)
        grads_out[:, k_at] = key_sum[...].astype(BF16)
        grads_out[:, v_at] = value_sum[...].astype(BF16)
    sums[...] = jnp.sum(grads_out[...].astype(F32), axis=0, keepdims=True)
    tile = 256
    for i in range(d // tile):
        here = slice(i * tile, (i + 1) * tile)
        full[here, :] = dot(normed[:, here], grads_out[...], TN).astype(BF16)
    cut = left_keep.shape[1]
    g = lay.size
    side = (spot[1] >> bits_of(lay.planes)) & 1
    cut_rows(full.at[:, 0:cut], side, 2 * g, d // (4 * g), left_keep, left_give)
    side = (spot[1] >> 1) & 1
    cut_rows(full.at[:, cut:], side, g * lay.planes, 2 * lay.each, right_keep, right_give)


def attend_back(lay, spot, bias, joint, wide, lse, normed, slope, cut):
    d, hw, length = lay.width, lay.share, lay.length
    outs = [shaped((length, 3 * hw), BF16)]
    outs += [shaped((d // 2, cut), BF16)] * 2 + [shaped((d // 2, 3 * hw - cut), BF16)] * 2
    outs += [shaped((1, 3 * hw), F32)]
    return kernel_call(
        lay.order,
        functools.partial(attend_back_kernel, lay),
        outs,
        spot,
        bias,
        joint,
        wide,
        lse,
        normed,
        slope,
        name="attend_back",
        smem=(0,),
        scratch=[
            pltpu.VMEM((length, LANES), F32),
            pltpu.VMEM((length, LANES), F32),
            pltpu.VMEM((LANES, length), F32),
            pltpu.VMEM((d, 3 * hw), BF16),
        ],
        vmem=24,
        flops=2 * length * d * 3 * hw + 4 * length * length * d,
    )


def input_kernel(
    lay, spot, grads, w, x, sums_two, joint_sum, bias_up_sum, keep, give, sums, sums_low
):
    rows, g, hw = lay.rows, lay.size, lay.share
    gain = jnp.zeros((1, lay.width), F32)
    shift = jnp.zeros((1, lay.width), F32)
    for i in range(2 * g):
        here = slice(i * rows, (i + 1) * rows)
        part = dot(grads[here, :], w[...], NT)
        normal, _ = centre(x[here, :].astype(F32))
        gain = gain + jnp.sum(part * normal, axis=0, keepdims=True)
        shift = shift + jnp.sum(part, axis=0, keepdims=True)
        low = part.astype(BF16)
        at = slice((i % g) * rows, (i % g + 1) * rows)

        @pl.when(spot[8] == i // g)
        def _():
            keep[at, :] = low

        @pl.when(spot[8] != i // g)
        def _():
            give[at, :] = low

    sums[...] = jnp.zeros_like(sums)
    sums[0:1, :] = gain
    sums[1:2, :] = shift
    mine = pl.ds(pl.multiple_of(spot[5] * hw, hw), hw)
    sums[2:3, mine] = joint_sum[:, 0:hw]
    sums[3:4, mine] = joint_sum[:, 2 * hw :]
    sums[4:8, :] = sums_two[0:4, :]
    piece = lay.piece

    def write(m):
        for b in range(2 * lay.planes):
            at = up_column(lay, b, m)
            line, column = 8 + at // lay.width, at % lay.width
            sums[line : line + 1, column : column + piece] = bias_up_sum[:, b * piece : (b + 1) * piece]

    for m in range(lay.members):
        pl.when(spot[5] == m)(functools.partial(write, m))
    sums_low[...] = sums[...].astype(BF16)


SUM_ROWS = 16


def up_column(lay, b, member):
    top, plane = b // lay.planes, b % lay.planes
    chip = top * lay.size + member // 2
    return ((chip * lay.planes + plane) * 2 + member % 2) * lay.piece


def sum_rows(width, columns):
    return -(-width // columns) * SUM_ROWS


def put_sums(ref, base, total):
    width, columns = total.shape[1], ref.shape[1]
    for k in range(-(-width // columns)):
        part = total[:, k * columns : min(width, (k + 1) * columns)]
        at = slice(base + k * SUM_ROWS, base + (k + 1) * SUM_ROWS)
        if part.shape[1] < columns:
            ref[at, :] = jnp.zeros((SUM_ROWS, columns), BF16)
        ref[at, 0 : part.shape[1]] = part.astype(BF16)


def take_sums(ref, base, width):
    columns = ref.shape[1]
    parts = []
    for k in range(-(-width // columns)):
        at = slice(base + k * SUM_ROWS, base + (k + 1) * SUM_ROWS)
        parts.append(ref[at, 0 : min(columns, width - k * columns)].astype(F32))
    return parts[0] if len(parts) == 1 else jnp.concatenate(parts, axis=1)


def input_call(lay, spot, grads, w, x, sums_two, joint_sum, bias_up_sum):
    d, rows, g = lay.width, lay.rows, lay.size
    small = (SUM_ROWS, d)
    return kernel_call(
        lay.order,
        functools.partial(input_kernel, lay),
        [shaped((g * rows, d), BF16)] * 2 + [shaped(small, F32), shaped(small, BF16)],
        spot,
        grads,
        w,
        x,
        sums_two,
        joint_sum,
        bias_up_sum,
        name="input_slope",
        smem=(0,),
        vmem=24,
        flops=2 * lay.length * d * 3 * lay.share,
    )


def fold_into(spot, cut, keep, came, hold, give, rows=None):
    slot, shift, a = cut
    count = keep.shape[0]
    b = count // (2 * a)
    side = (spot[slot] >> shift) & 1
    half = a * b

    def write(s):
        for i in range(a):
            for ref, t in ((hold, s), (give, 1 - s)):
                at = slice((2 * i + t) * b, (2 * i + t + 1) * b)
                value = keep[at, :].astype(F32) + came[at, :].astype(F32)
                ref[i * b : (i + 1) * b, :] = value.astype(BF16)

    each_way(side, write)


def two_fold_kernel(cuts, spot, one, one_came, two, two_came, one_keep, one_give, two_keep, two_give):
    fold_into(spot, cuts[0], one, one_came, one_keep, one_give)
    fold_into(spot, cuts[1], two, two_came, two_keep, two_give)


def two_fold(lay, spot, cuts, one, one_came, two, two_came):
    outs = []
    for v in (one, two):
        outs += [shaped((v.shape[0] // 2, v.shape[1]), BF16)] * 2
    return kernel_call(
        lay.order,
        functools.partial(two_fold_kernel, cuts),
        outs,
        spot,
        one,
        one_came,
        two,
        two_came,
        name="two_fold",
        smem=(0,),
    )


def sums_fold_kernel(
    cuts, spot, one, one_came, two, two_came, sums, sums_came, one_keep, one_give, two_keep, two_give, sums_out
):
    n, half, width = one.shape[0], one_keep.shape[0], sums.shape[1]
    if one_came.shape[0] > n:
        came = take_sums(one_came, n, width)
    else:
        came = sums_came[...].astype(F32)
    total = sums[...] + came
    sums_out[...] = total
    fold_into(spot, cuts[0], one, one_came, one_keep, one_give)
    put_sums(one_give, half, total)
    fold_into(spot, cuts[1], two, two_came, two_keep, two_give)


def sums_fold(lay, spot, cuts, one, one_came, two, two_came, sums, sums_came):
    half, other = one.shape[0] // 2, two.shape[0] // 2
    outs = [
        shaped((half, one.shape[1]), BF16),
        shaped((half + sum_rows(sums.shape[1], one.shape[1]), one.shape[1]), BF16),
        shaped((other, two.shape[1]), BF16),
        shaped((other, two.shape[1]), BF16),
        shaped(sums.shape, F32),
    ]
    args = (spot, one, one_came, two, two_came, sums, sums_came)
    return kernel_call(
        lay.order, functools.partial(sums_fold_kernel, cuts), outs, *args, name="sums_fold", smem=(0,)
    )


def top_fold_kernel(shift, spot, one, one_came, two, two_came, sums, keep, give, sums_out):
    n, cut = one.shape
    half = n // 2
    total = sums[...] + take_sums(one_came, n, sums.shape[1])
    sums_out[...] = total
    put_sums(give, half, total)

    def write(s):
        for here, x, y in ((slice(0, cut), one, one_came), (slice(cut, None), two, two_came)):
            for ref, t in ((keep, s), (give, 1 - s)):
                at = slice(t * half, (t + 1) * half)
                value = x[at, :].astype(F32) + y[at, :].astype(F32)
                ref[0:half, here] = value.astype(BF16)

    each_way((spot[0] >> shift) & 1, write)


def top_pair_kernel(shift, spot, one, one_came, two, two_came, one_keep, two_keep, give):
    half = one_keep.shape[0]

    def write(s):
        for i, (x, y, keep) in enumerate(((one, one_came, one_keep), (two, two_came, two_keep))):
            for ref, t in ((keep, s), (give.at[i], 1 - s)):
                at = slice(t * half, (t + 1) * half)
                ref[...] = (x[at, :].astype(F32) + y[at, :].astype(F32)).astype(BF16)

    each_way((spot[0] >> shift) & 1, write)


def home_first_kernel(slot, shift, spot, w_in, w_in_came, w_up, w_up_came, sums, keep, give, sums_out):
    n, cut = w_in.shape
    half = n // 2
    w_up_came = w_up_came.at[0] if len(w_up_came.shape) > len(w_up.shape) else w_up_came
    total = sums[...] + take_sums(w_in_came, n, sums.shape[1])
    sums_out[...] = total
    put_sums(give, half, total)

    def write(s):
        for here, x, y in ((slice(0, cut), w_in, w_in_came), (slice(cut, None), w_up, w_up_came)):
            for ref, t in ((keep, s), (give, 1 - s)):
                at = slice(t * half, (t + 1) * half)
                value = x[at, :].astype(F32) + y[at, :].astype(F32)
                ref[0:half, here] = value.astype(BF16)

    each_way((spot[slot] >> shift) & 1, write)


def home_next_kernel(slot, shift, spot, mine, came, sums, *refs):
    keep, give, sums_out = refs[-3:]
    n, columns = mine.shape
    half = n // 2
    total = sums[...] + take_sums(came, max(n, 16), sums.shape[1])
    sums_out[...] = total
    put_sums(give, max(half, 16), total)

    def write(s):
        for here, x in ((slice(0, columns), mine), (slice(columns, 2 * columns), came)):
            for ref, t in ((keep, s), (give, 1 - s)):
                put_rows(ref, here, x, t * half, half)
        if len(refs) > 3:
            total = (refs[0][...].astype(F32) + refs[1][...].astype(F32)).astype(BF16)
            for ref, t in ((keep, s), (give, 1 - s)):
                put_rows(ref, slice(2 * columns, None), total, t * half, half)

    each_way((spot[slot] >> shift) & 1, write)


def put_rows(ref, columns, source, start, count):
    if count >= 16:
        ref[0:count, columns] = source[start : start + count, :]
        return
    value = source[0:16, :].astype(F32)[start : start + count]
    value = jnp.concatenate([value, jnp.zeros((16 - count, value.shape[1]), F32)], axis=0)
    ref[0:16, columns] = value.astype(BF16)


def home_last_kernel(lay, spot, mine, came, sums, w_in, w_up, w_out, *vectors):
    n = lay.each
    hw, piece, cut = lay.share, lay.piece, 3 * lay.share
    span = cut + lay.ff_share
    for f, ref in enumerate((mine, came)):
        for e in range(lay.size):
            place = 0
            for k in range(bits_of(lay.size)):
                place |= ((e >> k) & 1) << (bits_of(lay.size) - 1 - k)
            member = (spot[4] ^ place) * 2 + (spot[2] ^ f)

            def write(m, ref=ref, e=e):
                for i in range(3):
                    at = i * lay.width + m * hw
                    start = e * span + i * hw
                    w_in[:, at : at + hw] = ref[0 : max(n, 16), start : start + hw].astype(F32)[0:n]
                for b in range(2 * lay.planes):
                    at = up_column(lay, b, m)
                    start = e * span + cut + b * piece
                    value = ref[0 : max(n, 16), start : start + piece].astype(F32)
                    w_up[:, at : at + piece] = value[0:n]

            for m in range(lay.members):
                pl.when(member == m)(functools.partial(write, m))
    half = lay.width // 2

    def write_out(side):
        for ref, s in ((mine, side), (came, 1 - side)):
            at = ref.shape[1] - half
            w_out[:, s * half : (s + 1) * half] = ref[0 : max(n, 16), at:].astype(F32)[0:n]

    each_way(spot[2], write_out)
    total = sums[...] + take_sums(came, max(n, 16), lay.width)

    def part_of(start, count):
        source, target = iota((lay.width, count), 0), iota((lay.width, count), 1)
        move = (source == start + target).astype(F32)
        return jnp.dot(total, move, precision=lax.Precision.HIGHEST)

    own = part_of(spot[7] * n, n)
    for v in range(8):
        vectors[v][...] = own[v : v + 1, :]
    first = spot[7] * piece
    own = part_of(first % lay.width, piece)
    line = iota(own.shape, 0) == 8 + first // lay.width
    vectors[8][...] = jnp.sum(jnp.where(line, own, 0.0), axis=0, keepdims=True)


def add_kernel(one, two, out):
    other = two[1] if len(two.shape) > len(one.shape) else two[...]
    out[...] = (one[...].astype(F32) + other.astype(F32)).astype(out.dtype)


def last_kernel(spot, vecs, keep, came, sent, own, grad_middle, out):
    total = keep[...].astype(F32) + came[...].astype(F32)
    slope = jnp.where(spot[6] == 1, total, sent[...].astype(F32))
    normal, scale = centre(own[...].astype(F32))
    out[...] = (grad_middle[...] + norm_back(slope, normal, scale, vecs[0:1, :])).astype(BF16)


def out_kernel(vecs, middle, keep, came, out):
    total = keep[...].astype(F32) + came[...].astype(F32)
    out[...] = (middle[...] + (total + vecs[7:8, :])).astype(BF16)


def solution(mesh):
    nb, nt = mesh.shape["blk"], mesh.shape["batch"]
    devices = nb * nt
    group_size = nb // 2
    total_bits = bits_of(devices)
    plane_bits = list(range(1, bits_of(nt)))
    group_bits = list(range(bits_of(nt), bits_of(nt) + bits_of(group_size)))
    top_bit = total_bits - 1
    members = 2 * group_size

    def at_home(i):
        return (i // nt) // group_size == i % 2

    def send(value, route):
        return lax.ppermute(value, AXES, route)

    def flip(value, bit, who=None):
        return send(value, [(i, i ^ (1 << bit)) for i in range(devices) if who is None or who(i)])

    def mirror(i):
        return (nb - 1 - i // nt) * nt + i % nt

    def local(
        hidden_in,
        key_mask,
        lengths,
        first_gain,
        first_shift,
        input_weight,
        query_bias,
        value_bias,
        output_weight,
        output_bias,
        second_gain,
        second_shift,
        up_weight,
        up_bias,
        down_weight,
        down_bias,
        cotangent,
    ):
        rows, width = hidden_in.shape[1:]
        length = key_mask.shape[1]
        head = width // HEADS
        blk, lane_id = lax.axis_index("blk"), lax.axis_index("batch")
        index = blk * nt + lane_id
        core = lane_id % 2
        group, place = blk // group_size, blk % group_size
        member = place * 2 + core
        home = group == core
        share = width // members
        ff = up_weight.shape[1]
        piece = ff // devices

        def bit(b):
            return (index >> b) & 1

        def ordered(mine, theirs, side, axis):
            return jnp.where(
                side == 0,
                jnp.concatenate([mine, theirs], axis),
                jnp.concatenate([theirs, mine], axis),
            )

        def side_of(value, side, axis):
            lo, hi = jnp.split(value, 2, axis)
            return jnp.where(side == 0, lo, hi)

        lay = Layout(nb, nt, rows, width, ff, length)
        each = lay.each
        own = hidden_in[0]
        kept_group = jnp.where(home, group, 1 - group)
        kept_place = jnp.where(home, place, group_size - 1 - place)
        spot = jnp.stack(
            [blk, lane_id, core, group, place, member, home.astype(jnp.int32), index]
            + [kept_group, kept_place]
        )
        away = lambda i: not at_home(i)
        across = [(i, mirror(i) ^ 1) for i in range(devices) if away(i)]
        mirrored = [(i, mirror(i)) for i in range(devices)]

        call = functools.partial(kernel_call, lay.order)
        wide_in = 3 * group_size * share + 2 * group_size * lay.planes * piece
        row = lambda value: value.reshape(1, -1)
        vectors = [
            row(v)
            for v in (
                first_gain,
                first_shift,
                query_bias,
                value_bias,
                output_bias,
                second_gain,
                second_shift,
                down_bias,
                up_bias,
            )
        ]

        def spread_group(values, who=None):
            for b in group_bits:
                values = values + [flip(v, b, who) for v in values]
            return values

        start = [input_weight, up_weight, key_mask, output_weight] + vectors
        half = width // 2
        base = max(each, 16)
        give, keep = call(
            functools.partial(pack_kernel, lay),
            [shaped((base + EXTRA, wide_in + half), BF16)] * 2,
            spot,
            lengths,
            *start,
            name="pack",
            smem=(0, 1),
            away=tuple(range(2, 15)),
            vmem=60,
            scratch=[pltpu.VMEM(v.shape, v.dtype) for v in start] + [pltpu.SemaphoreType.DMA((13,))],
        )
        came_w = flip(give, 0)
        far = [send(own, across)]
        near = spread_group([own])
        downs = down_weight[None]
        downs_came = flip(downs, plane_bits[-1])
        grad_low = call(
            mask_kernel,
            [shaped((rows, width), BF16)],
            spot,
            lengths,
            cotangent[0],
            name="mask",
            smem=(0, 1),
        )[0]
        count = group_size
        for step, b in enumerate(group_bits):
            tall = (2 << step) * each
            columns = wide_in >> (step + 1)
            give, keep, ready = call(
                functools.partial(trade_kernel, lay, step, count),
                [shaped((tall + EXTRA, columns + half), BF16)] * 2 + [shaped((8, length), F32)],
                spot,
                keep,
                came_w,
                name="trade",
                smem=(0,),
                scratch=[pltpu.VMEM((tall, 2 * columns + half), BF16)],
                after=(far[0], *near[1:], downs_came) if step == 0 else (),
            )
            valid = ready if step == 0 else valid
            came_w = flip(give, b)
            count //= 2
        for b in reversed(plane_bits[:-1]):
            downs = join(lay, downs, downs_came)
            downs_came = flip(downs, b)
        tall = members * each
        paired = ff // members == width
        up_tall = tall + tall * half // (ff // members)
        in_block, ups, far_later, pair = call(
            functools.partial(settle_kernel, lay, len(group_bits)),
            [
                shaped((tall + EXTRA, 3 * share), BF16),
                shaped((1, up_tall, ff // members), BF16),
                shaped(own.shape, BF16),
                shaped((up_tall + piece, width) if paired else (8, LANES), BF16),
            ],
            spot,
            keep,
            came_w,
            far[0],
            down_weight,
            name="settle",
            smem=(0,),
            scratch=[pltpu.VMEM((tall, 3 * share + ff // members + half), BF16)],
        )
        far = far + spread_group([far_later], away)[1:]
        ups_first = ups
        ups_came = flip(ups, plane_bits[0])
        bundle = call(
            functools.partial(bundle_kernel, group_size),
            [shaped((2 * group_size * rows, width), BF16)],
            spot,
            *near,
            *far,
            name="bundle",
            smem=(0,),
            after=(downs_came,),
        )[0]
        rows_came = flip(bundle, 0)
        cut = max(LANES, 3 * share // 2 // LANES * LANES)
        left, right, pair, grad_later = call(
            functools.partial(split_kernel, cut),
            [
                shaped((2, tall + EXTRA, cut), BF16),
                shaped((2, tall + EXTRA, 3 * share - cut), BF16),
                shaped(pair.shape, BF16),
                shaped(grad_low.shape, BF16),
            ],
            in_block,
            flip(in_block, top_bit),
            pair,
            grad_low,
            name="split",
            after=(ups_came,),
        )
        left_came, right_came = flip(left, plane_bits[0]), flip(right, plane_bits[-1])
        if paired:
            pair_came = flip(pair, top_bit)
        else:
            up_far, down_far = flip(ups_first, top_bit), flip(down_weight, top_bit)[None]
        down_m = [grad_low] + spread_group([grad_later])[1:]
        for k, (b, c) in list(enumerate(zip(plane_bits, reversed(plane_bits), strict=True)))[1:]:
            after = (rows_came,) if k == 1 else ()
            left, right = stack(lay, left, left_came, right, right_came, *after)
            left_came, right_came = flip(left, b), flip(right, c)
        in_pieces = (left, left_came, right, right_came)
        vecs = call(
            functools.partial(vector_kernel, lay),
            [shaped((16, width), F32)],
            spot,
            left,
            left_came,
            name="vectors",
            smem=(0,),
            away=(1, 2),
            scratch=[
                pltpu.VMEM((2 * lay.planes * EXTRA, -(-lay.small // LANES) * LANES), BF16),
                pltpu.SemaphoreType.DMA((2 * lay.planes,)),
            ],
        )[0]
        for b in plane_bits[1:]:
            ups = join(lay, ups, ups_came)
            ups_came = flip(ups, b)

        key_bias = jnp.where(valid[0] > 0.5, 0.0, MASKED).astype(F32).reshape(length, 1)
        near_att, far_att, joint, wide, lse, normed_one, x_all, w_in = attend(
            lay, spot, key_bias, vecs, near + far + [rows_came], in_pieces
        )
        far_att = [send(far_att, mirrored)]
        near_att = spread_group([near_att])
        att_c = [flip(near_att[0], 0)]

        if paired:
            up_far, down_far = call(
                unpair_kernel,
                [shaped((1, up_tall, width), BF16), shaped((1, piece, width), BF16)],
                pair_came,
                name="unpair",
                after=(ups_came, *down_m[1:]),
            )
        out_shape = [shaped((lay.planes, tall, half), BF16)]
        outs_w = []
        for k, (b, c) in enumerate(zip(plane_bits, reversed(plane_bits), strict=True)):
            if k:
                up_far, down_far = stack(
                    lay, up_far, up_far_came, down_far, down_far_came, att_c[0], outs_c
                )
            up_far_came, down_far_came = flip(up_far, b), flip(down_far, c)
            if k == 0:
                outs_w += call(out_kernel_rows, out_shape, ups, ups_came, name="out_rows")
                outs_c = flip(outs_w[0], 0)
        down_c = [flip(v, 0) for v in down_m]
        far_att = spread_group(far_att)
        att_c += [flip(v, 0) for v in near_att[1:] + far_att]
        outs_w += call(out_kernel_rows, out_shape, up_far, up_far_came, name="out_rows")
        out_blocks = (*outs_w, outs_c, flip(outs_w[1], 0))
        up_blocks = (ups, ups_came, up_far, up_far_came)
        down_blocks = (downs, downs_came, down_far, down_far_came)

        (
            dn_keep,
            dn_give,
            middle,
            att_own,
            normed_two,
            act,
            grad_pre,
            d_bias_up,
            w_out,
        ) = forward_call(
            lay,
            spot,
            vecs,
            out_blocks,
            near_att + far_att + att_c + near + down_m + down_c + [rows_came],
            up_blocks + down_blocks,
        )

        def reduce_group(keep, came, slot):
            for k in reversed(range(len(group_bits))):
                keep, give = fold(lay, spot, slot, k, 1, keep, came)
                came = flip(give, group_bits[k])
            return keep, came

        planes_down = list(reversed(plane_bits))
        top_shift = bits_of(group_size)

        def cuts_of(lead, order):
            here, cuts = list(planes_down), []
            for b in order:
                cuts.append((1, b, lead << here.index(b)))
                here.remove(b)
            return cuts

        dn_keep, dn_came = reduce_group(dn_keep, flip(dn_give, 0), 4)
        up_keep, up_give, down_keep, down_give, out_keep, out_give = gradient_call(
            lay, spot, normed_two, act, grad_pre, down_m, down_c, down_blocks
        )
        up_came, down_came = flip(up_give, planes_down[0]), flip(down_give, plane_bits[0])
        out_came = flip(out_give, 0)
        slope_keep, slope_give, grad_middle, grad_branch, sums_two = turn_call(
            lay, spot, vecs, dn_keep, dn_came, middle, grad_low, w_out
        )
        pieces = call(
            functools.partial(pick_kernel, lay),
            [shaped((rows, share), BF16)] * members,
            spot,
            slope_keep,
            flip(slope_give, 0),
            name="pick",
            smem=(0,),
        )
        parts = [pieces[0]]
        for r in range(1, members):
            parts.append(send(pieces[r], [(i, i ^ (r * nt)) for i in range(devices)]))
        o_keep, o_give = call(
            outer_kernel,
            [shaped((width, width // 2), BF16)] * 2,
            spot,
            att_own,
            grad_branch,
            name="output_gradient",
            smem=(0,),
        )
        o_came = flip(o_give, 0)
        out_keep, out_came = reduce_group(out_keep, out_came, 4)
        out_cuts = [(4, k, 2) for k in reversed(range(len(group_bits)))]
        out_cuts += cuts_of(2, planes_down) + [(0, top_shift, 1)]
        out_bits = list(reversed(group_bits)) + planes_down + [top_bit]
        out_steps = iter(range(len(out_bits)))

        def next_out(keep, came, count=1):
            for _ in range(count):
                k = next(out_steps)
                keep, give = fold(lay, spot, *out_cuts[k], keep, came)
                came = flip(give, out_bits[k])
            return keep, came

        o_keep, o_came = next_out(o_keep, o_came)
        slope = call(
            functools.partial(assemble_kernel, lay),
            [shaped((length, share), BF16)],
            spot,
            *parts,
            name="assemble",
            smem=(0,),
        )[0]
        up_cuts, down_cuts = cuts_of(members, planes_down), cuts_of(2, plane_bits)

        def next_planes(k, up_keep, up_came, down_keep, down_came):
            up_keep, up_give, down_keep, down_give = two_fold(
                lay, spot, (up_cuts[k], down_cuts[k]), up_keep, up_came, down_keep, down_came
            )
            return up_keep, flip(up_give, planes_down[k]), down_keep, flip(down_give, plane_bits[k])

        for k in range(1, len(plane_bits)):
            up_keep, up_came, down_keep, down_came = next_planes(
                k, up_keep, up_came, down_keep, down_came
            )

        grad_joint, left_keep, left_give, right_keep, right_give, joint_sum = attend_back(
            lay, spot, key_bias, joint, wide, lse, normed_one, slope, cut
        )
        left_came, right_came = flip(left_give, planes_down[0]), flip(right_give, plane_bits[0])
        if paired:
            shape = (up_keep.shape[0] // 2, up_keep.shape[1])
            up_keep, down_keep, give = call(
                functools.partial(top_pair_kernel, top_shift),
                [shaped(shape, BF16), shaped(shape, BF16), shaped((2,) + shape, BF16)],
                spot,
                up_keep,
                up_came,
                down_keep,
                down_came,
                name="top_pair",
                smem=(0,),
                after=(o_came,),
            )
            far_came = flip(give, top_bit)
        else:
            up_keep, up_give, down_keep, down_give = two_fold(
                lay, spot, ((0, top_shift, 1),) * 2, up_keep, up_came, down_keep, down_came
            )
            far_came = (flip(up_give, top_bit), flip(down_give, top_bit))
        in_keep, in_give, sums, sums_give = input_call(
            lay, spot, grad_joint, w_in, x_all, sums_two, joint_sum, d_bias_up
        )
        sums_came = flip(sums_give, planes_down[0])
        in_came = flip(in_give, 0)
        left_cuts, right_cuts = cuts_of(members, planes_down), cuts_of(members, plane_bits)
        for k in range(1, len(plane_bits)):
            left_keep, left_give, right_keep, right_give, sums = sums_fold(
                lay,
                spot,
                (left_cuts[k], right_cuts[k]),
                left_keep,
                left_came,
                right_keep,
                right_came,
                sums,
                sums_came,
            )
            left_came, right_came = flip(left_give, planes_down[k]), flip(right_give, plane_bits[k])
        in_keep, in_came = reduce_group(in_keep, in_came, 9)
        o_keep, o_came = next_out(o_keep, o_came, len(group_bits))
        layer_out = call(
            out_kernel,
            [shaped((rows, width), BF16)],
            vecs,
            middle,
            out_keep,
            out_came,
            name="layer_out",
        )[0]

        small = (SUM_ROWS, width)
        tall = left_keep.shape[0] // 2
        w_keep, w_give, sums = call(
            functools.partial(top_fold_kernel, top_shift),
            [
                shaped((tall, 3 * share), BF16),
                shaped((tall + sum_rows(width, 3 * share), 3 * share), BF16),
                shaped(small, F32),
            ],
            spot,
            left_keep,
            left_came,
            right_keep,
            right_came,
            sums,
            name="top_fold",
            smem=(0,),
        )
        w_came = flip(w_give, top_bit)
        in_sum = call(add_kernel, [shaped((rows, width), BF16)], in_keep, in_came, name="add")[0]
        sent = send(in_sum, across)
        o_keep, o_came = next_out(o_keep, o_came, len(plane_bits) - 1)
        up_came, down_came = (far_came, far_came) if paired else far_came
        d_down = call(
            add_kernel, [shaped((piece, width), F32)], down_keep, down_came, name="add"
        )[0]
        came = w_came
        columns = 3 * share + ff // members
        steps = [(4, k, b) for k, b in reversed(list(enumerate(group_bits)))] + [(2, 0, 0)]
        for step, (slot, shift, b) in enumerate(steps):
            tall //= 2
            outs = [
                shaped((max(tall, 16), columns), BF16),
                shaped((max(tall, 16) + sum_rows(width, columns), columns), BF16),
                shaped(small, F32),
            ]
            if step == 0:
                w_keep, w_give, sums = call(
                    functools.partial(home_first_kernel, slot, shift),
                    outs,
                    spot,
                    w_keep,
                    came,
                    up_keep,
                    up_came,
                    sums,
                    name="home_first",
                    smem=(0,),
                )
                came = flip(w_give, b)
                o_keep, o_came = next_out(o_keep, o_came)
                input_gradient = call(
                    last_kernel,
                    [shaped((rows, width), BF16)],
                    spot,
                    vecs,
                    in_keep,
                    in_came,
                    sent,
                    own,
                    grad_middle,
                    name="input_gradient",
                    smem=(0,),
                )[0]
            else:
                final = (o_keep, o_came) if b == 0 else ()
                if final:
                    outs = [shaped((v.shape[0], columns + width // 2), BF16) for v in outs[:2]] + outs[2:]
                w_keep, w_give, sums = call(
                    functools.partial(home_next_kernel, slot, shift),
                    outs,
                    spot,
                    w_keep,
                    came,
                    sums,
                    *final,
                    name="home_next",
                    smem=(0,),
                )
                came = flip(w_give, b)
            columns *= 2
        d_in, d_up, d_out, *vectors = call(
            functools.partial(home_last_kernel, lay),
            [shaped((each, 3 * width), F32), shaped((each, ff), F32), shaped((each, width), F32)]
            + [shaped((1, each), F32)] * 8
            + [shaped((1, piece), F32)],
            spot,
            w_keep,
            came,
            sums,
            name="home_last",
            smem=(0,),
        )
        vectors = [v.reshape(-1) for v in vectors]
        return (
            layer_out[None],
            input_gradient[None],
            vectors[0],
            vectors[1],
            d_in,
            vectors[2],
            vectors[3],
            d_out,
            vectors[4],
            vectors[5],
            vectors[6],
            d_up,
            vectors[8],
            d_down,
            vectors[7],
        )

    vector, matrix = P(AXES), P(AXES, None)
    tokens = P("batch", "blk", None)
    return jax.shard_map(
        local,
        mesh=mesh,
        in_specs=(
            tokens,
            P("batch", None),
            P("batch"),
            vector,
            vector,
            matrix,
            vector,
            vector,
            matrix,
            vector,
            vector,
            vector,
            matrix,
            vector,
            matrix,
            vector,
            tokens,
        ),
        out_specs=(
            tokens,
            tokens,
            vector,
            vector,
            matrix,
            vector,
            vector,
            matrix,
            vector,
            vector,
            vector,
            matrix,
            vector,
            matrix,
            vector,
        ),
        check_vma=False,
    )
```

```python
import functools

import jax
import jax.numpy as jnp
from jax import lax
from jax.experimental import pallas as pl
from jax.experimental.pallas import tpu as pltpu
from jax.sharding import PartitionSpec as P

HEADS = 16
EPSILON = 1e-05
SCORE_SCALE = 0.125
MASKED = -1e30
LANES = 128
AXES = ("blk", "batch")
F32 = jnp.float32
BF16 = jnp.bfloat16

NT = (((1,), (1,)), ((), ()))
NN = (((1,), (0,)), ((), ()))
TN = (((0,), (0,)), ((), ()))


def dot(a, b, dims=NN):
    return lax.dot_general(a, b, dims, preferred_element_type=F32)


def bits_of(size):
    return size.bit_length() - 1


def key_mask_terms(rows):
    key = lax.broadcasted_iota(jnp.int32, (rows, rows), 0)
    query = lax.broadcasted_iota(jnp.int32, (rows, rows), 1)
    return key < query, key == query


def centre(values):
    average = jnp.mean(values, axis=-1, keepdims=True)
    centred = values - average
    variance = jnp.mean(centred * centred, axis=-1, keepdims=True)
    scale = lax.rsqrt(variance + EPSILON)
    return centred * scale, scale


def norm_back(slope, normal, scale, gain):
    weighted = slope * gain
    return scale * (
        weighted
        - jnp.mean(weighted, axis=-1, keepdims=True)
        - normal * jnp.mean(weighted * normal, axis=-1, keepdims=True)
    )


GELU_A = 0.7978845608028654
GELU_B = 0.044715


def gelu_terms(pre):
    square = pre * pre
    bend = jnp.tanh(GELU_A * pre * (1.0 + GELU_B * square))
    half = 0.5 * (1.0 + bend)
    slope = half + 0.5 * pre * (1.0 - bend * bend) * (GELU_A * (1.0 + 3.0 * GELU_B * square))
    return pre * half, slope


EXTRA = 16


WEIGHTS = {'pack': 10000000000, 'unpair': 10000000000, 'trade': 1, 'join_down': 1, 'mask': 1}
FREE = {'trade': [0]}
WAITS = {}
GRANTS = {'o2': 32}
HEAVY = 10**11
PLAN = (
    "pack",
    "mask",
    "trade",
    "join_down",
    "settle",
    "bundle",
    "split",
    "stack",
    "vectors",
    "join_up",
    "attend",
    "unpair",
    "stack_far",
    "relay",
    "rows_own",
    "rows_far",
    "forward",
    "fold_norm",
    "gradients",
    "turn",
    "pick",
    "outer",
    "out_fold",
    "o0",
    "assemble",
    "planes",
    "attend_back",
    "top_pair",
    "input",
    "lr",
    "dn1",
    "o1",
    "top",
    "o2",
    "add",
    "layer",
    "d_down",
    "home0",
    "o3",
    "last",
    "home1",
    "home_last",
)


def shaped(shape, kind):
    return jax.ShapeDtypeStruct(shape, kind)


class Order:
    def __init__(self):
        self.ticket = jnp.zeros((8, LANES), F32)
        self.step = ""
        self.waits = ()


def kernel_call(order, body, outs, *args, name, smem=(), away=(), scratch=(), vmem=8, after=()):
    weight = WEIGHTS.get(order.step, HEAVY)
    after = tuple(v for i, v in enumerate(after) if i not in FREE.get(order.step, ()))
    after, order.waits = after + order.waits, ()
    count, given = len(args), len(outs)
    inner = body

    def body(*refs):
        ins, rest = refs[:count], refs[count + len(after) :]
        before, results, ticket = rest[0], rest[1 : 1 + given], rest[1 + given]
        ticket[...] = before[...]
        inner(*ins, *results, *rest[2 + given :])

    away = tuple(away) + tuple(range(count, count + len(after)))
    args = args + tuple(after) + (order.ticket,)
    outs = list(outs) + [shaped((8, LANES), F32)]

    def spec(i, places):
        if i in places:
            return pl.BlockSpec(memory_space=pl.ANY)
        return pl.BlockSpec(memory_space=pltpu.VMEM)

    ins = [
        pl.BlockSpec(memory_space=pltpu.SMEM) if i in smem else spec(i, away)
        for i in range(len(args))
    ]
    moved = sum(v.size * v.dtype.itemsize for v in args + tuple(outs))
    *results, order.ticket = pl.pallas_call(
        body,
        in_specs=ins,
        out_specs=[spec(i, ()) for i in range(len(outs))],
        out_shape=list(outs),
        scratch_shapes=list(scratch),
        compiler_params=pltpu.CompilerParams(vmem_limit_bytes=GRANTS.get(order.step, vmem) * 2**20),
        cost_estimate=pl.CostEstimate(flops=weight, bytes_accessed=1, transcendentals=0),
        name=name,
    )(*args)
    return results


def iota(shape, dim):
    return lax.broadcasted_iota(jnp.int32, shape, dim)


class Layout:
    def __init__(self, nb, nt, rows, width, ff, length):
        self.nb, self.nt, self.rows, self.width, self.ff, self.length = nb, nt, rows, width, ff, length
        self.devices = nb * nt
        self.size = nb // 2
        self.planes = nt // 2
        self.members = 2 * self.size
        self.each = width // self.devices
        self.piece = ff // self.devices
        self.share = width // self.members
        self.ff_share = ff // self.members
        self.small = 8 * self.each + self.piece
        self.valid_at = -(-self.small // 512) * 512
        self.head = width // HEADS
        self.order = Order()


def each_way(flag, write):
    pl.when(flag == 0)(lambda: write(0))
    pl.when(flag == 1)(lambda: write(1))


def write_half(lay, side, count, in_from, up_from, in_start, up_start, give, keep, n):
    hw, pc = lay.share, lay.piece
    tail = lay.planes * pc if count > 0 else pc
    spans = []
    if count == 0:
        for q in range(3 * lay.size):
            spans.append((in_from, in_start + 2 * q * hw, hw))
        for q in range(2 * lay.size * lay.planes):
            spans.append((up_from, up_start + 2 * q * pc, pc))
    else:
        for q in range(3 * count // 2):
            spans.append((in_from, in_start + 2 * q * hw, hw))
        for q in range(count):
            spans.append((up_from, up_start + 2 * q * tail, tail))
    at = 0
    for source, start, span in spans:
        mine = source[0:n, start + side * span : start + (side + 1) * span]
        other = source[0:n, start + (1 - side) * span : start + (2 - side) * span]
        keep[0:n, at : at + span] = mine
        give[0:n, at : at + span] = other
        at += span


def load_all(pairs, sems):
    copies = [pltpu.make_async_copy(a, b, sems.at[i]) for i, (a, b) in enumerate(pairs)]
    for copy in copies:
        copy.start()
    return copies


def wait_all(copies):
    for copy in copies:
        copy.wait()


def pack_kernel(lay, spot, lengths, *refs):
    sources, (give, keep), targets, sems = refs[:13], refs[13:15], refs[15:28], refs[28]
    wait_all(load_all(list(zip(sources, targets, strict=True)), sems))
    w_in, w_up, mask, w_out = targets[:4]
    smalls = targets[4:]
    n = lay.each
    base = max(n, 16)
    if base > n:
        for ref in (give, keep):
            ref[0:base, :] = jnp.zeros((base, ref.shape[1]), BF16)
    each_way(spot[2], lambda side: write_half(lay, side, 0, w_in, w_up, 0, 0, give, keep, n))
    half = lay.width // 2
    last = give.shape[1] - half

    def write_out(side):
        keep[0:n, last:] = w_out[:, side * half : (side + 1) * half]
        give[0:n, last:] = w_out[:, (1 - side) * half : (2 - side) * half]

    each_way(spot[2], write_out)
    line = jnp.zeros((1, lay.small), F32)
    at = 0
    for ref in smalls:
        span = ref.shape[1]
        where = iota((span, lay.small), 1) == iota((span, lay.small), 0) + at
        line = line + dot(ref[...], where.astype(F32).astype(BF16))
        at += span
    row = iota((EXTRA, lay.small), 0) == spot[5]
    extra = jnp.where(row, line, 0.0).astype(BF16)
    live = (mask[...] > 0) & (iota(mask.shape, 1) < lengths[0])
    valid = jnp.where(live, 1.0, 0.0) * jnp.ones((EXTRA, 1), F32)
    for ref in (give, keep):
        ref[base : base + EXTRA, :] = jnp.zeros((EXTRA, ref.shape[1]), BF16)
        ref[base : base + EXTRA, 0 : lay.small] = extra
        ref[base : base + EXTRA, lay.valid_at : lay.valid_at + lay.length] = valid.astype(BF16)


def merge_rows(keep, came, side, n, out):
    if n < 16:
        mine, theirs = keep[0:16, :].astype(F32)[0:n], came[0:16, :].astype(F32)[0:n]
        first = jnp.where(side == 0, mine, theirs)
        second = jnp.where(side == 0, theirs, mine)
        out[...] = jnp.concatenate([first, second], axis=0).astype(BF16)
        return
    out[pl.ds(pl.multiple_of(side * n, n), n), :] = keep[0:n, :]
    out[pl.ds(pl.multiple_of((1 - side) * n, n), n), :] = came[0:n, :]


def merge_extra(lay, keep, came, n):
    n = max(n, 16)
    total = keep[n : n + EXTRA, 0 : lay.small].astype(F32) + came[n : n + EXTRA, 0 : lay.small].astype(F32)
    return total.astype(BF16)


def trade_kernel(lay, step, count, spot, keep, came, give, hold, valid, both):
    n = (1 << step) * lay.each
    merge_rows(keep, came, spot[2] if step == 0 else (spot[4] >> (step - 1)) & 1, n, both)
    start = 3 * count * lay.share
    each_way(
        (spot[4] >> step) & 1,
        lambda side: write_half(lay, side, count, both, both, 0, start, give, hold, 2 * n),
    )
    half = lay.width // 2
    for ref in (give, hold):
        ref[0 : 2 * n, ref.shape[1] - half :] = both[:, both.shape[1] - half :]
    extra = merge_extra(lay, keep, came, n)
    for ref in (give, hold):
        ref[2 * n : 2 * n + EXTRA, :] = jnp.zeros((EXTRA, ref.shape[1]), BF16)
        ref[2 * n : 2 * n + EXTRA, 0 : lay.small] = extra
    if step == 0:
        place = slice(lay.valid_at, lay.valid_at + lay.length)
        base = max(n, 16)
        mine, theirs = (ref[base : base + 16, place].astype(F32)[0:8] for ref in (keep, came))
        valid[...] = jnp.where(spot[6] == 1, mine, theirs)
    else:
        valid[...] = jnp.zeros_like(valid)


def settle_kernel(
    lay, step, spot, keep, came, far, down, in_block, up_block, far_out, pair, both
):
    far_out[...] = far[...]
    n = (1 << step) * lay.each
    merge_rows(keep, came, (spot[4] >> (step - 1)) & 1, n, both)
    cut = 3 * lay.share
    in_block[0 : 2 * n, :] = both[:, 0:cut]
    last = cut + lay.ff_share
    tall, half = 2 * n, lay.width // 2
    chunks = lay.ff_share // half
    part = tall // chunks
    targets = [up_block.at[0]] + ([pair] if pair.shape[0] > 8 else [])
    for ref in targets:
        ref[0:tall, :] = both[:, cut:last]
        for i in range(chunks):
            rows = both[i * part : (i + 1) * part, last:]
            ref[tall : tall + part, i * half : (i + 1) * half] = rows
    if pair.shape[0] > 8:
        pair[tall + part :, :] = down[...]
    in_block[2 * n : 2 * n + EXTRA, :] = jnp.zeros((EXTRA, cut), BF16)
    in_block[2 * n : 2 * n + EXTRA, 0 : lay.small] = merge_extra(lay, keep, came, n)


def split_kernel(cut, mine, came, pair, grad, left, right, pair_out, grad_out):
    pair_out[...] = pair[...]
    grad_out[...] = grad[...]
    left[0], left[1] = mine[:, 0:cut], came[:, 0:cut]
    right[0], right[1] = mine[:, cut:], came[:, cut:]


def stack_kernel(one, one_came, two, two_came, one_out, two_out):
    n = one.shape[0]
    one_out[0:n], one_out[n : 2 * n] = one[...], one_came[...]
    two_out[0:n], two_out[n : 2 * n] = two[...], two_came[...]


def stack(lay, one, one_came, two, two_came, *after):
    outs = [shaped((2 * v.shape[0],) + v.shape[1:], BF16) for v in (one, two)]
    return kernel_call(
        lay.order, stack_kernel, outs, one, one_came, two, two_came, name="stack", after=after
    )


def unpair_kernel(pair, up, down):
    n = up.shape[1]
    up[0], down[0] = pair[0:n, :], pair[n:, :]


def bundle_kernel(g, spot, *refs):
    near, far, out = refs[:g], refs[g : 2 * g], refs[2 * g]
    rows = near[0].shape[0]

    def write(home):
        parts = list(near) if home else list(far) + list(near)
        for i, ref in enumerate(parts):
            out[i * rows : (i + 1) * rows, :] = ref[...]

    each_way(spot[6], write)


def copy_kernel(value, out):
    out[...] = value[...]


def out_kernel_rows(mine, came, out):
    count, tall, half = out.shape
    chunks = mine.shape[2] // half
    part = tall // chunks
    for k in range(count):
        source = (mine if k < count // 2 else came).at[k % (count // 2)]
        for i in range(chunks):
            rows = source[tall : tall + part, i * half : (i + 1) * half]
            out[k, i * part : (i + 1) * part, :] = rows


def join_kernel(one, one_came, out):
    n = one.shape[0]
    out[0:n], out[n : 2 * n] = one[...], one_came[...]


def join(lay, one, one_came, *after):
    out = shaped((2 * one.shape[0],) + one.shape[1:], BF16)
    return kernel_call(lay.order, join_kernel, [out], one, one_came, name="join", after=after)[0]


def block_spot(lay, spot, k, flipped):
    bits = bits_of(lay.planes)
    top = (spot[3] ^ k) & 1
    order = range(bits - 1, -1, -1) if flipped else range(bits)
    plane = spot[1] >> 1
    for position, b in enumerate(order):
        plane = plane ^ (((k >> (position + 1)) & 1) << b)
    return top, plane


def vector_kernel(lay, spot, first, second, out, rows, sems):
    n, count, wide = lay.members * lay.each, 2 * lay.planes, rows.shape[1]
    copies = []
    for k in range(count):
        source = first if k < count // 2 else second
        copy = pltpu.make_async_copy(
            source.at[k % (count // 2), n : n + EXTRA, 0:wide],
            rows.at[k * EXTRA : (k + 1) * EXTRA, :],
            sems.at[k],
        )
        copy.start()
        copies.append(copy)
    for copy in copies:
        copy.wait()
    out[...] = jnp.zeros_like(out)
    tall = count * EXTRA
    line, lane = iota((tall, lay.width), 0), iota((tall, lay.width), 1)
    holder, block = jnp.zeros_like(line), jnp.zeros_like(line)
    for k in range(count):
        top, plane = block_spot(lay, spot, k, False)
        inside = line - k * EXTRA
        here = (inside >= 0) & (inside < EXTRA)
        lead = (top * lay.size + inside // 2) * lay.nt + plane * 2 + inside % 2
        holder = jnp.where(here, jnp.where(inside < lay.members, lead, -1), holder)
        block = jnp.where(here & (inside == spot[5]), top * lay.planes + plane, jnp.where(here, -1, block))
    values = rows[...]
    source, target = iota((wide, lay.width), 0), iota((wide, lay.width), 1)
    for v in range(8):
        spread = (source == v * lay.each + target % lay.each).astype(F32).astype(BF16)
        tiled = jnp.where(lane // lay.each == holder, dot(values, spread), 0.0)
        out[v : v + 1, :] = jnp.sum(tiled, axis=0, keepdims=True)
    spread = (source == 8 * lay.each + target % lay.piece).astype(F32).astype(BF16)
    tiled = jnp.where(lane // lay.piece == block, dot(values, spread), 0.0)
    out[8:9, :] = jnp.sum(tiled, axis=0, keepdims=True)
    hw = lay.share
    mine = pl.ds(pl.multiple_of(spot[5] * hw, hw), hw)
    out[9:10, 0:hw] = out[2:3, mine]
    out[9:10, 2 * hw : 3 * hw] = out[3:4, mine]


def attend_kernel(lay, spot, bias, vecs, *refs):
    g, rows, hw, length, head = lay.size, lay.rows, lay.share, lay.length, lay.head
    near, far, came = refs[:g], refs[g : 2 * g], refs[2 * g]
    near_c = far_c = [came.at[e * rows : (e + 1) * rows, :] for e in range(g)]
    weights = refs[2 * g + 1 : 2 * g + 5]
    near_att, far_att, joint, wide, lse, normed, x, w, x_sems, w_sems = refs[2 * g + 5 :]
    group, place = spot[3], spot[4]
    pending = []
    for e in range(g):
        for side, (at_home, at_away) in enumerate(((near[e], near_c[e]), (far_c[e], far[e]))):
            spot_here = (place if side == 0 else g - 1 - place) ^ e
            spot_here = (group if side == 0 else 1 - group) * g + spot_here
            target = x.at[pl.ds(pl.multiple_of(spot_here * rows, rows), rows), :]
            sem = x_sems.at[side * g + e]
            home = pltpu.make_async_copy(at_home, target, sem)
            visit = pltpu.make_async_copy(at_away, target, sem)
            pl.when(spot[6] == 1)(home.start)
            pl.when(spot[6] == 0)(visit.start)
            pending.append(home)
    count = 2 * lay.planes
    span = 2 * lay.each
    cut = weights[0].shape[-1]
    loads = []
    for k in range(count):
        for side in range(2):
            source = weights[2 * side + (k >= count // 2)]
            top, plane = block_spot(lay, spot, k, side == 1)
            for q in range(g):
                start = ((top * g + q) * lay.planes + plane) * span
                copy = pltpu.make_async_copy(
                    source.at[k % (count // 2), q * span : (q + 1) * span, :],
                    w.at[pl.ds(pl.multiple_of(start, span), span), 0:cut]
                    if side == 0
                    else w.at[pl.ds(pl.multiple_of(start, span), span), cut:],
                    w_sems.at[(k * 2 + side) * g + q],
                )
                copy.start()
                loads.append(copy)
    for copy in pending:
        copy.wait()
    for j in range(length // rows):
        here = slice(j * rows, (j + 1) * rows)
        normal, _ = centre(x[here, :].astype(F32))
        normed[here, :] = (normal * vecs[0:1, :] + vecs[1:2, :]).astype(BF16)
    for copy in loads:
        copy.wait()
    for j in range(length // rows):
        here = slice(j * rows, (j + 1) * rows)
        joint[here, :] = (dot(normed[here, :], w[...]) + vecs[9:10, 0 : 3 * hw]).astype(BF16)
    earlier, same = key_mask_terms(rows)
    lane = iota((rows, LANES), 1)
    for p in range(hw // LANES):
        q_at, k_at, v_at = (slice(i * hw + p * LANES, i * hw + (p + 1) * LANES) for i in range(3))
        value_t = joint[:, v_at].astype(F32).T.astype(BF16)
        for j in range(length // rows):
            here, past = slice(j * rows, (j + 1) * rows), slice(0, j * rows)
            bias_here = bias[here, :]
            for h in range(LANES // head):
                mine = (lane >= h * head) & (lane < (h + 1) * head)
                query = jnp.where(mine, joint[here, q_at].astype(F32) * SCORE_SCALE, 0.0).astype(BF16)
                inner = dot(joint[here, k_at], query, NT)
                inner = jnp.where(same, inner, jnp.where(earlier, inner + bias_here, MASKED))
                top = jnp.max(inner, axis=0, keepdims=True)
                if j:
                    outer = dot(joint[past, k_at], query, NT) + bias[past, :]
                    top = jnp.maximum(top, jnp.max(outer, axis=0, keepdims=True))
                inner = jnp.exp(inner - top)
                total = jnp.sum(inner, axis=0, keepdims=True)
                if j:
                    outer = jnp.exp(outer - top)
                    total = total + jnp.sum(outer, axis=0, keepdims=True)
                share = 1.0 / total
                value_h = value_t[h * head : (h + 1) * head]
                out = dot(value_h[:, here], (inner * share).astype(BF16))
                if j:
                    out = out + dot(value_h[:, past], (outer * share).astype(BF16))
                at = p * LANES + h * head
                wide[at : at + head, here] = out
                lse[p, h : h + 1, here] = top + jnp.log(total)
    for i in range(g):
        here = slice(i * rows, (i + 1) * rows)
        for out_ref, first in ((near_att, group * g + i), (far_att, (1 - group) * g + i)):
            part = wide[:, pl.ds(pl.multiple_of(first * rows, rows), rows)]
            out_ref[here, :] = part.T.astype(BF16)


def attend(lay, spot, bias, vecs, hidden, weights):
    d, hw, length, g = lay.width, lay.share, lay.length, lay.size
    outs = [
        shaped((g * lay.rows, hw), BF16),
        shaped((g * lay.rows, hw), BF16),
        shaped((length, 3 * hw), BF16),
        shaped((hw, length), F32),
        shaped((hw // LANES, 8, length), F32),
        shaped((length, d), BF16),
        shaped((length, d), BF16),
        shaped((d, 3 * hw), BF16),
    ]
    copies = 2 * lay.planes * 2 * g
    args = (spot, bias, vecs) + tuple(hidden) + tuple(weights)
    return kernel_call(
        lay.order,
        functools.partial(attend_kernel, lay),
        outs,
        *args,
        name="attend",
        smem=(0,),
        away=tuple(range(3, len(args))),
        scratch=[
            pltpu.SemaphoreType.DMA((2 * g,)),
            pltpu.SemaphoreType.DMA((copies,)),
        ],
        vmem=24,
    )


def fold_kernel(slot, shift, a, b, spot, keep, came, hold, give):
    total = keep[...].astype(F32) + came[...].astype(F32)
    side = (spot[slot] >> shift) & 1
    view = total.reshape(a, 2, b, total.shape[-1])

    def write(s):
        hold[...] = view[:, s].reshape(a * b, -1).astype(BF16)
        give[...] = view[:, 1 - s].reshape(a * b, -1).astype(BF16)

    each_way(side, write)


def fold(lay, spot, slot, shift, a, keep, came):
    count, columns = keep.shape
    b = count // (2 * a)
    return kernel_call(
        lay.order,
        functools.partial(fold_kernel, slot, shift, a, b),
        [shaped((a * b, columns), BF16)] * 2,
        spot,
        keep,
        came,
        name="fold",
        smem=(0,),
    )


def mask_kernel(spot, lengths, cotangent, out):
    rows = out.shape[0]
    live = spot[0] * rows + iota((rows, 1), 0) < lengths[0]
    out[...] = jnp.where(live, cotangent[...].astype(F32), 0.0).astype(BF16)


def place_rows(lay, spot, e):
    return spot[4] ^ e


def block_of(lay, blocks, k):
    mine, came = blocks[2 * (k & 1)], blocks[2 * (k & 1) + 1]
    half = lay.planes // 2
    return (mine if k >> 1 < half else came).at[(k >> 1) % half]


def up_loads(lay, spot, blocks, w_up):
    pairs = []
    span, g = 2 * lay.each, lay.size
    for k in range(2 * lay.planes):
        source = block_of(lay, blocks, k)
        top, plane = block_spot(lay, spot, k, False)
        for q in range(g):
            start = ((top * g + q) * lay.planes + plane) * span
            pairs.append(
                (
                    source.at[q * span : (q + 1) * span, :],
                    w_up.at[pl.ds(pl.multiple_of(start, span), span), :],
                )
            )
    return pairs


def down_loads(lay, spot, blocks, w_down):
    pairs = []
    for k in range(2 * lay.planes):
        top, plane = block_spot(lay, spot, k, True)
        start = (top * lay.planes + plane) * lay.piece
        target = w_down.at[pl.ds(pl.multiple_of(start, lay.piece), lay.piece), :]
        pairs.append((block_of(lay, blocks, k), target))
    return pairs


def row_loads(lay, spot, mine, swapped, target):
    pairs = []
    g, rows = lay.size, lay.rows
    for e in range(g):
        for source, sequence in ((mine[e], spot[2]), (swapped[e], 1 - spot[2])):
            start = (sequence * g + (spot[4] ^ e)) * rows
            pairs.append((source, target.at[pl.ds(pl.multiple_of(start, rows), rows), :]))
    return pairs


def out_loads(lay, spot, blocks, target):
    pairs = []
    half, span, g = lay.width // 2, 2 * lay.each, lay.size
    for i, block in enumerate(blocks):
        column = pl.multiple_of((spot[2] ^ (i // 2)) * half, half)
        for k in range(lay.planes):
            top, plane = block_spot(lay, spot, 2 * k + i % 2, False)
            for q in range(g):
                row = pl.multiple_of(((top * g + q) * lay.planes + plane) * span, span)
                source = block.at[k, q * span : (q + 1) * span, :]
                pairs.append((source, target.at[pl.ds(row, span), pl.ds(column, half)]))
    return pairs


def forward_kernel(lay, spot, vecs, *refs):
    outs, refs = refs[:4], refs[4:]
    g, rows, hw, d = lay.size, lay.rows, lay.share, lay.width
    lists = [refs[i * g : (i + 1) * g] for i in range(7)]
    near, far, near_c, far_c, base_m, down_m, down_c = lists
    refs = refs[7 * g :]
    bundle, ups, downs = refs[0], refs[1:5], refs[5:9]
    (
        dn_keep,
        dn_give,
        middle_own,
        att_own,
        normed,
        act,
        grad_pre,
        bias_sum,
        wo,
        att,
        base,
        gd,
        w_up,
        w_down,
        sems,
    ) = refs[9:]
    core, group, place = spot[2], spot[3], spot[4]
    span = g * rows
    pairs = out_loads(lay, spot, outs, wo)
    for e in range(g):
        for source, sequence, at, side in (
            (near[e], group, place ^ e, core),
            (near_c[e], group, place ^ e, 1 - core),
            (far[e], 1 - group, (g - 1 - place) ^ e, core),
            (far_c[e], 1 - group, (g - 1 - place) ^ e, 1 - core),
        ):
            row = pl.multiple_of(sequence * span, span)
            column = pl.multiple_of((at * 2 + side) * hw, hw)
            pairs.append((source, att.at[pl.ds(row, span), pl.ds(column, hw)]))
    first_row = jnp.where(spot[6] == 1, span, 0)
    base_c = [
        bundle.at[pl.ds(pl.multiple_of(first_row + e * rows, rows), rows), :] for e in range(g)
    ]
    pairs += row_loads(lay, spot, base_m, base_c, base)
    first = len(pairs)
    pairs += up_loads(lay, spot, ups, w_up) + down_loads(lay, spot, downs, w_down)
    pairs += row_loads(lay, spot, down_m, down_c, gd)
    copies = [pltpu.make_async_copy(a, b, sems.at[i]) for i, (a, b) in enumerate(pairs)]
    for copy in copies[:first]:
        copy.start()
    wait_all(copies[:first])
    for copy in copies[first:]:
        copy.start()
    bias_out, gain, shift = vecs[4:5, :], vecs[5:6, :], vecs[6:7, :]
    bias_up = vecs[8:9, 0 : lay.ff_share]
    total = jnp.zeros((1, lay.ff_share), F32)
    for i in range(2 * g):
        here = slice(i * rows, (i + 1) * rows)
        middle = base[here, :].astype(F32) + (dot(att[here, :], wo[...]) + bias_out)
        normal, _ = centre(middle)
        normed[here, :] = (normal * gain + shift).astype(BF16)

        @pl.when((core == i // g) & (place == i % g))
        def _():
            middle_own[...] = middle
            att_own[...] = att[here, :]

    wait_all(copies[first:])
    for i in range(2 * g):
        here = slice(i * rows, (i + 1) * rows)
        pre = dot(normed[here, :], w_up[...]) + bias_up
        value, slope = gelu_terms(pre)
        act[here, :] = value.astype(BF16)
        grad = (dot(gd[here, :], w_down[...], NT) * slope).astype(BF16)
        grad_pre[here, :] = grad
        total = total + jnp.sum(grad.astype(F32), axis=0, keepdims=True)
        back = dot(grad, w_up[...], NT).astype(BF16)
        at = slice((i % g) * rows, (i % g + 1) * rows)

        @pl.when(core == i // g)
        def _():
            dn_keep[at, :] = back

        @pl.when(core != i // g)
        def _():
            dn_give[at, :] = back

    bias_sum[...] = total


def forward_call(lay, spot, vecs, outs_w, lists, blocks):
    d, f, rows, g = lay.width, lay.ff_share, lay.rows, lay.size
    tokens = 2 * g * rows
    outs = [
        shaped((g * rows, d), BF16),
        shaped((g * rows, d), BF16),
        shaped((rows, d), F32),
        shaped((rows, d), BF16),
        shaped((tokens, d), BF16),
        shaped((tokens, f), BF16),
        shaped((tokens, f), BF16),
        shaped((1, f), F32),
        shaped((d, d), BF16),
    ]
    args = (spot, vecs) + tuple(outs_w) + tuple(lists) + tuple(blocks)
    copies = 4 * lay.planes * g + 8 * g + 2 * lay.planes * (g + 1)
    return kernel_call(
        lay.order,
        functools.partial(forward_kernel, lay),
        outs,
        *args,
        name="feed_forward",
        smem=(0,),
        away=tuple(range(2, len(args))),
        scratch=[
            pltpu.VMEM((tokens, d), BF16),
            pltpu.VMEM((tokens, d), BF16),
            pltpu.VMEM((tokens, d), BF16),
            pltpu.VMEM((d, f), BF16),
            pltpu.VMEM((f, d), BF16),
            pltpu.SemaphoreType.DMA((copies,)),
        ],
        vmem=24,
    )


def cut_rows(value, side, a, b, keep, give):
    for i in range(a):
        for ref, s in ((keep, side), (give, 1 - side)):
            start = pl.multiple_of((2 * i + s) * b, b)
            ref[i * b : (i + 1) * b, :] = value[pl.ds(start, b), :]


def gradient_kernel(lay, spot, normed, act, grad_pre, *refs):
    g, rows, d, f = lay.size, lay.rows, lay.width, lay.ff_share
    down_m, down_c, blocks = refs[:g], refs[g : 2 * g], refs[2 * g : 2 * g + 4]
    up_keep, up_give, down_keep, down_give, out_keep, out_give, gd, w_down, full, sems = refs[
        2 * g + 4 :
    ]
    pairs = row_loads(lay, spot, down_m, down_c, gd)
    pairs += down_loads(lay, spot, blocks, w_down)
    copies = load_all(pairs, sems)
    tile = 256
    for i in range(d // tile):
        here = slice(i * tile, (i + 1) * tile)
        full[here, 0:f] = dot(normed[:, here], grad_pre[...], TN).astype(BF16)
    plane_bits = bits_of(lay.planes)
    side = (spot[1] >> plane_bits) & 1
    cut_rows(full.at[0:d, 0:f], side, 2 * g, d // (4 * g), up_keep, up_give)
    wait_all(copies)
    tile = min(256, f)
    for i in range(f // tile):
        here = slice(i * tile, (i + 1) * tile)
        full[here, 0:d] = dot(act[:, here], gd[...], TN).astype(BF16)
    side = (spot[1] >> 1) & 1
    cut_rows(full.at[0:f, 0:d], side, lay.planes, lay.piece, down_keep, down_give)
    for i in range(2 * g):
        here = slice(i * rows, (i + 1) * rows)
        at = slice((i % g) * rows, (i % g + 1) * rows)
        part = dot(act[here, :], w_down[...]).astype(BF16)

        @pl.when(spot[2] == i // g)
        def _():
            out_keep[at, :] = part

        @pl.when(spot[2] != i // g)
        def _():
            out_give[at, :] = part


def gradient_call(lay, spot, normed, act, grad_pre, down_m, down_c, blocks):
    d, f, rows, g = lay.width, lay.ff_share, lay.rows, lay.size
    tokens = 2 * g * rows
    outs = [shaped((d // 2, f), BF16)] * 2 + [shaped((f // 2, d), BF16)] * 2
    outs += [shaped((g * rows, d), BF16)] * 2
    args = (spot, normed, act, grad_pre) + tuple(down_m) + tuple(down_c) + tuple(blocks)
    return kernel_call(
        lay.order,
        functools.partial(gradient_kernel, lay),
        outs,
        *args,
        name="gradients",
        smem=(0,),
        away=tuple(range(4, len(args))),
        scratch=[
            pltpu.VMEM((tokens, d), BF16),
            pltpu.VMEM((f, d), BF16),
            pltpu.VMEM((d, d), BF16),
            pltpu.SemaphoreType.DMA((2 * g + 2 * lay.planes,)),
        ],
        vmem=24,
    )


def turn_kernel(lay, spot, vecs, keep, came, middle, grad_low, w_out, *refs):
    keep_out, give_out, grad_middle, grad_branch, sums, wo, att_grad, sems = refs
    copies = load_all([(w_out, wo)], sems)
    normal, scale = centre(middle[...])
    slope = keep[...].astype(F32) + came[...].astype(F32)
    total = grad_low[...].astype(F32) + norm_back(slope, normal, scale, vecs[5:6, :])
    grad_middle[...] = total
    branch = total.astype(BF16)
    grad_branch[...] = branch
    sums[...] = jnp.zeros_like(sums)
    add = lambda value: jnp.sum(value, axis=0, keepdims=True)
    sums[0:1, :] = add(branch.astype(F32))
    sums[1:2, :] = add(slope * normal)
    sums[2:3, :] = add(slope)
    sums[3:4, :] = add(grad_low[...].astype(F32))
    wait_all(copies)
    att_grad[...] = dot(branch, wo[...], NT).astype(BF16)
    hw = lay.share
    for i in range(lay.size):
        for ref, side in ((keep_out, spot[2]), (give_out, 1 - spot[2])):
            start = pl.multiple_of((2 * i + side) * hw, hw)
            ref[:, i * hw : (i + 1) * hw] = att_grad[:, pl.ds(start, hw)]


def outer_kernel(spot, att, branch, keep, give):
    tile, half = 256, keep.shape[1]

    def write(side):
        for i in range(keep.shape[0] // tile):
            here = slice(i * tile, (i + 1) * tile)
            value = dot(att[:, here], branch[...], TN).astype(BF16)
            keep[here, :] = value[:, side * half : (side + 1) * half]
            give[here, :] = value[:, (1 - side) * half : (2 - side) * half]

    each_way(spot[2], write)


def pick_kernel(lay, spot, mine, came, *pieces):
    hw = lay.share
    for r in range(lay.members):
        chip = spot[0] ^ r
        column = pl.ds(pl.multiple_of(chip % lay.size * hw, hw), hw)
        own = chip // lay.size == spot[2]

        @pl.when(own)
        def _(r=r, column=column):
            pieces[r][...] = mine[:, column]

        @pl.when(jnp.logical_not(own))
        def _(r=r, column=column):
            pieces[r][...] = came[:, column]


def turn_call(lay, spot, vecs, keep, came, middle, grad_low, w_out):
    d, rows = lay.width, lay.rows
    outs = [shaped((rows, d // 2), BF16)] * 2
    outs += [shaped((rows, d), F32), shaped((rows, d), BF16), shaped((8, d), F32)]
    return kernel_call(
        lay.order,
        functools.partial(turn_kernel, lay),
        outs,
        spot,
        vecs,
        keep,
        came,
        middle,
        grad_low,
        w_out,
        name="turn",
        smem=(0,),
        away=(6,),
        scratch=[
            pltpu.VMEM((d, d), BF16),
            pltpu.VMEM((rows, d), BF16),
            pltpu.SemaphoreType.DMA((1,)),
        ],
        vmem=24,
    )


def assemble_kernel(lay, spot, *refs):
    out = refs[-1]
    for r in range(lay.members):
        start = pl.multiple_of((spot[0] ^ r) * lay.rows, lay.rows)
        out[pl.ds(start, lay.rows), :] = refs[r][...]


def attend_back_kernel(lay, spot, bias, joint, wide, lse, normed, slope_all, *refs):
    rows, hw, length, head, d = lay.rows, lay.share, lay.length, lay.head, lay.width
    (
        grads_out,
        left_keep,
        left_give,
        right_keep,
        right_give,
        sums,
        key_sum,
        value_sum,
        query_t,
        full,
    ) = refs
    earlier, same = key_mask_terms(rows)
    lane = iota((rows, LANES), 1)
    for p in range(hw // LANES):
        q_at, k_at, v_at = (slice(i * hw + p * LANES, i * hw + (p + 1) * LANES) for i in range(3))
        s_at = slice(p * LANES, (p + 1) * LANES)
        key_t = joint[:, k_at].astype(F32).T.astype(BF16)
        product = slope_all[:, s_at].astype(F32).T * wide[s_at, :]
        key_sum[...] = jnp.zeros_like(key_sum)
        value_sum[...] = jnp.zeros_like(value_sum)
        for j in range(length // rows):
            here = slice(j * rows, (j + 1) * rows)
            for h in range(LANES // head):
                mine = (lane >= h * head) & (lane < (h + 1) * head)
                query = jnp.where(mine, joint[here, q_at].astype(F32) * SCORE_SCALE, 0.0).astype(BF16)
                slope = jnp.where(mine, slope_all[here, s_at].astype(F32), 0.0).astype(BF16)
                top = lse[p, h : h + 1, here]
                delta = jnp.sum(product[h * head : (h + 1) * head, here], axis=0, keepdims=True)
                key_h = key_t[h * head : (h + 1) * head]
                back = None
                for part in (slice(0, j * rows), here) if j else (here,):
                    scores = dot(joint[part, k_at], query, NT)
                    if part is here:
                        scores = jnp.where(
                            same, scores, jnp.where(earlier, scores + bias[part, :], MASKED)
                        )
                    else:
                        scores = scores + bias[part, :]
                    chances = jnp.exp(scores - top)
                    slopes = dot(joint[part, v_at], slope, NT)
                    grads = (chances * (slopes - delta)).astype(BF16)
                    value_sum[part, :] += dot(chances.astype(BF16), slope)
                    key_sum[part, :] += dot(grads, query)
                    term = dot(key_h[:, part], grads)
                    back = term if back is None else back + term
                query_t[h * head : (h + 1) * head, here] = back * SCORE_SCALE
        grads_out[:, q_at] = query_t[...].T.astype(BF16)
        grads_out[:, k_at] = key_sum[...].astype(BF16)
        grads_out[:, v_at] = value_sum[...].astype(BF16)
    sums[...] = jnp.sum(grads_out[...].astype(F32), axis=0, keepdims=True)
    tile = 256
    for i in range(d // tile):
        here = slice(i * tile, (i + 1) * tile)
        full[here, :] = dot(normed[:, here], grads_out[...], TN).astype(BF16)
    cut = left_keep.shape[1]
    g = lay.size
    side = (spot[1] >> bits_of(lay.planes)) & 1
    cut_rows(full.at[:, 0:cut], side, 2 * g, d // (4 * g), left_keep, left_give)
    side = (spot[1] >> 1) & 1
    cut_rows(full.at[:, cut:], side, g * lay.planes, 2 * lay.each, right_keep, right_give)


def attend_back(lay, spot, bias, joint, wide, lse, normed, slope, cut):
    d, hw, length = lay.width, lay.share, lay.length
    outs = [shaped((length, 3 * hw), BF16)]
    outs += [shaped((d // 2, cut), BF16)] * 2 + [shaped((d // 2, 3 * hw - cut), BF16)] * 2
    outs += [shaped((1, 3 * hw), F32)]
    return kernel_call(
        lay.order,
        functools.partial(attend_back_kernel, lay),
        outs,
        spot,
        bias,
        joint,
        wide,
        lse,
        normed,
        slope,
        name="attend_back",
        smem=(0,),
        scratch=[
            pltpu.VMEM((length, LANES), F32),
            pltpu.VMEM((length, LANES), F32),
            pltpu.VMEM((LANES, length), F32),
            pltpu.VMEM((d, 3 * hw), BF16),
        ],
        vmem=24,
    )


def input_kernel(
    lay, spot, grads, w, x, sums_two, joint_sum, bias_up_sum, keep, give, sums, sums_low
):
    rows, g, hw = lay.rows, lay.size, lay.share
    gain = jnp.zeros((1, lay.width), F32)
    shift = jnp.zeros((1, lay.width), F32)
    for i in range(2 * g):
        here = slice(i * rows, (i + 1) * rows)
        part = dot(grads[here, :], w[...], NT)
        normal, _ = centre(x[here, :].astype(F32))
        gain = gain + jnp.sum(part * normal, axis=0, keepdims=True)
        shift = shift + jnp.sum(part, axis=0, keepdims=True)
        low = part.astype(BF16)
        at = slice((i % g) * rows, (i % g + 1) * rows)

        @pl.when(spot[8] == i // g)
        def _():
            keep[at, :] = low

        @pl.when(spot[8] != i // g)
        def _():
            give[at, :] = low

    sums[...] = jnp.zeros_like(sums)
    sums[0:1, :] = gain
    sums[1:2, :] = shift
    mine = pl.ds(pl.multiple_of(spot[5] * hw, hw), hw)
    sums[2:3, mine] = joint_sum[:, 0:hw]
    sums[3:4, mine] = joint_sum[:, 2 * hw :]
    sums[4:8, :] = sums_two[0:4, :]
    piece = lay.piece

    def write(m):
        for b in range(2 * lay.planes):
            at = up_column(lay, b, m)
            line, column = 8 + at // lay.width, at % lay.width
            sums[line : line + 1, column : column + piece] = bias_up_sum[:, b * piece : (b + 1) * piece]

    for m in range(lay.members):
        pl.when(spot[5] == m)(functools.partial(write, m))
    sums_low[...] = sums[...].astype(BF16)


SUM_ROWS = 16


def up_column(lay, b, member):
    top, plane = b // lay.planes, b % lay.planes
    chip = top * lay.size + member // 2
    return ((chip * lay.planes + plane) * 2 + member % 2) * lay.piece


def sum_rows(width, columns):
    return -(-width // columns) * SUM_ROWS


def put_sums(ref, base, total):
    width, columns = total.shape[1], ref.shape[1]
    for k in range(-(-width // columns)):
        part = total[:, k * columns : min(width, (k + 1) * columns)]
        at = slice(base + k * SUM_ROWS, base + (k + 1) * SUM_ROWS)
        if part.shape[1] < columns:
            ref[at, :] = jnp.zeros((SUM_ROWS, columns), BF16)
        ref[at, 0 : part.shape[1]] = part.astype(BF16)


def take_sums(ref, base, width):
    columns = ref.shape[1]
    parts = []
    for k in range(-(-width // columns)):
        at = slice(base + k * SUM_ROWS, base + (k + 1) * SUM_ROWS)
        parts.append(ref[at, 0 : min(columns, width - k * columns)].astype(F32))
    return parts[0] if len(parts) == 1 else jnp.concatenate(parts, axis=1)


def input_call(lay, spot, grads, w, x, sums_two, joint_sum, bias_up_sum):
    d, rows, g = lay.width, lay.rows, lay.size
    small = (SUM_ROWS, d)
    return kernel_call(
        lay.order,
        functools.partial(input_kernel, lay),
        [shaped((g * rows, d), BF16)] * 2 + [shaped(small, F32), shaped(small, BF16)],
        spot,
        grads,
        w,
        x,
        sums_two,
        joint_sum,
        bias_up_sum,
        name="input_slope",
        smem=(0,),
        vmem=24,
    )


def fold_into(spot, cut, keep, came, hold, give, rows=None):
    slot, shift, a = cut
    count = keep.shape[0]
    b = count // (2 * a)
    side = (spot[slot] >> shift) & 1
    half = a * b

    def write(s):
        for i in range(a):
            for ref, t in ((hold, s), (give, 1 - s)):
                at = slice((2 * i + t) * b, (2 * i + t + 1) * b)
                value = keep[at, :].astype(F32) + came[at, :].astype(F32)
                ref[i * b : (i + 1) * b, :] = value.astype(BF16)

    each_way(side, write)


def two_fold_kernel(cuts, spot, one, one_came, two, two_came, one_keep, one_give, two_keep, two_give):
    fold_into(spot, cuts[0], one, one_came, one_keep, one_give)
    fold_into(spot, cuts[1], two, two_came, two_keep, two_give)


def two_fold(lay, spot, cuts, one, one_came, two, two_came):
    outs = []
    for v in (one, two):
        outs += [shaped((v.shape[0] // 2, v.shape[1]), BF16)] * 2
    return kernel_call(
        lay.order,
        functools.partial(two_fold_kernel, cuts),
        outs,
        spot,
        one,
        one_came,
        two,
        two_came,
        name="two_fold",
        smem=(0,),
    )


def sums_fold_kernel(
    cuts, spot, one, one_came, two, two_came, sums, sums_came, one_keep, one_give, two_keep, two_give, sums_out
):
    n, half, width = one.shape[0], one_keep.shape[0], sums.shape[1]
    if one_came.shape[0] > n:
        came = take_sums(one_came, n, width)
    else:
        came = sums_came[...].astype(F32)
    total = sums[...] + came
    sums_out[...] = total
    fold_into(spot, cuts[0], one, one_came, one_keep, one_give)
    put_sums(one_give, half, total)
    fold_into(spot, cuts[1], two, two_came, two_keep, two_give)


def sums_fold(lay, spot, cuts, one, one_came, two, two_came, sums, sums_came):
    half, other = one.shape[0] // 2, two.shape[0] // 2
    outs = [
        shaped((half, one.shape[1]), BF16),
        shaped((half + sum_rows(sums.shape[1], one.shape[1]), one.shape[1]), BF16),
        shaped((other, two.shape[1]), BF16),
        shaped((other, two.shape[1]), BF16),
        shaped(sums.shape, F32),
    ]
    args = (spot, one, one_came, two, two_came, sums, sums_came)
    return kernel_call(
        lay.order, functools.partial(sums_fold_kernel, cuts), outs, *args, name="sums_fold", smem=(0,)
    )


def top_fold_kernel(shift, spot, one, one_came, two, two_came, sums, keep, give, sums_out):
    n, cut = one.shape
    half = n // 2
    total = sums[...] + take_sums(one_came, n, sums.shape[1])
    sums_out[...] = total
    put_sums(give, half, total)

    def write(s):
        for here, x, y in ((slice(0, cut), one, one_came), (slice(cut, None), two, two_came)):
            for ref, t in ((keep, s), (give, 1 - s)):
                at = slice(t * half, (t + 1) * half)
                value = x[at, :].astype(F32) + y[at, :].astype(F32)
                ref[0:half, here] = value.astype(BF16)

    each_way((spot[0] >> shift) & 1, write)


def top_pair_kernel(shift, spot, one, one_came, two, two_came, one_keep, two_keep, give):
    half = one_keep.shape[0]

    def write(s):
        for i, (x, y, keep) in enumerate(((one, one_came, one_keep), (two, two_came, two_keep))):
            for ref, t in ((keep, s), (give.at[i], 1 - s)):
                at = slice(t * half, (t + 1) * half)
                ref[...] = (x[at, :].astype(F32) + y[at, :].astype(F32)).astype(BF16)

    each_way((spot[0] >> shift) & 1, write)


def home_first_kernel(slot, shift, spot, w_in, w_in_came, w_up, w_up_came, sums, keep, give, sums_out):
    n, cut = w_in.shape
    half = n // 2
    w_up_came = w_up_came.at[0] if len(w_up_came.shape) > len(w_up.shape) else w_up_came
    total = sums[...] + take_sums(w_in_came, n, sums.shape[1])
    sums_out[...] = total
    put_sums(give, half, total)

    def write(s):
        for here, x, y in ((slice(0, cut), w_in, w_in_came), (slice(cut, None), w_up, w_up_came)):
            for ref, t in ((keep, s), (give, 1 - s)):
                at = slice(t * half, (t + 1) * half)
                value = x[at, :].astype(F32) + y[at, :].astype(F32)
                ref[0:half, here] = value.astype(BF16)

    each_way((spot[slot] >> shift) & 1, write)


def home_next_kernel(slot, shift, spot, mine, came, sums, *refs):
    keep, give, sums_out = refs[-3:]
    n, columns = mine.shape
    half = n // 2
    total = sums[...] + take_sums(came, max(n, 16), sums.shape[1])
    sums_out[...] = total
    put_sums(give, max(half, 16), total)

    def write(s):
        for here, x in ((slice(0, columns), mine), (slice(columns, 2 * columns), came)):
            for ref, t in ((keep, s), (give, 1 - s)):
                put_rows(ref, here, x, t * half, half)
        if len(refs) > 3:
            total = (refs[0][...].astype(F32) + refs[1][...].astype(F32)).astype(BF16)
            for ref, t in ((keep, s), (give, 1 - s)):
                put_rows(ref, slice(2 * columns, None), total, t * half, half)

    each_way((spot[slot] >> shift) & 1, write)


def put_rows(ref, columns, source, start, count):
    if count >= 16:
        ref[0:count, columns] = source[start : start + count, :]
        return
    value = source[0:16, :].astype(F32)[start : start + count]
    value = jnp.concatenate([value, jnp.zeros((16 - count, value.shape[1]), F32)], axis=0)
    ref[0:16, columns] = value.astype(BF16)


def home_last_kernel(lay, spot, mine, came, sums, w_in, w_up, w_out, *vectors):
    n = lay.each
    hw, piece, cut = lay.share, lay.piece, 3 * lay.share
    span = cut + lay.ff_share
    for f, ref in enumerate((mine, came)):
        for e in range(lay.size):
            place = 0
            for k in range(bits_of(lay.size)):
                place |= ((e >> k) & 1) << (bits_of(lay.size) - 1 - k)
            member = (spot[4] ^ place) * 2 + (spot[2] ^ f)

            def write(m, ref=ref, e=e):
                for i in range(3):
                    at = i * lay.width + m * hw
                    start = e * span + i * hw
                    w_in[:, at : at + hw] = ref[0 : max(n, 16), start : start + hw].astype(F32)[0:n]
                for b in range(2 * lay.planes):
                    at = up_column(lay, b, m)
                    start = e * span + cut + b * piece
                    value = ref[0 : max(n, 16), start : start + piece].astype(F32)
                    w_up[:, at : at + piece] = value[0:n]

            for m in range(lay.members):
                pl.when(member == m)(functools.partial(write, m))
    half = lay.width // 2

    def write_out(side):
        for ref, s in ((mine, side), (came, 1 - side)):
            at = ref.shape[1] - half
            w_out[:, s * half : (s + 1) * half] = ref[0 : max(n, 16), at:].astype(F32)[0:n]

    each_way(spot[2], write_out)
    total = sums[...] + take_sums(came, max(n, 16), lay.width)

    def part_of(start, count):
        source, target = iota((lay.width, count), 0), iota((lay.width, count), 1)
        move = (source == start + target).astype(F32)
        return jnp.dot(total, move, precision=lax.Precision.HIGHEST)

    own = part_of(spot[7] * n, n)
    for v in range(8):
        vectors[v][...] = own[v : v + 1, :]
    first = spot[7] * piece
    own = part_of(first % lay.width, piece)
    line = iota(own.shape, 0) == 8 + first // lay.width
    vectors[8][...] = jnp.sum(jnp.where(line, own, 0.0), axis=0, keepdims=True)


def add_kernel(one, two, out):
    other = two[1] if len(two.shape) > len(one.shape) else two[...]
    out[...] = (one[...].astype(F32) + other.astype(F32)).astype(out.dtype)


def last_kernel(spot, vecs, keep, came, sent, own, grad_middle, out):
    total = keep[...].astype(F32) + came[...].astype(F32)
    slope = jnp.where(spot[6] == 1, total, sent[...].astype(F32))
    normal, scale = centre(own[...].astype(F32))
    out[...] = (grad_middle[...] + norm_back(slope, normal, scale, vecs[0:1, :])).astype(BF16)


def out_kernel(vecs, middle, keep, came, out):
    total = keep[...].astype(F32) + came[...].astype(F32)
    out[...] = (middle[...] + (total + vecs[7:8, :])).astype(BF16)


def solution(mesh):
    nb, nt = mesh.shape["blk"], mesh.shape["batch"]
    devices = nb * nt
    group_size = nb // 2
    total_bits = bits_of(devices)
    plane_bits = list(range(1, bits_of(nt)))
    group_bits = list(range(bits_of(nt), bits_of(nt) + bits_of(group_size)))
    top_bit = total_bits - 1
    members = 2 * group_size

    def at_home(i):
        return (i // nt) // group_size == i % 2

    def send(value, route):
        return lax.ppermute(value, AXES, route)

    def flip(value, bit, who=None):
        return send(value, [(i, i ^ (1 << bit)) for i in range(devices) if who is None or who(i)])

    def mirror(i):
        return (nb - 1 - i // nt) * nt + i % nt

    def local(
        hidden_in,
        key_mask,
        lengths,
        first_gain,
        first_shift,
        input_weight,
        query_bias,
        value_bias,
        output_weight,
        output_bias,
        second_gain,
        second_shift,
        up_weight,
        up_bias,
        down_weight,
        down_bias,
        cotangent,
    ):
        rows, width = hidden_in.shape[1:]
        length = key_mask.shape[1]
        head = width // HEADS
        blk, lane_id = lax.axis_index("blk"), lax.axis_index("batch")
        index = blk * nt + lane_id
        core = lane_id % 2
        group, place = blk // group_size, blk % group_size
        member = place * 2 + core
        home = group == core
        share = width // members
        ff = up_weight.shape[1]
        piece = ff // devices

        def bit(b):
            return (index >> b) & 1

        def ordered(mine, theirs, side, axis):
            return jnp.where(
                side == 0,
                jnp.concatenate([mine, theirs], axis),
                jnp.concatenate([theirs, mine], axis),
            )

        def side_of(value, side, axis):
            lo, hi = jnp.split(value, 2, axis)
            return jnp.where(side == 0, lo, hi)

        lay = Layout(nb, nt, rows, width, ff, length)
        each = lay.each
        own = hidden_in[0]
        kept_group = jnp.where(home, group, 1 - group)
        kept_place = jnp.where(home, place, group_size - 1 - place)
        spot = jnp.stack(
            [blk, lane_id, core, group, place, member, home.astype(jnp.int32), index]
            + [kept_group, kept_place]
        )
        away = lambda i: not at_home(i)
        across = [(i, mirror(i) ^ 1) for i in range(devices) if away(i)]
        mirrored = [(i, mirror(i)) for i in range(devices)]

        call = functools.partial(kernel_call, lay.order)
        wide_in = 3 * group_size * share + 2 * group_size * lay.planes * piece
        row = lambda value: value.reshape(1, -1)
        vectors = [
            row(v)
            for v in (
                first_gain,
                first_shift,
                query_bias,
                value_bias,
                output_bias,
                second_gain,
                second_shift,
                down_bias,
                up_bias,
            )
        ]

        def spread_group(values, who=None):
            for b in group_bits:
                values = values + [flip(v, b, who) for v in values]
            return values

        act = None
        after = None
        att_c = None
        att_own = None
        b = None
        base = None
        bundle = None
        c = None
        came_w = None
        columns = None
        count = None
        cut = None
        cuts_of = None
        d_bias_up = None
        d_down = None
        d_in = None
        d_out = None
        d_up = None
        dn_came = None
        dn_give = None
        dn_keep = None
        down_blocks = None
        down_c = None
        down_came = None
        down_cuts = None
        down_far = None
        down_far_came = None
        down_give = None
        down_keep = None
        down_m = None
        downs = None
        downs_came = None
        far = None
        far_att = None
        far_came = None
        far_later = None
        final = None
        give = None
        grad_branch = None
        grad_joint = None
        grad_later = None
        grad_low = None
        grad_middle = None
        grad_pre = None
        half = None
        home_outs = None
        home_steps = None
        in_block = None
        in_came = None
        in_give = None
        in_keep = None
        in_pieces = None
        in_sum = None
        input_gradient = None
        joint = None
        joint_sum = None
        k = None
        keep = None
        key_bias = None
        layer_out = None
        left = None
        left_came = None
        left_cuts = None
        left_give = None
        left_keep = None
        lse = None
        middle = None
        near = None
        near_att = None
        next_out = None
        next_planes = None
        normed_one = None
        normed_two = None
        o_came = None
        o_give = None
        o_keep = None
        out_bits = None
        out_blocks = None
        out_came = None
        out_cuts = None
        out_give = None
        out_keep = None
        out_shape = None
        out_steps = None
        outs = None
        outs_c = None
        outs_far = None
        outs_w = None
        pair = None
        pair_came = None
        paired = None
        parts = None
        pieces = None
        planes_down = None
        r = None
        ready = None
        reduce_group = None
        right = None
        right_came = None
        right_cuts = None
        right_give = None
        right_keep = None
        rows_came = None
        sent = None
        shape = None
        shift = None
        slope = None
        slope_give = None
        slope_keep = None
        slot = None
        small = None
        start = None
        step = None
        sums = None
        sums_came = None
        sums_give = None
        sums_two = None
        tall = None
        top_shift = None
        up_blocks = None
        up_came = None
        up_cuts = None
        up_far = None
        up_far_came = None
        up_give = None
        up_keep = None
        up_tall = None
        ups = None
        ups_came = None
        ups_first = None
        valid = None
        vecs = None
        w_came = None
        w_give = None
        w_in = None
        w_keep = None
        w_out = None
        wide = None
        x_all = None
        def do_pack():
            nonlocal base, came_w, downs, downs_came, far, give, half, keep, near, start
            start = [input_weight, up_weight, key_mask, output_weight] + vectors
            half = width // 2
            base = max(each, 16)
            give, keep = call(
                functools.partial(pack_kernel, lay),
                [shaped((base + EXTRA, wide_in + half), BF16)] * 2,
                spot,
                lengths,
                *start,
                name="pack",
                smem=(0, 1),
                away=tuple(range(2, 15)),
                vmem=60,
                scratch=[pltpu.VMEM(v.shape, v.dtype) for v in start] + [pltpu.SemaphoreType.DMA((13,))],
            )
            came_w = flip(give, 0)
            far = [send(own, across)]
            near = spread_group([own])
            downs = down_weight[None]
            downs_came = flip(downs, plane_bits[-1])

        def do_mask():
            nonlocal grad_low
            grad_low = call(
                mask_kernel,
                [shaped((rows, width), BF16)],
                spot,
                lengths,
                cotangent[0],
                name="mask",
                smem=(0, 1),
            )[0]

        def do_trade():
            nonlocal b, came_w, columns, count, give, keep, ready, step, tall, valid
            count = group_size
            for step, b in enumerate(group_bits):
                tall = (2 << step) * each
                columns = wide_in >> (step + 1)
                give, keep, ready = call(
                    functools.partial(trade_kernel, lay, step, count),
                    [shaped((tall + EXTRA, columns + half), BF16)] * 2 + [shaped((8, length), F32)],
                    spot,
                    keep,
                    came_w,
                    name="trade",
                    smem=(0,),
                    scratch=[pltpu.VMEM((tall, 2 * columns + half), BF16)],
                    after=(far[0], *near[1:], downs_came) if step == 0 else (),
                )
                valid = ready if step == 0 else valid
                came_w = flip(give, b)
                count //= 2

        def do_join_down():
            nonlocal b, downs, downs_came
            for b in reversed(plane_bits[:-1]):
                downs = join(lay, downs, downs_came)
                downs_came = flip(downs, b)

        def do_settle():
            nonlocal far, far_later, in_block, pair, paired, tall, up_tall, ups, ups_came, ups_first
            tall = members * each
            paired = ff // members == width
            up_tall = tall + tall * half // (ff // members)
            in_block, ups, far_later, pair = call(
                functools.partial(settle_kernel, lay, len(group_bits)),
                [
                    shaped((tall + EXTRA, 3 * share), BF16),
                    shaped((1, up_tall, ff // members), BF16),
                    shaped(own.shape, BF16),
                    shaped((up_tall + piece, width) if paired else (8, LANES), BF16),
                ],
                spot,
                keep,
                came_w,
                far[0],
                down_weight,
                name="settle",
                smem=(0,),
                scratch=[pltpu.VMEM((tall, 3 * share + ff // members + half), BF16)],
            )
            far = far + spread_group([far_later], away)[1:]
            ups_first = ups
            ups_came = flip(ups, plane_bits[0])

        def do_bundle():
            nonlocal bundle, cut, rows_came
            bundle = call(
                functools.partial(bundle_kernel, group_size),
                [shaped((2 * group_size * rows, width), BF16)],
                spot,
                *near,
                *far,
                name="bundle",
                smem=(0,),
                after=(downs_came,),
            )[0]
            rows_came = flip(bundle, 0)
            cut = max(LANES, 3 * share // 2 // LANES * LANES)

        def do_split():
            nonlocal down_far, down_m, grad_later, left, left_came, pair, pair_came, right, right_came, up_far
            left, right, pair, grad_later = call(
                functools.partial(split_kernel, cut),
                [
                    shaped((2, tall + EXTRA, cut), BF16),
                    shaped((2, tall + EXTRA, 3 * share - cut), BF16),
                    shaped(pair.shape, BF16),
                    shaped(grad_low.shape, BF16),
                ],
                in_block,
                flip(in_block, top_bit),
                pair,
                grad_low,
                name="split",
                after=(ups_came,),
            )
            left_came, right_came = flip(left, plane_bits[0]), flip(right, plane_bits[-1])
            if paired:
                pair_came = flip(pair, top_bit)
            else:
                up_far, down_far = flip(ups_first, top_bit), flip(down_weight, top_bit)[None]
            down_m = [grad_low] + spread_group([grad_later])[1:]

        def do_stack():
            nonlocal after, b, c, k, left, left_came, right, right_came
            for k, (b, c) in list(enumerate(zip(plane_bits, reversed(plane_bits), strict=True)))[1:]:
                after = (rows_came,) if k == 1 else ()
                left, right = stack(lay, left, left_came, right, right_came, *after)
                left_came, right_came = flip(left, b), flip(right, c)

        def do_vectors():
            nonlocal in_pieces, vecs
            in_pieces = (left, left_came, right, right_came)
            vecs = call(
                functools.partial(vector_kernel, lay),
                [shaped((16, width), F32)],
                spot,
                left,
                left_came,
                name="vectors",
                smem=(0,),
                away=(1, 2),
                scratch=[
                    pltpu.VMEM((2 * lay.planes * EXTRA, -(-lay.small // LANES) * LANES), BF16),
                    pltpu.SemaphoreType.DMA((2 * lay.planes,)),
                ],
            )[0]

        def do_join_up():
            nonlocal b, ups, ups_came
            for b in plane_bits[1:]:
                ups = join(lay, ups, ups_came)
                ups_came = flip(ups, b)

        def do_attend():
            nonlocal att_c, far_att, joint, key_bias, lse, near_att, normed_one, w_in, wide, x_all
            key_bias = jnp.where(valid[0] > 0.5, 0.0, MASKED).astype(F32).reshape(length, 1)
            near_att, far_att, joint, wide, lse, normed_one, x_all, w_in = attend(
                lay, spot, key_bias, vecs, near + far + [rows_came], in_pieces
            )
            far_att = [send(far_att, mirrored)]
            near_att = spread_group([near_att])
            att_c = [flip(near_att[0], 0)]

        def do_unpair():
            nonlocal down_far, down_far_came, up_far, up_far_came
            if paired:
                up_far, down_far = call(
                    unpair_kernel,
                    [shaped((1, up_tall, width), BF16), shaped((1, piece, width), BF16)],
                    pair_came,
                    name="unpair",
                    after=(ups_came, *down_m[1:]),
                )
            up_far_came, down_far_came = flip(up_far, plane_bits[0]), flip(down_far, plane_bits[-1])

        def do_rows_own():
            nonlocal out_shape, outs_c, outs_w
            out_shape = [shaped((lay.planes, tall, half), BF16)]
            outs_w = call(out_kernel_rows, out_shape, ups, ups_came, name="out_rows")
            outs_c = flip(outs_w[0], 0)

        def do_stack_far():
            nonlocal b, c, down_far, down_far_came, k, up_far, up_far_came
            for k, (b, c) in list(enumerate(zip(plane_bits, reversed(plane_bits), strict=True)))[1:]:
                up_far, down_far = stack(lay, up_far, up_far_came, down_far, down_far_came, att_c[0])
                up_far_came, down_far_came = flip(up_far, b), flip(down_far, c)

        def do_rows_far():
            nonlocal att_c, down_blocks, down_c, far_att, out_blocks, outs_far, up_blocks
            down_c = [flip(v, 0) for v in down_m]
            far_att = spread_group(far_att)
            att_c = att_c[:1] + [flip(v, 0) for v in near_att[1:] + far_att]
            outs_far = call(out_kernel_rows, out_shape, up_far, up_far_came, name="out_rows", after=(outs_c,))[0]
            out_blocks = (*outs_w, outs_far, outs_c, flip(outs_far, 0))
            up_blocks = (ups, ups_came, up_far, up_far_came)
            down_blocks = (downs, downs_came, down_far, down_far_came)

        def do_forward():
            nonlocal act, att_own, cuts_of, d_bias_up, dn_give, dn_keep, grad_pre, middle, normed_two, planes_down, reduce_group, top_shift, w_out
            (
                dn_keep,
                dn_give,
                middle,
                att_own,
                normed_two,
                act,
                grad_pre,
                d_bias_up,
                w_out,
            ) = forward_call(
                lay,
                spot,
                vecs,
                out_blocks,
                near_att + far_att + att_c + near + down_m + down_c + [rows_came],
                up_blocks + down_blocks,
            )

            def reduce_group(keep, came, slot):
                for k in reversed(range(len(group_bits))):
                    keep, give = fold(lay, spot, slot, k, 1, keep, came)
                    came = flip(give, group_bits[k])
                return keep, came

            planes_down = list(reversed(plane_bits))
            top_shift = bits_of(group_size)

            def cuts_of(lead, order):
                here, cuts = list(planes_down), []
                for b in order:
                    cuts.append((1, b, lead << here.index(b)))
                    here.remove(b)
                return cuts

        def do_fold_norm():
            nonlocal dn_came, dn_keep
            dn_keep, dn_came = reduce_group(dn_keep, flip(dn_give, 0), 4)

        def do_gradients():
            nonlocal down_came, down_give, down_keep, out_came, out_give, out_keep, up_came, up_give, up_keep
            up_keep, up_give, down_keep, down_give, out_keep, out_give = gradient_call(
                lay, spot, normed_two, act, grad_pre, down_m, down_c, down_blocks
            )
            up_came, down_came = flip(up_give, planes_down[0]), flip(down_give, plane_bits[0])
            out_came = flip(out_give, 0)

        def do_turn():
            nonlocal grad_branch, grad_middle, slope_give, slope_keep, sums_two
            slope_keep, slope_give, grad_middle, grad_branch, sums_two = turn_call(
                lay, spot, vecs, dn_keep, dn_came, middle, grad_low, w_out
            )

        def do_pick():
            nonlocal parts, pieces, r
            pieces = call(
                functools.partial(pick_kernel, lay),
                [shaped((rows, share), BF16)] * members,
                spot,
                slope_keep,
                flip(slope_give, 0),
                name="pick",
                smem=(0,),
            )
            parts = [pieces[0]]
            for r in range(1, members):
                parts.append(send(pieces[r], [(i, i ^ (r * nt)) for i in range(devices)]))

        def do_outer():
            nonlocal o_came, o_give, o_keep
            o_keep, o_give = call(
                outer_kernel,
                [shaped((width, width // 2), BF16)] * 2,
                spot,
                att_own,
                grad_branch,
                name="output_gradient",
                smem=(0,),
            )
            o_came = flip(o_give, 0)

        def do_out_fold():
            nonlocal out_came, out_keep
            out_keep, out_came = reduce_group(out_keep, out_came, 4)

        def do_o0():
            nonlocal next_out, o_came, o_keep, out_bits, out_cuts, out_steps
            out_cuts = [(4, k, 2) for k in reversed(range(len(group_bits)))]
            out_cuts += cuts_of(2, planes_down) + [(0, top_shift, 1)]
            out_bits = list(reversed(group_bits)) + planes_down + [top_bit]
            out_steps = iter(range(len(out_bits)))

            def next_out(keep, came, count=1):
                for _ in range(count):
                    k = next(out_steps)
                    keep, give = fold(lay, spot, *out_cuts[k], keep, came)
                    came = flip(give, out_bits[k])
                return keep, came

            o_keep, o_came = next_out(o_keep, o_came)

        def do_assemble():
            nonlocal slope
            slope = call(
                functools.partial(assemble_kernel, lay),
                [shaped((length, share), BF16)],
                spot,
                *parts,
                name="assemble",
                smem=(0,),
            )[0]

        def do_planes():
            nonlocal down_came, down_cuts, down_keep, k, next_planes, up_came, up_cuts, up_keep
            up_cuts, down_cuts = cuts_of(members, planes_down), cuts_of(2, plane_bits)

            def next_planes(k, up_keep, up_came, down_keep, down_came):
                up_keep, up_give, down_keep, down_give = two_fold(
                    lay, spot, (up_cuts[k], down_cuts[k]), up_keep, up_came, down_keep, down_came
                )
                return up_keep, flip(up_give, planes_down[k]), down_keep, flip(down_give, plane_bits[k])

            for k in range(1, len(plane_bits)):
                up_keep, up_came, down_keep, down_came = next_planes(
                    k, up_keep, up_came, down_keep, down_came
                )

        def do_attend_back():
            nonlocal grad_joint, joint_sum, left_came, left_give, left_keep, right_came, right_give, right_keep
            grad_joint, left_keep, left_give, right_keep, right_give, joint_sum = attend_back(
                lay, spot, key_bias, joint, wide, lse, normed_one, slope, cut
            )
            left_came, right_came = flip(left_give, planes_down[0]), flip(right_give, plane_bits[0])

        def do_top_pair():
            nonlocal down_give, down_keep, far_came, give, shape, up_give, up_keep
            if paired:
                shape = (up_keep.shape[0] // 2, up_keep.shape[1])
                up_keep, down_keep, give = call(
                    functools.partial(top_pair_kernel, top_shift),
                    [shaped(shape, BF16), shaped(shape, BF16), shaped((2,) + shape, BF16)],
                    spot,
                    up_keep,
                    up_came,
                    down_keep,
                    down_came,
                    name="top_pair",
                    smem=(0,),
                    after=(o_came,),
                )
                far_came = flip(give, top_bit)
            else:
                up_keep, up_give, down_keep, down_give = two_fold(
                    lay, spot, ((0, top_shift, 1),) * 2, up_keep, up_came, down_keep, down_came
                )
                far_came = (flip(up_give, top_bit), flip(down_give, top_bit))

        def do_input():
            nonlocal in_came, in_give, in_keep, sums, sums_came, sums_give
            in_keep, in_give, sums, sums_give = input_call(
                lay, spot, grad_joint, w_in, x_all, sums_two, joint_sum, d_bias_up
            )
            sums_came = flip(sums_give, planes_down[0])
            in_came = flip(in_give, 0)

        def do_lr():
            nonlocal k, left_came, left_cuts, left_give, left_keep, right_came, right_cuts, right_give, right_keep, sums
            left_cuts, right_cuts = cuts_of(members, planes_down), cuts_of(members, plane_bits)
            for k in range(1, len(plane_bits)):
                left_keep, left_give, right_keep, right_give, sums = sums_fold(
                    lay,
                    spot,
                    (left_cuts[k], right_cuts[k]),
                    left_keep,
                    left_came,
                    right_keep,
                    right_came,
                    sums,
                    sums_came,
                )
                left_came, right_came = flip(left_give, planes_down[k]), flip(right_give, plane_bits[k])

        def do_dn1():
            nonlocal in_came, in_keep
            in_keep, in_came = reduce_group(in_keep, in_came, 9)

        def do_o1():
            nonlocal o_came, o_keep
            o_keep, o_came = next_out(o_keep, o_came, len(group_bits))

        def do_layer():
            nonlocal layer_out
            layer_out = call(
                out_kernel,
                [shaped((rows, width), BF16)],
                vecs,
                middle,
                out_keep,
                out_came,
                name="layer_out",
            )[0]

        def do_top():
            nonlocal small, sums, tall, w_came, w_give, w_keep
            small = (SUM_ROWS, width)
            tall = left_keep.shape[0] // 2
            w_keep, w_give, sums = call(
                functools.partial(top_fold_kernel, top_shift),
                [
                    shaped((tall, 3 * share), BF16),
                    shaped((tall + sum_rows(width, 3 * share), 3 * share), BF16),
                    shaped(small, F32),
                ],
                spot,
                left_keep,
                left_came,
                right_keep,
                right_came,
                sums,
                name="top_fold",
                smem=(0,),
            )
            w_came = flip(w_give, top_bit)

        def do_add():
            nonlocal in_sum, sent
            in_sum = call(add_kernel, [shaped((rows, width), BF16)], in_keep, in_came, name="add")[0]
            sent = send(in_sum, across)

        def do_o2():
            nonlocal o_came, o_keep
            o_keep, o_came = next_out(o_keep, o_came, len(plane_bits) - 1)

        def do_d_down():
            nonlocal d_down
            d_down = call(
                add_kernel,
                [shaped((piece, width), F32)],
                down_keep,
                far_came if paired else far_came[1],
                name="add",
            )[0]

        def do_home0():
            nonlocal columns, down_came, home_outs, home_steps, sums, tall, up_came, w_came, w_give, w_keep
            up_came, down_came = (far_came, far_came) if paired else far_came
            columns = 3 * share + ff // members
            home_steps = [(4, k, b) for k, b in reversed(list(enumerate(group_bits)))] + [(2, 0, 0)]

            def home_outs():
                rows_here = max(tall, 16)
                return [
                    shaped((rows_here, columns), BF16),
                    shaped((rows_here + sum_rows(width, columns), columns), BF16),
                    shaped(small, F32),
                ]

            tall //= 2
            w_keep, w_give, sums = call(
                functools.partial(home_first_kernel, *home_steps[0][:2]),
                home_outs(),
                spot,
                w_keep,
                w_came,
                up_keep,
                up_came,
                sums,
                name="home_first",
                smem=(0,),
            )
            w_came = flip(w_give, home_steps[0][2])

        def do_o3():
            nonlocal o_came, o_keep
            o_keep, o_came = next_out(o_keep, o_came)

        def do_last():
            nonlocal input_gradient
            input_gradient = call(
                last_kernel,
                [shaped((rows, width), BF16)],
                spot,
                vecs,
                in_keep,
                in_came,
                sent,
                own,
                grad_middle,
                name="input_gradient",
                smem=(0,),
            )[0]

        def do_home1():
            nonlocal b, columns, final, outs, shift, slot, sums, tall, w_came, w_give, w_keep
            for slot, shift, b in home_steps[1:]:
                tall //= 2
                columns *= 2
                outs = home_outs()
                final = (o_keep, o_came) if b == 0 else ()
                if final:
                    outs = [shaped((v.shape[0], columns + width // 2), BF16) for v in outs[:2]] + outs[2:]
                w_keep, w_give, sums = call(
                    functools.partial(home_next_kernel, slot, shift),
                    outs,
                    spot,
                    w_keep,
                    w_came,
                    sums,
                    *final,
                    name="home_next",
                    smem=(0,),
                )
                w_came = flip(w_give, b)

        def do_home_last():
            nonlocal d_in, d_out, d_up, vectors
            d_in, d_up, d_out, *vectors = call(
                functools.partial(home_last_kernel, lay),
                [shaped((each, 3 * width), F32), shaped((each, ff), F32), shaped((each, width), F32)]
                + [shaped((1, each), F32)] * 8
                + [shaped((1, piece), F32)],
                spot,
                w_keep,
                w_came,
                sums,
                name="home_last",
                smem=(0,),
            )
            vectors = [v.reshape(-1) for v in vectors]

        def do_relay():
            nonlocal far_att
            far_att = call(
                copy_kernel, [shaped(far_att[0].shape, BF16)], far_att[0], name="relay", after=tuple(near_att[1:])
            )

        steps = {
            "pack": do_pack,
            "mask": do_mask,
            "trade": do_trade,
            "join_down": do_join_down,
            "settle": do_settle,
            "bundle": do_bundle,
            "split": do_split,
            "stack": do_stack,
            "vectors": do_vectors,
            "join_up": do_join_up,
            "attend": do_attend,
            "unpair": do_unpair,
            "rows_own": do_rows_own,
            "stack_far": do_stack_far,
            "rows_far": do_rows_far,
            "forward": do_forward,
            "fold_norm": do_fold_norm,
            "gradients": do_gradients,
            "turn": do_turn,
            "pick": do_pick,
            "outer": do_outer,
            "out_fold": do_out_fold,
            "o0": do_o0,
            "assemble": do_assemble,
            "planes": do_planes,
            "attend_back": do_attend_back,
            "top_pair": do_top_pair,
            "input": do_input,
            "lr": do_lr,
            "dn1": do_dn1,
            "o1": do_o1,
            "layer": do_layer,
            "top": do_top,
            "add": do_add,
            "o2": do_o2,
            "d_down": do_d_down,
            "home0": do_home0,
            "o3": do_o3,
            "last": do_last,
            "home1": do_home1,
            "home_last": do_home_last,
            "relay": do_relay,
        }
        for name in PLAN:
            lay.order.step = name
            known = {
                "near": near,
                "far": far,
                "downs_came": downs_came,
                "ups_came": ups_came,
                "rows_came": rows_came,
                "pair_came": pair_came,
                "down_m": down_m,
                "down_c": down_c,
                "near_att": near_att,
                "far_att": far_att,
                "att_c": att_c,
                "outs_c": outs_c,
                "up_far_came": up_far_came,
                "down_far_came": down_far_came,
                "up_came": up_came,
                "down_came": down_came,
                "out_came": out_came,
                "o_came": o_came,
                "far_came": far_came,
                "sums_came": sums_came,
                "in_came": in_came,
            }
            lay.order.waits = tuple(
                v for w in WAITS.get(name, ()) for v in jax.tree.leaves(known[w])
            )
            steps[name]()
        return (
            layer_out[None],
            input_gradient[None],
            vectors[0],
            vectors[1],
            d_in,
            vectors[2],
            vectors[3],
            d_out,
            vectors[4],
            vectors[5],
            vectors[6],
            d_up,
            vectors[8],
            d_down,
            vectors[7],
        )

    vector, matrix = P(AXES), P(AXES, None)
    tokens = P("batch", "blk", None)
    return jax.shard_map(
        local,
        mesh=mesh,
        in_specs=(
            tokens,
            P("batch", None),
            P("batch"),
            vector,
            vector,
            matrix,
            vector,
            vector,
            matrix,
            vector,
            vector,
            vector,
            matrix,
            vector,
            matrix,
            vector,
            tokens,
        ),
        out_specs=(
            tokens,
            tokens,
            vector,
            vector,
            matrix,
            vector,
            vector,
            matrix,
            vector,
            vector,
            vector,
            matrix,
            vector,
            matrix,
            vector,
        ),
        check_vma=False,
    )
```

```python
import functools

import jax
import jax.numpy as jnp
from jax import lax
from jax.experimental import pallas as pl
from jax.experimental.pallas import tpu as pltpu
from jax.sharding import PartitionSpec as P

HEADS = 16
EPSILON = 1e-05
SCORE_SCALE = 0.125
MASKED = -1e30
LANES = 128
AXES = ("blk", "batch")
F32 = jnp.float32
BF16 = jnp.bfloat16

NT = (((1,), (1,)), ((), ()))
NN = (((1,), (0,)), ((), ()))
TN = (((0,), (0,)), ((), ()))


def dot(a, b, dims=NN):
    return lax.dot_general(a, b, dims, preferred_element_type=F32)


def bits_of(size):
    return size.bit_length() - 1


def key_mask_terms(rows):
    key = lax.broadcasted_iota(jnp.int32, (rows, rows), 0)
    query = lax.broadcasted_iota(jnp.int32, (rows, rows), 1)
    return key < query, key == query


def centre(values):
    average = jnp.mean(values, axis=-1, keepdims=True)
    centred = values - average
    variance = jnp.mean(centred * centred, axis=-1, keepdims=True)
    scale = lax.rsqrt(variance + EPSILON)
    return centred * scale, scale


def norm_back(slope, normal, scale, gain):
    weighted = slope * gain
    return scale * (
        weighted
        - jnp.mean(weighted, axis=-1, keepdims=True)
        - normal * jnp.mean(weighted * normal, axis=-1, keepdims=True)
    )


GELU_A = 0.7978845608028654
GELU_B = 0.044715


def gelu_terms(pre):
    square = pre * pre
    bend = jnp.tanh(GELU_A * pre * (1.0 + GELU_B * square))
    half = 0.5 * (1.0 + bend)
    slope = half + 0.5 * pre * (1.0 - bend * bend) * (GELU_A * (1.0 + 3.0 * GELU_B * square))
    return pre * half, slope


EXTRA = 16


WEIGHTS = {'pack': 10000000000, 'unpair': 10000000000, 'trade': 1, 'join_down': 1, 'mask': 1}
FREE = {'trade': [0]}
WAITS = {'stack_far': ['down_c'], 'pick': ['ups_came'], 'd_down': ['down_came']}
GRANTS = {'o2': 32}
HEAVY = 10**11
PLAN = (
    "pack",
    "mask",
    "trade",
    "join_down",
    "settle",
    "bundle",
    "split",
    "stack",
    "vectors",
    "join_up",
    "attend",
    "unpair",
    "stack_far",
    "relay",
    "rows_own",
    "rows_far",
    "forward",
    "fold_norm",
    "gradients",
    "turn",
    "outer",
    "pick",
    "o0",
    "out_fold",
    "assemble",
    "planes",
    "attend_back",
    "top_pair",
    "input",
    "lr",
    "dn1",
    "o1",
    "top",
    "o2",
    "add",
    "d_down",
    "home0",
    "layer",
    "o3",
    "last",
    "home1",
    "home_last",
)


def shaped(shape, kind):
    return jax.ShapeDtypeStruct(shape, kind)


class Order:
    def __init__(self):
        self.ticket = ()
        self.step = ""
        self.waits = ()


def kernel_call(order, body, outs, *args, name, smem=(), away=(), scratch=(), vmem=8, after=()):
    weight = WEIGHTS.get(order.step, HEAVY)
    after = tuple(v for i, v in enumerate(after) if i not in FREE.get(order.step, ()))
    after, order.waits = after + order.waits, ()
    count, given, held = len(args), len(outs), len(order.ticket)
    inner = body

    def body(*refs):
        ins, rest = refs[:count], refs[count + len(after) :]
        before, rest = rest[:held], rest[held:]
        results, ticket = rest[:given], rest[given]
        ticket[...] = before[0][...] if held else jnp.zeros_like(ticket)
        inner(*ins, *results, *rest[given + 1 :])

    away = tuple(away) + tuple(range(count, count + len(after)))
    args = args + tuple(after) + order.ticket
    outs = list(outs) + [shaped((8, LANES), F32)]

    def spec(i, places):
        if i in places:
            return pl.BlockSpec(memory_space=pl.ANY)
        return pl.BlockSpec(memory_space=pltpu.VMEM)

    ins = [
        pl.BlockSpec(memory_space=pltpu.SMEM) if i in smem else spec(i, away)
        for i in range(len(args))
    ]
    moved = sum(v.size * v.dtype.itemsize for v in args + tuple(outs))
    *results, ticket = pl.pallas_call(
        body,
        in_specs=ins,
        out_specs=[spec(i, ()) for i in range(len(outs))],
        out_shape=list(outs),
        scratch_shapes=list(scratch),
        compiler_params=pltpu.CompilerParams(vmem_limit_bytes=GRANTS.get(order.step, vmem) * 2**20),
        cost_estimate=pl.CostEstimate(flops=weight, bytes_accessed=1, transcendentals=0),
        name=name,
    )(*args)
    order.ticket = (ticket,)
    return results


def iota(shape, dim):
    return lax.broadcasted_iota(jnp.int32, shape, dim)


class Layout:
    def __init__(self, nb, nt, rows, width, ff, length):
        self.nb, self.nt, self.rows, self.width, self.ff, self.length = nb, nt, rows, width, ff, length
        self.devices = nb * nt
        self.size = nb // 2
        self.planes = nt // 2
        self.members = 2 * self.size
        self.each = width // self.devices
        self.piece = ff // self.devices
        self.share = width // self.members
        self.ff_share = ff // self.members
        self.small = 8 * self.each + self.piece
        self.valid_at = -(-self.small // 512) * 512
        self.head = width // HEADS
        self.order = Order()


def each_way(flag, write):
    pl.when(flag == 0)(lambda: write(0))
    pl.when(flag == 1)(lambda: write(1))


def write_half(lay, side, count, in_from, up_from, in_start, up_start, give, keep, n):
    hw, pc = lay.share, lay.piece
    tail = lay.planes * pc if count > 0 else pc
    spans = []
    if count == 0:
        for q in range(3 * lay.size):
            spans.append((in_from, in_start + 2 * q * hw, hw))
        for q in range(2 * lay.size * lay.planes):
            spans.append((up_from, up_start + 2 * q * pc, pc))
    else:
        for q in range(3 * count // 2):
            spans.append((in_from, in_start + 2 * q * hw, hw))
        for q in range(count):
            spans.append((up_from, up_start + 2 * q * tail, tail))
    at = 0
    for source, start, span in spans:
        mine = source[0:n, start + side * span : start + (side + 1) * span]
        other = source[0:n, start + (1 - side) * span : start + (2 - side) * span]
        keep[0:n, at : at + span] = mine
        give[0:n, at : at + span] = other
        at += span


def load_all(pairs, sems):
    copies = [pltpu.make_async_copy(a, b, sems.at[i]) for i, (a, b) in enumerate(pairs)]
    for copy in copies:
        copy.start()
    return copies


def wait_all(copies):
    for copy in copies:
        copy.wait()


def pack_kernel(lay, spot, lengths, *refs):
    sources, (give, keep), targets, sems = refs[:13], refs[13:15], refs[15:28], refs[28]
    wait_all(load_all(list(zip(sources, targets, strict=True)), sems))
    w_in, w_up, mask, w_out = targets[:4]
    smalls = targets[4:]
    n = lay.each
    base = max(n, 16)
    if base > n:
        for ref in (give, keep):
            ref[0:base, :] = jnp.zeros((base, ref.shape[1]), BF16)
    each_way(spot[2], lambda side: write_half(lay, side, 0, w_in, w_up, 0, 0, give, keep, n))
    half = lay.width // 2
    last = give.shape[1] - half

    def write_out(side):
        keep[0:n, last:] = w_out[:, side * half : (side + 1) * half]
        give[0:n, last:] = w_out[:, (1 - side) * half : (2 - side) * half]

    each_way(spot[2], write_out)
    line = jnp.zeros((1, lay.small), F32)
    at = 0
    for ref in smalls:
        span = ref.shape[1]
        where = iota((span, lay.small), 1) == iota((span, lay.small), 0) + at
        line = line + dot(ref[...], where.astype(F32).astype(BF16))
        at += span
    row = iota((EXTRA, lay.small), 0) == spot[5]
    extra = jnp.where(row, line, 0.0).astype(BF16)
    live = (mask[...] > 0) & (iota(mask.shape, 1) < lengths[0])
    valid = jnp.where(live, 1.0, 0.0) * jnp.ones((EXTRA, 1), F32)
    for ref in (give, keep):
        ref[base : base + EXTRA, :] = jnp.zeros((EXTRA, ref.shape[1]), BF16)
        ref[base : base + EXTRA, 0 : lay.small] = extra
        ref[base : base + EXTRA, lay.valid_at : lay.valid_at + lay.length] = valid.astype(BF16)


def merge_rows(keep, came, side, n, out):
    if n < 16:
        mine, theirs = keep[0:16, :].astype(F32)[0:n], came[0:16, :].astype(F32)[0:n]
        first = jnp.where(side == 0, mine, theirs)
        second = jnp.where(side == 0, theirs, mine)
        out[...] = jnp.concatenate([first, second], axis=0).astype(BF16)
        return
    out[pl.ds(pl.multiple_of(side * n, n), n), :] = keep[0:n, :]
    out[pl.ds(pl.multiple_of((1 - side) * n, n), n), :] = came[0:n, :]


def merge_extra(lay, keep, came, n):
    n = max(n, 16)
    total = keep[n : n + EXTRA, 0 : lay.small].astype(F32) + came[n : n + EXTRA, 0 : lay.small].astype(F32)
    return total.astype(BF16)


def trade_kernel(lay, step, count, spot, keep, came, give, hold, valid, both):
    n = (1 << step) * lay.each
    merge_rows(keep, came, spot[2] if step == 0 else (spot[4] >> (step - 1)) & 1, n, both)
    start = 3 * count * lay.share
    each_way(
        (spot[4] >> step) & 1,
        lambda side: write_half(lay, side, count, both, both, 0, start, give, hold, 2 * n),
    )
    half = lay.width // 2
    for ref in (give, hold):
        ref[0 : 2 * n, ref.shape[1] - half :] = both[:, both.shape[1] - half :]
    extra = merge_extra(lay, keep, came, n)
    for ref in (give, hold):
        ref[2 * n : 2 * n + EXTRA, :] = jnp.zeros((EXTRA, ref.shape[1]), BF16)
        ref[2 * n : 2 * n + EXTRA, 0 : lay.small] = extra
    if step == 0:
        place = slice(lay.valid_at, lay.valid_at + lay.length)
        base = max(n, 16)
        mine, theirs = (ref[base : base + 16, place].astype(F32)[0:8] for ref in (keep, came))
        valid[...] = jnp.where(spot[6] == 1, mine, theirs)
    else:
        valid[...] = jnp.zeros_like(valid)


def settle_kernel(
    lay, step, spot, keep, came, far, down, in_block, up_block, far_out, pair, both
):
    far_out[...] = far[...]
    n = (1 << step) * lay.each
    merge_rows(keep, came, (spot[4] >> (step - 1)) & 1, n, both)
    cut = 3 * lay.share
    in_block[0 : 2 * n, :] = both[:, 0:cut]
    last = cut + lay.ff_share
    tall, half = 2 * n, lay.width // 2
    chunks = lay.ff_share // half
    part = tall // chunks
    targets = [up_block.at[0]] + ([pair] if pair.shape[0] > 8 else [])
    for ref in targets:
        ref[0:tall, :] = both[:, cut:last]
        for i in range(chunks):
            rows = both[i * part : (i + 1) * part, last:]
            ref[tall : tall + part, i * half : (i + 1) * half] = rows
    if pair.shape[0] > 8:
        pair[tall + part :, :] = down[...]
    in_block[2 * n : 2 * n + EXTRA, :] = jnp.zeros((EXTRA, cut), BF16)
    in_block[2 * n : 2 * n + EXTRA, 0 : lay.small] = merge_extra(lay, keep, came, n)


def split_kernel(cut, mine, came, pair, grad, left, right, pair_out, grad_out):
    pair_out[...] = pair[...]
    grad_out[...] = grad[...]
    left[0], left[1] = mine[:, 0:cut], came[:, 0:cut]
    right[0], right[1] = mine[:, cut:], came[:, cut:]


def stack_kernel(one, one_came, two, two_came, one_out, two_out):
    n = one.shape[0]
    one_out[0:n], one_out[n : 2 * n] = one[...], one_came[...]
    two_out[0:n], two_out[n : 2 * n] = two[...], two_came[...]


def stack(lay, one, one_came, two, two_came, *after):
    outs = [shaped((2 * v.shape[0],) + v.shape[1:], BF16) for v in (one, two)]
    return kernel_call(
        lay.order, stack_kernel, outs, one, one_came, two, two_came, name="stack", after=after
    )


def unpair_kernel(pair, up, down):
    n = up.shape[1]
    up[0], down[0] = pair[0:n, :], pair[n:, :]


def bundle_kernel(g, spot, *refs):
    near, far, out = refs[:g], refs[g : 2 * g], refs[2 * g]
    rows = near[0].shape[0]

    def write(home):
        parts = list(near) if home else list(far) + list(near)
        for i, ref in enumerate(parts):
            out[i * rows : (i + 1) * rows, :] = ref[...]

    each_way(spot[6], write)


def copy_kernel(value, out):
    out[...] = value[...]


def out_kernel_rows(mine, came, out):
    count, tall, half = out.shape
    chunks = mine.shape[2] // half
    part = tall // chunks
    for k in range(count):
        source = (mine if k < count // 2 else came).at[k % (count // 2)]
        for i in range(chunks):
            rows = source[tall : tall + part, i * half : (i + 1) * half]
            out[k, i * part : (i + 1) * part, :] = rows


def join_kernel(one, one_came, out):
    n = one.shape[0]
    out[0:n], out[n : 2 * n] = one[...], one_came[...]


def join(lay, one, one_came, *after):
    out = shaped((2 * one.shape[0],) + one.shape[1:], BF16)
    return kernel_call(lay.order, join_kernel, [out], one, one_came, name="join", after=after)[0]


def block_spot(lay, spot, k, flipped):
    bits = bits_of(lay.planes)
    top = (spot[3] ^ k) & 1
    order = range(bits - 1, -1, -1) if flipped else range(bits)
    plane = spot[1] >> 1
    for position, b in enumerate(order):
        plane = plane ^ (((k >> (position + 1)) & 1) << b)
    return top, plane


def vector_kernel(lay, spot, first, second, out, rows, sems):
    n, count, wide = lay.members * lay.each, 2 * lay.planes, rows.shape[1]
    copies = []
    for k in range(count):
        source = first if k < count // 2 else second
        copy = pltpu.make_async_copy(
            source.at[k % (count // 2), n : n + EXTRA, 0:wide],
            rows.at[k * EXTRA : (k + 1) * EXTRA, :],
            sems.at[k],
        )
        copy.start()
        copies.append(copy)
    for copy in copies:
        copy.wait()
    out[...] = jnp.zeros_like(out)
    tall = count * EXTRA
    line, lane = iota((tall, lay.width), 0), iota((tall, lay.width), 1)
    holder, block = jnp.zeros_like(line), jnp.zeros_like(line)
    for k in range(count):
        top, plane = block_spot(lay, spot, k, False)
        inside = line - k * EXTRA
        here = (inside >= 0) & (inside < EXTRA)
        lead = (top * lay.size + inside // 2) * lay.nt + plane * 2 + inside % 2
        holder = jnp.where(here, jnp.where(inside < lay.members, lead, -1), holder)
        block = jnp.where(here & (inside == spot[5]), top * lay.planes + plane, jnp.where(here, -1, block))
    values = rows[...]
    source, target = iota((wide, lay.width), 0), iota((wide, lay.width), 1)
    for v in range(8):
        spread = (source == v * lay.each + target % lay.each).astype(F32).astype(BF16)
        tiled = jnp.where(lane // lay.each == holder, dot(values, spread), 0.0)
        out[v : v + 1, :] = jnp.sum(tiled, axis=0, keepdims=True)
    spread = (source == 8 * lay.each + target % lay.piece).astype(F32).astype(BF16)
    tiled = jnp.where(lane // lay.piece == block, dot(values, spread), 0.0)
    out[8:9, :] = jnp.sum(tiled, axis=0, keepdims=True)
    hw = lay.share
    mine = pl.ds(pl.multiple_of(spot[5] * hw, hw), hw)
    out[9:10, 0:hw] = out[2:3, mine]
    out[9:10, 2 * hw : 3 * hw] = out[3:4, mine]


def attend_kernel(lay, spot, bias, vecs, *refs):
    g, rows, hw, length, head = lay.size, lay.rows, lay.share, lay.length, lay.head
    near, far, came = refs[:g], refs[g : 2 * g], refs[2 * g]
    near_c = far_c = [came.at[e * rows : (e + 1) * rows, :] for e in range(g)]
    weights = refs[2 * g + 1 : 2 * g + 5]
    near_att, far_att, joint, wide, lse, normed, x, w, x_sems, w_sems = refs[2 * g + 5 :]
    group, place = spot[3], spot[4]
    pending = []
    for e in range(g):
        for side, (at_home, at_away) in enumerate(((near[e], near_c[e]), (far_c[e], far[e]))):
            spot_here = (place if side == 0 else g - 1 - place) ^ e
            spot_here = (group if side == 0 else 1 - group) * g + spot_here
            target = x.at[pl.ds(pl.multiple_of(spot_here * rows, rows), rows), :]
            sem = x_sems.at[side * g + e]
            home = pltpu.make_async_copy(at_home, target, sem)
            visit = pltpu.make_async_copy(at_away, target, sem)
            pl.when(spot[6] == 1)(home.start)
            pl.when(spot[6] == 0)(visit.start)
            pending.append(home)
    count = 2 * lay.planes
    span = 2 * lay.each
    cut = weights[0].shape[-1]
    loads = []
    for k in range(count):
        for side in range(2):
            source = weights[2 * side + (k >= count // 2)]
            top, plane = block_spot(lay, spot, k, side == 1)
            for q in range(g):
                start = ((top * g + q) * lay.planes + plane) * span
                copy = pltpu.make_async_copy(
                    source.at[k % (count // 2), q * span : (q + 1) * span, :],
                    w.at[pl.ds(pl.multiple_of(start, span), span), 0:cut]
                    if side == 0
                    else w.at[pl.ds(pl.multiple_of(start, span), span), cut:],
                    w_sems.at[(k * 2 + side) * g + q],
                )
                copy.start()
                loads.append(copy)
    for copy in pending:
        copy.wait()
    for j in range(length // rows):
        here = slice(j * rows, (j + 1) * rows)
        normal, _ = centre(x[here, :].astype(F32))
        normed[here, :] = (normal * vecs[0:1, :] + vecs[1:2, :]).astype(BF16)
    for copy in loads:
        copy.wait()
    for j in range(length // rows):
        here = slice(j * rows, (j + 1) * rows)
        joint[here, :] = (dot(normed[here, :], w[...]) + vecs[9:10, 0 : 3 * hw]).astype(BF16)
    earlier, same = key_mask_terms(rows)
    lane = iota((rows, LANES), 1)
    for p in range(hw // LANES):
        q_at, k_at, v_at = (slice(i * hw + p * LANES, i * hw + (p + 1) * LANES) for i in range(3))
        value_t = joint[:, v_at].astype(F32).T.astype(BF16)
        for j in range(length // rows):
            here, past = slice(j * rows, (j + 1) * rows), slice(0, j * rows)
            bias_here = bias[here, :]
            for h in range(LANES // head):
                mine = (lane >= h * head) & (lane < (h + 1) * head)
                query = jnp.where(mine, joint[here, q_at].astype(F32) * SCORE_SCALE, 0.0).astype(BF16)
                inner = dot(joint[here, k_at], query, NT)
                inner = jnp.where(same, inner, jnp.where(earlier, inner + bias_here, MASKED))
                top = jnp.max(inner, axis=0, keepdims=True)
                if j:
                    outer = dot(joint[past, k_at], query, NT) + bias[past, :]
                    top = jnp.maximum(top, jnp.max(outer, axis=0, keepdims=True))
                inner = jnp.exp(inner - top)
                total = jnp.sum(inner, axis=0, keepdims=True)
                if j:
                    outer = jnp.exp(outer - top)
                    total = total + jnp.sum(outer, axis=0, keepdims=True)
                share = 1.0 / total
                value_h = value_t[h * head : (h + 1) * head]
                out = dot(value_h[:, here], (inner * share).astype(BF16))
                if j:
                    out = out + dot(value_h[:, past], (outer * share).astype(BF16))
                at = p * LANES + h * head
                wide[at : at + head, here] = out
                lse[p, h : h + 1, here] = top + jnp.log(total)
    for i in range(g):
        here = slice(i * rows, (i + 1) * rows)
        for out_ref, first in ((near_att, group * g + i), (far_att, (1 - group) * g + i)):
            part = wide[:, pl.ds(pl.multiple_of(first * rows, rows), rows)]
            out_ref[here, :] = part.T.astype(BF16)


def attend(lay, spot, bias, vecs, hidden, weights):
    d, hw, length, g = lay.width, lay.share, lay.length, lay.size
    outs = [
        shaped((g * lay.rows, hw), BF16),
        shaped((g * lay.rows, hw), BF16),
        shaped((length, 3 * hw), BF16),
        shaped((hw, length), F32),
        shaped((hw // LANES, 8, length), F32),
        shaped((length, d), BF16),
        shaped((length, d), BF16),
        shaped((d, 3 * hw), BF16),
    ]
    copies = 2 * lay.planes * 2 * g
    args = (spot, bias, vecs) + tuple(hidden) + tuple(weights)
    return kernel_call(
        lay.order,
        functools.partial(attend_kernel, lay),
        outs,
        *args,
        name="attend",
        smem=(0,),
        away=tuple(range(3, len(args))),
        scratch=[
            pltpu.SemaphoreType.DMA((2 * g,)),
            pltpu.SemaphoreType.DMA((copies,)),
        ],
        vmem=24,
    )


def fold_kernel(slot, shift, a, b, spot, keep, came, hold, give):
    total = keep[...].astype(F32) + came[...].astype(F32)
    side = (spot[slot] >> shift) & 1
    view = total.reshape(a, 2, b, total.shape[-1])

    def write(s):
        hold[...] = view[:, s].reshape(a * b, -1).astype(BF16)
        give[...] = view[:, 1 - s].reshape(a * b, -1).astype(BF16)

    each_way(side, write)


def fold(lay, spot, slot, shift, a, keep, came):
    count, columns = keep.shape
    b = count // (2 * a)
    return kernel_call(
        lay.order,
        functools.partial(fold_kernel, slot, shift, a, b),
        [shaped((a * b, columns), BF16)] * 2,
        spot,
        keep,
        came,
        name="fold",
        smem=(0,),
    )


def mask_kernel(spot, lengths, cotangent, out):
    rows = out.shape[0]
    live = spot[0] * rows + iota((rows, 1), 0) < lengths[0]
    out[...] = jnp.where(live, cotangent[...].astype(F32), 0.0).astype(BF16)


def place_rows(lay, spot, e):
    return spot[4] ^ e


def block_of(lay, blocks, k):
    mine, came = blocks[2 * (k & 1)], blocks[2 * (k & 1) + 1]
    half = lay.planes // 2
    return (mine if k >> 1 < half else came).at[(k >> 1) % half]


def up_loads(lay, spot, blocks, w_up):
    pairs = []
    span, g = 2 * lay.each, lay.size
    for k in range(2 * lay.planes):
        source = block_of(lay, blocks, k)
        top, plane = block_spot(lay, spot, k, False)
        for q in range(g):
            start = ((top * g + q) * lay.planes + plane) * span
            pairs.append(
                (
                    source.at[q * span : (q + 1) * span, :],
                    w_up.at[pl.ds(pl.multiple_of(start, span), span), :],
                )
            )
    return pairs


def down_loads(lay, spot, blocks, w_down):
    pairs = []
    for k in range(2 * lay.planes):
        top, plane = block_spot(lay, spot, k, True)
        start = (top * lay.planes + plane) * lay.piece
        target = w_down.at[pl.ds(pl.multiple_of(start, lay.piece), lay.piece), :]
        pairs.append((block_of(lay, blocks, k), target))
    return pairs


def row_loads(lay, spot, mine, swapped, target):
    pairs = []
    g, rows = lay.size, lay.rows
    for e in range(g):
        for source, sequence in ((mine[e], spot[2]), (swapped[e], 1 - spot[2])):
            start = (sequence * g + (spot[4] ^ e)) * rows
            pairs.append((source, target.at[pl.ds(pl.multiple_of(start, rows), rows), :]))
    return pairs


def out_loads(lay, spot, blocks, target):
    pairs = []
    half, span, g = lay.width // 2, 2 * lay.each, lay.size
    for i, block in enumerate(blocks):
        column = pl.multiple_of((spot[2] ^ (i // 2)) * half, half)
        for k in range(lay.planes):
            top, plane = block_spot(lay, spot, 2 * k + i % 2, False)
            for q in range(g):
                row = pl.multiple_of(((top * g + q) * lay.planes + plane) * span, span)
                source = block.at[k, q * span : (q + 1) * span, :]
                pairs.append((source, target.at[pl.ds(row, span), pl.ds(column, half)]))
    return pairs


def forward_kernel(lay, spot, vecs, *refs):
    outs, refs = refs[:4], refs[4:]
    g, rows, hw, d = lay.size, lay.rows, lay.share, lay.width
    lists = [refs[i * g : (i + 1) * g] for i in range(7)]
    near, far, near_c, far_c, base_m, down_m, down_c = lists
    refs = refs[7 * g :]
    bundle, ups, downs = refs[0], refs[1:5], refs[5:9]
    (
        dn_keep,
        dn_give,
        middle_own,
        att_own,
        normed,
        act,
        grad_pre,
        bias_sum,
        wo,
        att,
        base,
        gd,
        w_up,
        w_down,
        sems,
    ) = refs[9:]
    core, group, place = spot[2], spot[3], spot[4]
    span = g * rows
    pairs = out_loads(lay, spot, outs, wo)
    for e in range(g):
        for source, sequence, at, side in (
            (near[e], group, place ^ e, core),
            (near_c[e], group, place ^ e, 1 - core),
            (far[e], 1 - group, (g - 1 - place) ^ e, core),
            (far_c[e], 1 - group, (g - 1 - place) ^ e, 1 - core),
        ):
            row = pl.multiple_of(sequence * span, span)
            column = pl.multiple_of((at * 2 + side) * hw, hw)
            pairs.append((source, att.at[pl.ds(row, span), pl.ds(column, hw)]))
    first_row = jnp.where(spot[6] == 1, span, 0)
    base_c = [
        bundle.at[pl.ds(pl.multiple_of(first_row + e * rows, rows), rows), :] for e in range(g)
    ]
    pairs += row_loads(lay, spot, base_m, base_c, base)
    first = len(pairs)
    pairs += up_loads(lay, spot, ups, w_up) + down_loads(lay, spot, downs, w_down)
    pairs += row_loads(lay, spot, down_m, down_c, gd)
    copies = [pltpu.make_async_copy(a, b, sems.at[i]) for i, (a, b) in enumerate(pairs)]
    for copy in copies[:first]:
        copy.start()
    wait_all(copies[:first])
    for copy in copies[first:]:
        copy.start()
    bias_out, gain, shift = vecs[4:5, :], vecs[5:6, :], vecs[6:7, :]
    bias_up = vecs[8:9, 0 : lay.ff_share]
    total = jnp.zeros((1, lay.ff_share), F32)
    for i in range(2 * g):
        here = slice(i * rows, (i + 1) * rows)
        middle = base[here, :].astype(F32) + (dot(att[here, :], wo[...]) + bias_out)
        normal, _ = centre(middle)
        normed[here, :] = (normal * gain + shift).astype(BF16)

        @pl.when((core == i // g) & (place == i % g))
        def _():
            middle_own[...] = middle
            att_own[...] = att[here, :]

    wait_all(copies[first:])
    for i in range(2 * g):
        here = slice(i * rows, (i + 1) * rows)
        pre = dot(normed[here, :], w_up[...]) + bias_up
        value, slope = gelu_terms(pre)
        act[here, :] = value.astype(BF16)
        grad = (dot(gd[here, :], w_down[...], NT) * slope).astype(BF16)
        grad_pre[here, :] = grad
        total = total + jnp.sum(grad.astype(F32), axis=0, keepdims=True)
        back = dot(grad, w_up[...], NT).astype(BF16)
        at = slice((i % g) * rows, (i % g + 1) * rows)

        @pl.when(core == i // g)
        def _():
            dn_keep[at, :] = back

        @pl.when(core != i // g)
        def _():
            dn_give[at, :] = back

    bias_sum[...] = total


def forward_call(lay, spot, vecs, outs_w, lists, blocks):
    d, f, rows, g = lay.width, lay.ff_share, lay.rows, lay.size
    tokens = 2 * g * rows
    outs = [
        shaped((g * rows, d), BF16),
        shaped((g * rows, d), BF16),
        shaped((rows, d), F32),
        shaped((rows, d), BF16),
        shaped((tokens, d), BF16),
        shaped((tokens, f), BF16),
        shaped((tokens, f), BF16),
        shaped((1, f), F32),
        shaped((d, d), BF16),
    ]
    args = (spot, vecs) + tuple(outs_w) + tuple(lists) + tuple(blocks)
    copies = 4 * lay.planes * g + 8 * g + 2 * lay.planes * (g + 1)
    return kernel_call(
        lay.order,
        functools.partial(forward_kernel, lay),
        outs,
        *args,
        name="feed_forward",
        smem=(0,),
        away=tuple(range(2, len(args))),
        scratch=[
            pltpu.VMEM((tokens, d), BF16),
            pltpu.VMEM((tokens, d), BF16),
            pltpu.VMEM((tokens, d), BF16),
            pltpu.VMEM((d, f), BF16),
            pltpu.VMEM((f, d), BF16),
            pltpu.SemaphoreType.DMA((copies,)),
        ],
        vmem=24,
    )


def cut_rows(value, side, a, b, keep, give):
    for i in range(a):
        for ref, s in ((keep, side), (give, 1 - side)):
            start = pl.multiple_of((2 * i + s) * b, b)
            ref[i * b : (i + 1) * b, :] = value[pl.ds(start, b), :]


def gradient_kernel(lay, spot, normed, act, grad_pre, *refs):
    g, rows, d, f = lay.size, lay.rows, lay.width, lay.ff_share
    down_m, down_c, blocks = refs[:g], refs[g : 2 * g], refs[2 * g : 2 * g + 4]
    up_keep, up_give, down_keep, down_give, out_keep, out_give, gd, w_down, full, sems = refs[
        2 * g + 4 :
    ]
    pairs = row_loads(lay, spot, down_m, down_c, gd)
    pairs += down_loads(lay, spot, blocks, w_down)
    copies = load_all(pairs, sems)
    tile = 256
    for i in range(d // tile):
        here = slice(i * tile, (i + 1) * tile)
        full[here, 0:f] = dot(normed[:, here], grad_pre[...], TN).astype(BF16)
    plane_bits = bits_of(lay.planes)
    side = (spot[1] >> plane_bits) & 1
    cut_rows(full.at[0:d, 0:f], side, 2 * g, d // (4 * g), up_keep, up_give)
    wait_all(copies)
    tile = min(256, f)
    for i in range(f // tile):
        here = slice(i * tile, (i + 1) * tile)
        full[here, 0:d] = dot(act[:, here], gd[...], TN).astype(BF16)
    side = (spot[1] >> 1) & 1
    cut_rows(full.at[0:f, 0:d], side, lay.planes, lay.piece, down_keep, down_give)
    for i in range(2 * g):
        here = slice(i * rows, (i + 1) * rows)
        at = slice((i % g) * rows, (i % g + 1) * rows)
        part = dot(act[here, :], w_down[...]).astype(BF16)

        @pl.when(spot[2] == i // g)
        def _():
            out_keep[at, :] = part

        @pl.when(spot[2] != i // g)
        def _():
            out_give[at, :] = part


def gradient_call(lay, spot, normed, act, grad_pre, down_m, down_c, blocks):
    d, f, rows, g = lay.width, lay.ff_share, lay.rows, lay.size
    tokens = 2 * g * rows
    outs = [shaped((d // 2, f), BF16)] * 2 + [shaped((f // 2, d), BF16)] * 2
    outs += [shaped((g * rows, d), BF16)] * 2
    args = (spot, normed, act, grad_pre) + tuple(down_m) + tuple(down_c) + tuple(blocks)
    return kernel_call(
        lay.order,
        functools.partial(gradient_kernel, lay),
        outs,
        *args,
        name="gradients",
        smem=(0,),
        away=tuple(range(4, len(args))),
        scratch=[
            pltpu.VMEM((tokens, d), BF16),
            pltpu.VMEM((f, d), BF16),
            pltpu.VMEM((d, d), BF16),
            pltpu.SemaphoreType.DMA((2 * g + 2 * lay.planes,)),
        ],
        vmem=24,
    )


def turn_kernel(lay, spot, vecs, keep, came, middle, grad_low, w_out, *refs):
    keep_out, give_out, grad_middle, grad_branch, sums, wo, att_grad, sems = refs
    copies = load_all([(w_out, wo)], sems)
    normal, scale = centre(middle[...])
    slope = keep[...].astype(F32) + came[...].astype(F32)
    total = grad_low[...].astype(F32) + norm_back(slope, normal, scale, vecs[5:6, :])
    grad_middle[...] = total
    branch = total.astype(BF16)
    grad_branch[...] = branch
    sums[...] = jnp.zeros_like(sums)
    add = lambda value: jnp.sum(value, axis=0, keepdims=True)
    sums[0:1, :] = add(branch.astype(F32))
    sums[1:2, :] = add(slope * normal)
    sums[2:3, :] = add(slope)
    sums[3:4, :] = add(grad_low[...].astype(F32))
    wait_all(copies)
    att_grad[...] = dot(branch, wo[...], NT).astype(BF16)
    hw = lay.share
    for i in range(lay.size):
        for ref, side in ((keep_out, spot[2]), (give_out, 1 - spot[2])):
            start = pl.multiple_of((2 * i + side) * hw, hw)
            ref[:, i * hw : (i + 1) * hw] = att_grad[:, pl.ds(start, hw)]


def outer_kernel(spot, att, branch, keep, give):
    tile, half = 256, keep.shape[1]

    def write(side):
        for i in range(keep.shape[0] // tile):
            here = slice(i * tile, (i + 1) * tile)
            value = dot(att[:, here], branch[...], TN).astype(BF16)
            keep[here, :] = value[:, side * half : (side + 1) * half]
            give[here, :] = value[:, (1 - side) * half : (2 - side) * half]

    each_way(spot[2], write)


def pick_kernel(lay, spot, mine, came, *pieces):
    hw = lay.share
    for r in range(lay.members):
        chip = spot[0] ^ r
        column = pl.ds(pl.multiple_of(chip % lay.size * hw, hw), hw)
        own = chip // lay.size == spot[2]

        @pl.when(own)
        def _(r=r, column=column):
            pieces[r][...] = mine[:, column]

        @pl.when(jnp.logical_not(own))
        def _(r=r, column=column):
            pieces[r][...] = came[:, column]


def turn_call(lay, spot, vecs, keep, came, middle, grad_low, w_out):
    d, rows = lay.width, lay.rows
    outs = [shaped((rows, d // 2), BF16)] * 2
    outs += [shaped((rows, d), F32), shaped((rows, d), BF16), shaped((8, d), F32)]
    return kernel_call(
        lay.order,
        functools.partial(turn_kernel, lay),
        outs,
        spot,
        vecs,
        keep,
        came,
        middle,
        grad_low,
        w_out,
        name="turn",
        smem=(0,),
        away=(6,),
        scratch=[
            pltpu.VMEM((d, d), BF16),
            pltpu.VMEM((rows, d), BF16),
            pltpu.SemaphoreType.DMA((1,)),
        ],
        vmem=24,
    )


def assemble_kernel(lay, spot, *refs):
    out = refs[-1]
    for r in range(lay.members):
        start = pl.multiple_of((spot[0] ^ r) * lay.rows, lay.rows)
        out[pl.ds(start, lay.rows), :] = refs[r][...]


def attend_back_kernel(lay, spot, bias, joint, wide, lse, normed, slope_all, *refs):
    rows, hw, length, head, d = lay.rows, lay.share, lay.length, lay.head, lay.width
    (
        grads_out,
        left_keep,
        left_give,
        right_keep,
        right_give,
        sums,
        key_sum,
        value_sum,
        query_t,
        full,
    ) = refs
    earlier, same = key_mask_terms(rows)
    lane = iota((rows, LANES), 1)
    for p in range(hw // LANES):
        q_at, k_at, v_at = (slice(i * hw + p * LANES, i * hw + (p + 1) * LANES) for i in range(3))
        s_at = slice(p * LANES, (p + 1) * LANES)
        key_t = joint[:, k_at].astype(F32).T.astype(BF16)
        product = slope_all[:, s_at].astype(F32).T * wide[s_at, :]
        key_sum[...] = jnp.zeros_like(key_sum)
        value_sum[...] = jnp.zeros_like(value_sum)
        for j in range(length // rows):
            here = slice(j * rows, (j + 1) * rows)
            for h in range(LANES // head):
                mine = (lane >= h * head) & (lane < (h + 1) * head)
                query = jnp.where(mine, joint[here, q_at].astype(F32) * SCORE_SCALE, 0.0).astype(BF16)
                slope = jnp.where(mine, slope_all[here, s_at].astype(F32), 0.0).astype(BF16)
                top = lse[p, h : h + 1, here]
                delta = jnp.sum(product[h * head : (h + 1) * head, here], axis=0, keepdims=True)
                key_h = key_t[h * head : (h + 1) * head]
                back = None
                for part in (slice(0, j * rows), here) if j else (here,):
                    scores = dot(joint[part, k_at], query, NT)
                    if part is here:
                        scores = jnp.where(
                            same, scores, jnp.where(earlier, scores + bias[part, :], MASKED)
                        )
                    else:
                        scores = scores + bias[part, :]
                    chances = jnp.exp(scores - top)
                    slopes = dot(joint[part, v_at], slope, NT)
                    grads = (chances * (slopes - delta)).astype(BF16)
                    value_sum[part, :] += dot(chances.astype(BF16), slope)
                    key_sum[part, :] += dot(grads, query)
                    term = dot(key_h[:, part], grads)
                    back = term if back is None else back + term
                query_t[h * head : (h + 1) * head, here] = back * SCORE_SCALE
        grads_out[:, q_at] = query_t[...].T.astype(BF16)
        grads_out[:, k_at] = key_sum[...].astype(BF16)
        grads_out[:, v_at] = value_sum[...].astype(BF16)
    sums[...] = jnp.sum(grads_out[...].astype(F32), axis=0, keepdims=True)
    tile = 256
    for i in range(d // tile):
        here = slice(i * tile, (i + 1) * tile)
        full[here, :] = dot(normed[:, here], grads_out[...], TN).astype(BF16)
    cut = left_keep.shape[1]
    g = lay.size
    side = (spot[1] >> bits_of(lay.planes)) & 1
    cut_rows(full.at[:, 0:cut], side, 2 * g, d // (4 * g), left_keep, left_give)
    side = (spot[1] >> 1) & 1
    cut_rows(full.at[:, cut:], side, g * lay.planes, 2 * lay.each, right_keep, right_give)


def attend_back(lay, spot, bias, joint, wide, lse, normed, slope, cut):
    d, hw, length = lay.width, lay.share, lay.length
    outs = [shaped((length, 3 * hw), BF16)]
    outs += [shaped((d // 2, cut), BF16)] * 2 + [shaped((d // 2, 3 * hw - cut), BF16)] * 2
    outs += [shaped((1, 3 * hw), F32)]
    return kernel_call(
        lay.order,
        functools.partial(attend_back_kernel, lay),
        outs,
        spot,
        bias,
        joint,
        wide,
        lse,
        normed,
        slope,
        name="attend_back",
        smem=(0,),
        scratch=[
            pltpu.VMEM((length, LANES), F32),
            pltpu.VMEM((length, LANES), F32),
            pltpu.VMEM((LANES, length), F32),
            pltpu.VMEM((d, 3 * hw), BF16),
        ],
        vmem=24,
    )


def input_kernel(
    lay, spot, grads, w, x, sums_two, joint_sum, bias_up_sum, keep, give, sums, sums_low
):
    rows, g, hw = lay.rows, lay.size, lay.share
    gain = jnp.zeros((1, lay.width), F32)
    shift = jnp.zeros((1, lay.width), F32)
    for i in range(2 * g):
        here = slice(i * rows, (i + 1) * rows)
        part = dot(grads[here, :], w[...], NT)
        normal, _ = centre(x[here, :].astype(F32))
        gain = gain + jnp.sum(part * normal, axis=0, keepdims=True)
        shift = shift + jnp.sum(part, axis=0, keepdims=True)
        low = part.astype(BF16)
        at = slice((i % g) * rows, (i % g + 1) * rows)

        @pl.when(spot[8] == i // g)
        def _():
            keep[at, :] = low

        @pl.when(spot[8] != i // g)
        def _():
            give[at, :] = low

    sums[...] = jnp.zeros_like(sums)
    sums[0:1, :] = gain
    sums[1:2, :] = shift
    mine = pl.ds(pl.multiple_of(spot[5] * hw, hw), hw)
    sums[2:3, mine] = joint_sum[:, 0:hw]
    sums[3:4, mine] = joint_sum[:, 2 * hw :]
    sums[4:8, :] = sums_two[0:4, :]
    piece = lay.piece

    def write(m):
        for b in range(2 * lay.planes):
            at = up_column(lay, b, m)
            line, column = 8 + at // lay.width, at % lay.width
            sums[line : line + 1, column : column + piece] = bias_up_sum[:, b * piece : (b + 1) * piece]

    for m in range(lay.members):
        pl.when(spot[5] == m)(functools.partial(write, m))
    sums_low[...] = sums[...].astype(BF16)


SUM_ROWS = 16


def up_column(lay, b, member):
    top, plane = b // lay.planes, b % lay.planes
    chip = top * lay.size + member // 2
    return ((chip * lay.planes + plane) * 2 + member % 2) * lay.piece


def sum_rows(width, columns):
    return -(-width // columns) * SUM_ROWS


def put_sums(ref, base, total):
    width, columns = total.shape[1], ref.shape[1]
    for k in range(-(-width // columns)):
        part = total[:, k * columns : min(width, (k + 1) * columns)]
        at = slice(base + k * SUM_ROWS, base + (k + 1) * SUM_ROWS)
        if part.shape[1] < columns:
            ref[at, :] = jnp.zeros((SUM_ROWS, columns), BF16)
        ref[at, 0 : part.shape[1]] = part.astype(BF16)


def take_sums(ref, base, width):
    columns = ref.shape[1]
    parts = []
    for k in range(-(-width // columns)):
        at = slice(base + k * SUM_ROWS, base + (k + 1) * SUM_ROWS)
        parts.append(ref[at, 0 : min(columns, width - k * columns)].astype(F32))
    return parts[0] if len(parts) == 1 else jnp.concatenate(parts, axis=1)


def input_call(lay, spot, grads, w, x, sums_two, joint_sum, bias_up_sum):
    d, rows, g = lay.width, lay.rows, lay.size
    small = (SUM_ROWS, d)
    return kernel_call(
        lay.order,
        functools.partial(input_kernel, lay),
        [shaped((g * rows, d), BF16)] * 2 + [shaped(small, F32), shaped(small, BF16)],
        spot,
        grads,
        w,
        x,
        sums_two,
        joint_sum,
        bias_up_sum,
        name="input_slope",
        smem=(0,),
        vmem=24,
    )


def fold_into(spot, cut, keep, came, hold, give, rows=None):
    slot, shift, a = cut
    count = keep.shape[0]
    b = count // (2 * a)
    side = (spot[slot] >> shift) & 1
    half = a * b

    def write(s):
        for i in range(a):
            for ref, t in ((hold, s), (give, 1 - s)):
                at = slice((2 * i + t) * b, (2 * i + t + 1) * b)
                value = keep[at, :].astype(F32) + came[at, :].astype(F32)
                ref[i * b : (i + 1) * b, :] = value.astype(BF16)

    each_way(side, write)


def two_fold_kernel(cuts, spot, one, one_came, two, two_came, one_keep, one_give, two_keep, two_give):
    fold_into(spot, cuts[0], one, one_came, one_keep, one_give)
    fold_into(spot, cuts[1], two, two_came, two_keep, two_give)


def two_fold(lay, spot, cuts, one, one_came, two, two_came):
    outs = []
    for v in (one, two):
        outs += [shaped((v.shape[0] // 2, v.shape[1]), BF16)] * 2
    return kernel_call(
        lay.order,
        functools.partial(two_fold_kernel, cuts),
        outs,
        spot,
        one,
        one_came,
        two,
        two_came,
        name="two_fold",
        smem=(0,),
    )


def sums_fold_kernel(
    cuts, spot, one, one_came, two, two_came, sums, sums_came, one_keep, one_give, two_keep, two_give, sums_out
):
    n, half, width = one.shape[0], one_keep.shape[0], sums.shape[1]
    if one_came.shape[0] > n:
        came = take_sums(one_came, n, width)
    else:
        came = sums_came[...].astype(F32)
    total = sums[...] + came
    sums_out[...] = total
    fold_into(spot, cuts[0], one, one_came, one_keep, one_give)
    put_sums(one_give, half, total)
    fold_into(spot, cuts[1], two, two_came, two_keep, two_give)


def sums_fold(lay, spot, cuts, one, one_came, two, two_came, sums, sums_came):
    half, other = one.shape[0] // 2, two.shape[0] // 2
    outs = [
        shaped((half, one.shape[1]), BF16),
        shaped((half + sum_rows(sums.shape[1], one.shape[1]), one.shape[1]), BF16),
        shaped((other, two.shape[1]), BF16),
        shaped((other, two.shape[1]), BF16),
        shaped(sums.shape, F32),
    ]
    args = (spot, one, one_came, two, two_came, sums, sums_came)
    return kernel_call(
        lay.order, functools.partial(sums_fold_kernel, cuts), outs, *args, name="sums_fold", smem=(0,)
    )


def top_fold_kernel(shift, spot, one, one_came, two, two_came, sums, keep, give, sums_out):
    n, cut = one.shape
    half = n // 2
    total = sums[...] + take_sums(one_came, n, sums.shape[1])
    sums_out[...] = total
    put_sums(give, half, total)

    def write(s):
        for here, x, y in ((slice(0, cut), one, one_came), (slice(cut, None), two, two_came)):
            for ref, t in ((keep, s), (give, 1 - s)):
                at = slice(t * half, (t + 1) * half)
                value = x[at, :].astype(F32) + y[at, :].astype(F32)
                ref[0:half, here] = value.astype(BF16)

    each_way((spot[0] >> shift) & 1, write)


def top_pair_kernel(shift, spot, one, one_came, two, two_came, one_keep, two_keep, give):
    half = one_keep.shape[0]

    def write(s):
        for i, (x, y, keep) in enumerate(((one, one_came, one_keep), (two, two_came, two_keep))):
            for ref, t in ((keep, s), (give.at[i], 1 - s)):
                at = slice(t * half, (t + 1) * half)
                ref[...] = (x[at, :].astype(F32) + y[at, :].astype(F32)).astype(BF16)

    each_way((spot[0] >> shift) & 1, write)


def home_first_kernel(slot, shift, spot, w_in, w_in_came, w_up, w_up_came, sums, keep, give, sums_out):
    n, cut = w_in.shape
    half = n // 2
    w_up_came = w_up_came.at[0] if len(w_up_came.shape) > len(w_up.shape) else w_up_came
    total = sums[...] + take_sums(w_in_came, n, sums.shape[1])
    sums_out[...] = total
    put_sums(give, half, total)

    def write(s):
        for here, x, y in ((slice(0, cut), w_in, w_in_came), (slice(cut, None), w_up, w_up_came)):
            for ref, t in ((keep, s), (give, 1 - s)):
                at = slice(t * half, (t + 1) * half)
                value = x[at, :].astype(F32) + y[at, :].astype(F32)
                ref[0:half, here] = value.astype(BF16)

    each_way((spot[slot] >> shift) & 1, write)


def home_next_kernel(slot, shift, spot, mine, came, sums, *refs):
    keep, give, sums_out = refs[-3:]
    n, columns = mine.shape
    half = n // 2
    total = sums[...] + take_sums(came, max(n, 16), sums.shape[1])
    sums_out[...] = total
    put_sums(give, max(half, 16), total)

    def write(s):
        for here, x in ((slice(0, columns), mine), (slice(columns, 2 * columns), came)):
            for ref, t in ((keep, s), (give, 1 - s)):
                put_rows(ref, here, x, t * half, half)
        if len(refs) > 3:
            total = (refs[0][...].astype(F32) + refs[1][...].astype(F32)).astype(BF16)
            for ref, t in ((keep, s), (give, 1 - s)):
                put_rows(ref, slice(2 * columns, None), total, t * half, half)

    each_way((spot[slot] >> shift) & 1, write)


def put_rows(ref, columns, source, start, count):
    if count >= 16:
        ref[0:count, columns] = source[start : start + count, :]
        return
    value = source[0:16, :].astype(F32)[start : start + count]
    value = jnp.concatenate([value, jnp.zeros((16 - count, value.shape[1]), F32)], axis=0)
    ref[0:16, columns] = value.astype(BF16)


def home_last_kernel(lay, spot, mine, came, sums, w_in, w_up, w_out, *vectors):
    n = lay.each
    hw, piece, cut = lay.share, lay.piece, 3 * lay.share
    span = cut + lay.ff_share
    for f, ref in enumerate((mine, came)):
        for e in range(lay.size):
            place = 0
            for k in range(bits_of(lay.size)):
                place |= ((e >> k) & 1) << (bits_of(lay.size) - 1 - k)
            member = (spot[4] ^ place) * 2 + (spot[2] ^ f)

            def write(m, ref=ref, e=e):
                for i in range(3):
                    at = i * lay.width + m * hw
                    start = e * span + i * hw
                    w_in[:, at : at + hw] = ref[0 : max(n, 16), start : start + hw].astype(F32)[0:n]
                for b in range(2 * lay.planes):
                    at = up_column(lay, b, m)
                    start = e * span + cut + b * piece
                    value = ref[0 : max(n, 16), start : start + piece].astype(F32)
                    w_up[:, at : at + piece] = value[0:n]

            for m in range(lay.members):
                pl.when(member == m)(functools.partial(write, m))
    half = lay.width // 2

    def write_out(side):
        for ref, s in ((mine, side), (came, 1 - side)):
            at = ref.shape[1] - half
            w_out[:, s * half : (s + 1) * half] = ref[0 : max(n, 16), at:].astype(F32)[0:n]

    each_way(spot[2], write_out)
    total = sums[...] + take_sums(came, max(n, 16), lay.width)

    def part_of(start, count):
        source, target = iota((lay.width, count), 0), iota((lay.width, count), 1)
        move = (source == start + target).astype(F32)
        return jnp.dot(total, move, precision=lax.Precision.HIGHEST)

    own = part_of(spot[7] * n, n)
    for v in range(8):
        vectors[v][...] = own[v : v + 1, :]
    first = spot[7] * piece
    own = part_of(first % lay.width, piece)
    line = iota(own.shape, 0) == 8 + first // lay.width
    vectors[8][...] = jnp.sum(jnp.where(line, own, 0.0), axis=0, keepdims=True)


def add_kernel(one, two, out):
    other = two[1] if len(two.shape) > len(one.shape) else two[...]
    out[...] = (one[...].astype(F32) + other.astype(F32)).astype(out.dtype)


def last_kernel(spot, vecs, keep, came, sent, own, grad_middle, out):
    total = keep[...].astype(F32) + came[...].astype(F32)
    slope = jnp.where(spot[6] == 1, total, sent[...].astype(F32))
    normal, scale = centre(own[...].astype(F32))
    out[...] = (grad_middle[...] + norm_back(slope, normal, scale, vecs[0:1, :])).astype(BF16)


def out_kernel(vecs, middle, keep, came, out):
    total = keep[...].astype(F32) + came[...].astype(F32)
    out[...] = (middle[...] + (total + vecs[7:8, :])).astype(BF16)


def solution(mesh):
    nb, nt = mesh.shape["blk"], mesh.shape["batch"]
    devices = nb * nt
    group_size = nb // 2
    total_bits = bits_of(devices)
    plane_bits = list(range(1, bits_of(nt)))
    group_bits = list(range(bits_of(nt), bits_of(nt) + bits_of(group_size)))
    top_bit = total_bits - 1
    members = 2 * group_size

    def at_home(i):
        return (i // nt) // group_size == i % 2

    def send(value, route):
        return lax.ppermute(value, AXES, route)

    def flip(value, bit, who=None):
        return send(value, [(i, i ^ (1 << bit)) for i in range(devices) if who is None or who(i)])

    def mirror(i):
        return (nb - 1 - i // nt) * nt + i % nt

    def local(
        hidden_in,
        key_mask,
        lengths,
        first_gain,
        first_shift,
        input_weight,
        query_bias,
        value_bias,
        output_weight,
        output_bias,
        second_gain,
        second_shift,
        up_weight,
        up_bias,
        down_weight,
        down_bias,
        cotangent,
    ):
        rows, width = hidden_in.shape[1:]
        length = key_mask.shape[1]
        head = width // HEADS
        blk, lane_id = lax.axis_index("blk"), lax.axis_index("batch")
        index = blk * nt + lane_id
        core = lane_id % 2
        group, place = blk // group_size, blk % group_size
        member = place * 2 + core
        home = group == core
        share = width // members
        ff = up_weight.shape[1]
        piece = ff // devices

        def bit(b):
            return (index >> b) & 1

        def ordered(mine, theirs, side, axis):
            return jnp.where(
                side == 0,
                jnp.concatenate([mine, theirs], axis),
                jnp.concatenate([theirs, mine], axis),
            )

        def side_of(value, side, axis):
            lo, hi = jnp.split(value, 2, axis)
            return jnp.where(side == 0, lo, hi)

        lay = Layout(nb, nt, rows, width, ff, length)
        each = lay.each
        own = hidden_in[0]
        kept_group = jnp.where(home, group, 1 - group)
        kept_place = jnp.where(home, place, group_size - 1 - place)
        spot = jnp.stack(
            [blk, lane_id, core, group, place, member, home.astype(jnp.int32), index]
            + [kept_group, kept_place]
        )
        away = lambda i: not at_home(i)
        across = [(i, mirror(i) ^ 1) for i in range(devices) if away(i)]
        mirrored = [(i, mirror(i)) for i in range(devices)]

        call = functools.partial(kernel_call, lay.order)
        wide_in = 3 * group_size * share + 2 * group_size * lay.planes * piece
        row = lambda value: value.reshape(1, -1)
        vectors = [
            row(v)
            for v in (
                first_gain,
                first_shift,
                query_bias,
                value_bias,
                output_bias,
                second_gain,
                second_shift,
                down_bias,
                up_bias,
            )
        ]

        def spread_group(values, who=None):
            for b in group_bits:
                values = values + [flip(v, b, who) for v in values]
            return values

        act = None
        after = None
        att_c = None
        att_own = None
        b = None
        base = None
        bundle = None
        c = None
        came_w = None
        columns = None
        count = None
        cut = None
        cuts_of = None
        d_bias_up = None
        d_down = None
        d_in = None
        d_out = None
        d_up = None
        dn_came = None
        dn_give = None
        dn_keep = None
        down_blocks = None
        down_c = None
        down_came = None
        down_cuts = None
        down_far = None
        down_far_came = None
        down_give = None
        down_keep = None
        down_m = None
        downs = None
        downs_came = None
        far = None
        far_att = None
        far_came = None
        far_later = None
        final = None
        give = None
        grad_branch = None
        grad_joint = None
        grad_later = None
        grad_low = None
        grad_middle = None
        grad_pre = None
        half = None
        home_outs = None
        home_steps = None
        in_block = None
        in_came = None
        in_give = None
        in_keep = None
        in_pieces = None
        in_sum = None
        input_gradient = None
        joint = None
        joint_sum = None
        k = None
        keep = None
        key_bias = None
        layer_out = None
        left = None
        left_came = None
        left_cuts = None
        left_give = None
        left_keep = None
        lse = None
        middle = None
        near = None
        near_att = None
        next_out = None
        next_planes = None
        normed_one = None
        normed_two = None
        o_came = None
        o_give = None
        o_keep = None
        out_bits = None
        out_blocks = None
        out_came = None
        out_cuts = None
        out_give = None
        out_keep = None
        out_shape = None
        out_steps = None
        outs = None
        outs_c = None
        outs_far = None
        outs_w = None
        pair = None
        pair_came = None
        paired = None
        parts = None
        pieces = None
        planes_down = None
        r = None
        ready = None
        reduce_group = None
        right = None
        right_came = None
        right_cuts = None
        right_give = None
        right_keep = None
        rows_came = None
        sent = None
        shape = None
        shift = None
        slope = None
        slope_give = None
        slope_keep = None
        slot = None
        small = None
        start = None
        step = None
        sums = None
        sums_came = None
        sums_give = None
        sums_two = None
        tall = None
        top_shift = None
        up_blocks = None
        up_came = None
        up_cuts = None
        up_far = None
        up_far_came = None
        up_give = None
        up_keep = None
        up_tall = None
        ups = None
        ups_came = None
        ups_first = None
        valid = None
        vecs = None
        w_came = None
        w_give = None
        w_in = None
        w_keep = None
        w_out = None
        wide = None
        x_all = None
        def do_pack():
            nonlocal base, came_w, downs, downs_came, far, give, half, keep, near, start
            start = [input_weight, up_weight, key_mask, output_weight] + vectors
            half = width // 2
            base = max(each, 16)
            give, keep = call(
                functools.partial(pack_kernel, lay),
                [shaped((base + EXTRA, wide_in + half), BF16)] * 2,
                spot,
                lengths,
                *start,
                name="pack",
                smem=(0, 1),
                away=tuple(range(2, 15)),
                vmem=60,
                scratch=[pltpu.VMEM(v.shape, v.dtype) for v in start] + [pltpu.SemaphoreType.DMA((13,))],
            )
            came_w = flip(give, 0)
            far = [send(own, across)]
            near = spread_group([own])
            downs = down_weight[None]
            downs_came = flip(downs, plane_bits[-1])

        def do_mask():
            nonlocal grad_low
            grad_low = call(
                mask_kernel,
                [shaped((rows, width), BF16)],
                spot,
                lengths,
                cotangent[0],
                name="mask",
                smem=(0, 1),
            )[0]

        def do_trade():
            nonlocal b, came_w, columns, count, give, keep, ready, step, tall, valid
            count = group_size
            for step, b in enumerate(group_bits):
                tall = (2 << step) * each
                columns = wide_in >> (step + 1)
                give, keep, ready = call(
                    functools.partial(trade_kernel, lay, step, count),
                    [shaped((tall + EXTRA, columns + half), BF16)] * 2 + [shaped((8, length), F32)],
                    spot,
                    keep,
                    came_w,
                    name="trade",
                    smem=(0,),
                    scratch=[pltpu.VMEM((tall, 2 * columns + half), BF16)],
                    after=(far[0], *near[1:], downs_came) if step == 0 else (),
                )
                valid = ready if step == 0 else valid
                came_w = flip(give, b)
                count //= 2

        def do_join_down():
            nonlocal b, downs, downs_came
            for b in reversed(plane_bits[:-1]):
                downs = join(lay, downs, downs_came)
                downs_came = flip(downs, b)

        def do_settle():
            nonlocal far, far_later, in_block, pair, paired, tall, up_tall, ups, ups_came, ups_first
            tall = members * each
            paired = ff // members == width
            up_tall = tall + tall * half // (ff // members)
            in_block, ups, far_later, pair = call(
                functools.partial(settle_kernel, lay, len(group_bits)),
                [
                    shaped((tall + EXTRA, 3 * share), BF16),
                    shaped((1, up_tall, ff // members), BF16),
                    shaped(own.shape, BF16),
                    shaped((up_tall + piece, width) if paired else (8, LANES), BF16),
                ],
                spot,
                keep,
                came_w,
                far[0],
                down_weight,
                name="settle",
                smem=(0,),
                scratch=[pltpu.VMEM((tall, 3 * share + ff // members + half), BF16)],
            )
            far = far + spread_group([far_later], away)[1:]
            ups_first = ups
            ups_came = flip(ups, plane_bits[0])

        def do_bundle():
            nonlocal bundle, cut, rows_came
            bundle = call(
                functools.partial(bundle_kernel, group_size),
                [shaped((2 * group_size * rows, width), BF16)],
                spot,
                *near,
                *far,
                name="bundle",
                smem=(0,),
                after=(downs_came,),
            )[0]
            rows_came = flip(bundle, 0)
            cut = max(LANES, 3 * share // 2 // LANES * LANES)

        def do_split():
            nonlocal down_far, down_m, grad_later, left, left_came, pair, pair_came, right, right_came, up_far
            left, right, pair, grad_later = call(
                functools.partial(split_kernel, cut),
                [
                    shaped((2, tall + EXTRA, cut), BF16),
                    shaped((2, tall + EXTRA, 3 * share - cut), BF16),
                    shaped(pair.shape, BF16),
                    shaped(grad_low.shape, BF16),
                ],
                in_block,
                flip(in_block, top_bit),
                pair,
                grad_low,
                name="split",
                after=(ups_came,),
            )
            left_came, right_came = flip(left, plane_bits[0]), flip(right, plane_bits[-1])
            if paired:
                pair_came = flip(pair, top_bit)
            else:
                up_far, down_far = flip(ups_first, top_bit), flip(down_weight, top_bit)[None]
            down_m = [grad_low] + spread_group([grad_later])[1:]

        def do_stack():
            nonlocal after, b, c, k, left, left_came, right, right_came
            for k, (b, c) in list(enumerate(zip(plane_bits, reversed(plane_bits), strict=True)))[1:]:
                after = (rows_came,) if k == 1 else ()
                left, right = stack(lay, left, left_came, right, right_came, *after)
                left_came, right_came = flip(left, b), flip(right, c)

        def do_vectors():
            nonlocal in_pieces, vecs
            in_pieces = (left, left_came, right, right_came)
            vecs = call(
                functools.partial(vector_kernel, lay),
                [shaped((16, width), F32)],
                spot,
                left,
                left_came,
                name="vectors",
                smem=(0,),
                away=(1, 2),
                scratch=[
                    pltpu.VMEM((2 * lay.planes * EXTRA, -(-lay.small // LANES) * LANES), BF16),
                    pltpu.SemaphoreType.DMA((2 * lay.planes,)),
                ],
            )[0]

        def do_join_up():
            nonlocal b, ups, ups_came
            for b in plane_bits[1:]:
                ups = join(lay, ups, ups_came)
                ups_came = flip(ups, b)

        def do_attend():
            nonlocal att_c, far_att, joint, key_bias, lse, near_att, normed_one, w_in, wide, x_all
            key_bias = jnp.where(valid[0] > 0.5, 0.0, MASKED).astype(F32).reshape(length, 1)
            near_att, far_att, joint, wide, lse, normed_one, x_all, w_in = attend(
                lay, spot, key_bias, vecs, near + far + [rows_came], in_pieces
            )
            far_att = [send(far_att, mirrored)]
            near_att = spread_group([near_att])
            att_c = [flip(near_att[0], 0)]

        def do_unpair():
            nonlocal down_far, down_far_came, up_far, up_far_came
            if paired:
                up_far, down_far = call(
                    unpair_kernel,
                    [shaped((1, up_tall, width), BF16), shaped((1, piece, width), BF16)],
                    pair_came,
                    name="unpair",
                    after=(ups_came, *down_m[1:]),
                )
            up_far_came, down_far_came = flip(up_far, plane_bits[0]), flip(down_far, plane_bits[-1])

        def do_rows_own():
            nonlocal out_shape, outs_c, outs_w
            out_shape = [shaped((lay.planes, tall, half), BF16)]
            outs_w = call(out_kernel_rows, out_shape, ups, ups_came, name="out_rows")
            outs_c = flip(outs_w[0], 0)

        def do_stack_far():
            nonlocal b, c, down_far, down_far_came, k, up_far, up_far_came
            for k, (b, c) in list(enumerate(zip(plane_bits, reversed(plane_bits), strict=True)))[1:]:
                up_far, down_far = stack(lay, up_far, up_far_came, down_far, down_far_came, att_c[0])
                up_far_came, down_far_came = flip(up_far, b), flip(down_far, c)

        def do_rows_far():
            nonlocal att_c, down_blocks, down_c, far_att, out_blocks, outs_far, up_blocks
            down_c = [flip(v, 0) for v in down_m]
            far_att = spread_group(far_att)
            att_c = att_c[:1] + [flip(v, 0) for v in near_att[1:] + far_att]
            outs_far = call(out_kernel_rows, out_shape, up_far, up_far_came, name="out_rows", after=(outs_c,))[0]
            out_blocks = (*outs_w, outs_far, outs_c, flip(outs_far, 0))
            up_blocks = (ups, ups_came, up_far, up_far_came)
            down_blocks = (downs, downs_came, down_far, down_far_came)

        def do_forward():
            nonlocal act, att_own, cuts_of, d_bias_up, dn_give, dn_keep, grad_pre, middle, normed_two, planes_down, reduce_group, top_shift, w_out
            (
                dn_keep,
                dn_give,
                middle,
                att_own,
                normed_two,
                act,
                grad_pre,
                d_bias_up,
                w_out,
            ) = forward_call(
                lay,
                spot,
                vecs,
                out_blocks,
                near_att + far_att + att_c + near + down_m + down_c + [rows_came],
                up_blocks + down_blocks,
            )

            def reduce_group(keep, came, slot):
                for k in reversed(range(len(group_bits))):
                    keep, give = fold(lay, spot, slot, k, 1, keep, came)
                    came = flip(give, group_bits[k])
                return keep, came

            planes_down = list(reversed(plane_bits))
            top_shift = bits_of(group_size)

            def cuts_of(lead, order):
                here, cuts = list(planes_down), []
                for b in order:
                    cuts.append((1, b, lead << here.index(b)))
                    here.remove(b)
                return cuts

        def do_fold_norm():
            nonlocal dn_came, dn_keep
            dn_keep, dn_came = reduce_group(dn_keep, flip(dn_give, 0), 4)

        def do_gradients():
            nonlocal down_came, down_give, down_keep, out_came, out_give, out_keep, up_came, up_give, up_keep
            up_keep, up_give, down_keep, down_give, out_keep, out_give = gradient_call(
                lay, spot, normed_two, act, grad_pre, down_m, down_c, down_blocks
            )
            up_came, down_came = flip(up_give, planes_down[0]), flip(down_give, plane_bits[0])
            out_came = flip(out_give, 0)

        def do_turn():
            nonlocal grad_branch, grad_middle, slope_give, slope_keep, sums_two
            slope_keep, slope_give, grad_middle, grad_branch, sums_two = turn_call(
                lay, spot, vecs, dn_keep, dn_came, middle, grad_low, w_out
            )

        def do_pick():
            nonlocal parts, pieces, r
            pieces = call(
                functools.partial(pick_kernel, lay),
                [shaped((rows, share), BF16)] * members,
                spot,
                slope_keep,
                flip(slope_give, 0),
                name="pick",
                smem=(0,),
            )
            parts = [pieces[0]]
            for r in range(1, members):
                parts.append(send(pieces[r], [(i, i ^ (r * nt)) for i in range(devices)]))

        def do_outer():
            nonlocal o_came, o_give, o_keep
            o_keep, o_give = call(
                outer_kernel,
                [shaped((width, width // 2), BF16)] * 2,
                spot,
                att_own,
                grad_branch,
                name="output_gradient",
                smem=(0,),
            )
            o_came = flip(o_give, 0)

        def do_out_fold():
            nonlocal out_came, out_keep
            out_keep, out_came = reduce_group(out_keep, out_came, 4)

        def do_o0():
            nonlocal next_out, o_came, o_keep, out_bits, out_cuts, out_steps
            out_cuts = [(4, k, 2) for k in reversed(range(len(group_bits)))]
            out_cuts += cuts_of(2, planes_down) + [(0, top_shift, 1)]
            out_bits = list(reversed(group_bits)) + planes_down + [top_bit]
            out_steps = iter(range(len(out_bits)))

            def next_out(keep, came, count=1):
                for _ in range(count):
                    k = next(out_steps)
                    keep, give = fold(lay, spot, *out_cuts[k], keep, came)
                    came = flip(give, out_bits[k])
                return keep, came

            o_keep, o_came = next_out(o_keep, o_came)

        def do_assemble():
            nonlocal slope
            slope = call(
                functools.partial(assemble_kernel, lay),
                [shaped((length, share), BF16)],
                spot,
                *parts,
                name="assemble",
                smem=(0,),
            )[0]

        def do_planes():
            nonlocal down_came, down_cuts, down_keep, k, next_planes, up_came, up_cuts, up_keep
            up_cuts, down_cuts = cuts_of(members, planes_down), cuts_of(2, plane_bits)

            def next_planes(k, up_keep, up_came, down_keep, down_came):
                up_keep, up_give, down_keep, down_give = two_fold(
                    lay, spot, (up_cuts[k], down_cuts[k]), up_keep, up_came, down_keep, down_came
                )
                return up_keep, flip(up_give, planes_down[k]), down_keep, flip(down_give, plane_bits[k])

            for k in range(1, len(plane_bits)):
                up_keep, up_came, down_keep, down_came = next_planes(
                    k, up_keep, up_came, down_keep, down_came
                )

        def do_attend_back():
            nonlocal grad_joint, joint_sum, left_came, left_give, left_keep, right_came, right_give, right_keep
            grad_joint, left_keep, left_give, right_keep, right_give, joint_sum = attend_back(
                lay, spot, key_bias, joint, wide, lse, normed_one, slope, cut
            )
            left_came, right_came = flip(left_give, planes_down[0]), flip(right_give, plane_bits[0])

        def do_top_pair():
            nonlocal down_give, down_keep, far_came, give, shape, up_give, up_keep
            if paired:
                shape = (up_keep.shape[0] // 2, up_keep.shape[1])
                up_keep, down_keep, give = call(
                    functools.partial(top_pair_kernel, top_shift),
                    [shaped(shape, BF16), shaped(shape, BF16), shaped((2,) + shape, BF16)],
                    spot,
                    up_keep,
                    up_came,
                    down_keep,
                    down_came,
                    name="top_pair",
                    smem=(0,),
                    after=(o_came,),
                )
                far_came = flip(give, top_bit)
            else:
                up_keep, up_give, down_keep, down_give = two_fold(
                    lay, spot, ((0, top_shift, 1),) * 2, up_keep, up_came, down_keep, down_came
                )
                far_came = (flip(up_give, top_bit), flip(down_give, top_bit))

        def do_input():
            nonlocal in_came, in_give, in_keep, sums, sums_came, sums_give
            in_keep, in_give, sums, sums_give = input_call(
                lay, spot, grad_joint, w_in, x_all, sums_two, joint_sum, d_bias_up
            )
            sums_came = flip(sums_give, planes_down[0])
            in_came = flip(in_give, 0)

        def do_lr():
            nonlocal k, left_came, left_cuts, left_give, left_keep, right_came, right_cuts, right_give, right_keep, sums
            left_cuts, right_cuts = cuts_of(members, planes_down), cuts_of(members, plane_bits)
            for k in range(1, len(plane_bits)):
                left_keep, left_give, right_keep, right_give, sums = sums_fold(
                    lay,
                    spot,
                    (left_cuts[k], right_cuts[k]),
                    left_keep,
                    left_came,
                    right_keep,
                    right_came,
                    sums,
                    sums_came,
                )
                left_came, right_came = flip(left_give, planes_down[k]), flip(right_give, plane_bits[k])

        def do_dn1():
            nonlocal in_came, in_keep
            in_keep, in_came = reduce_group(in_keep, in_came, 9)

        def do_o1():
            nonlocal o_came, o_keep
            o_keep, o_came = next_out(o_keep, o_came, len(group_bits))

        def do_layer():
            nonlocal layer_out
            layer_out = call(
                out_kernel,
                [shaped((rows, width), BF16)],
                vecs,
                middle,
                out_keep,
                out_came,
                name="layer_out",
            )[0]

        def do_top():
            nonlocal small, sums, tall, w_came, w_give, w_keep
            small = (SUM_ROWS, width)
            tall = left_keep.shape[0] // 2
            w_keep, w_give, sums = call(
                functools.partial(top_fold_kernel, top_shift),
                [
                    shaped((tall, 3 * share), BF16),
                    shaped((tall + sum_rows(width, 3 * share), 3 * share), BF16),
                    shaped(small, F32),
                ],
                spot,
                left_keep,
                left_came,
                right_keep,
                right_came,
                sums,
                name="top_fold",
                smem=(0,),
            )
            w_came = flip(w_give, top_bit)

        def do_add():
            nonlocal in_sum, sent
            in_sum = call(add_kernel, [shaped((rows, width), BF16)], in_keep, in_came, name="add")[0]
            sent = send(in_sum, across)

        def do_o2():
            nonlocal o_came, o_keep
            o_keep, o_came = next_out(o_keep, o_came, len(plane_bits) - 1)

        def do_d_down():
            nonlocal d_down
            d_down = call(
                add_kernel,
                [shaped((piece, width), F32)],
                down_keep,
                far_came if paired else far_came[1],
                name="add",
            )[0]

        def do_home0():
            nonlocal columns, down_came, home_outs, home_steps, sums, tall, up_came, w_came, w_give, w_keep
            up_came, down_came = (far_came, far_came) if paired else far_came
            columns = 3 * share + ff // members
            home_steps = [(4, k, b) for k, b in reversed(list(enumerate(group_bits)))] + [(2, 0, 0)]

            def home_outs():
                rows_here = max(tall, 16)
                return [
                    shaped((rows_here, columns), BF16),
                    shaped((rows_here + sum_rows(width, columns), columns), BF16),
                    shaped(small, F32),
                ]

            tall //= 2
            w_keep, w_give, sums = call(
                functools.partial(home_first_kernel, *home_steps[0][:2]),
                home_outs(),
                spot,
                w_keep,
                w_came,
                up_keep,
                up_came,
                sums,
                name="home_first",
                smem=(0,),
            )
            w_came = flip(w_give, home_steps[0][2])

        def do_o3():
            nonlocal o_came, o_keep
            o_keep, o_came = next_out(o_keep, o_came)

        def do_last():
            nonlocal input_gradient
            input_gradient = call(
                last_kernel,
                [shaped((rows, width), BF16)],
                spot,
                vecs,
                in_keep,
                in_came,
                sent,
                own,
                grad_middle,
                name="input_gradient",
                smem=(0,),
            )[0]

        def do_home1():
            nonlocal b, columns, final, outs, shift, slot, sums, tall, w_came, w_give, w_keep
            for slot, shift, b in home_steps[1:]:
                tall //= 2
                columns *= 2
                outs = home_outs()
                final = (o_keep, o_came) if b == 0 else ()
                if final:
                    outs = [shaped((v.shape[0], columns + width // 2), BF16) for v in outs[:2]] + outs[2:]
                w_keep, w_give, sums = call(
                    functools.partial(home_next_kernel, slot, shift),
                    outs,
                    spot,
                    w_keep,
                    w_came,
                    sums,
                    *final,
                    name="home_next",
                    smem=(0,),
                )
                w_came = flip(w_give, b)

        def do_home_last():
            nonlocal d_in, d_out, d_up, vectors
            d_in, d_up, d_out, *vectors = call(
                functools.partial(home_last_kernel, lay),
                [shaped((each, 3 * width), F32), shaped((each, ff), F32), shaped((each, width), F32)]
                + [shaped((1, each), F32)] * 8
                + [shaped((1, piece), F32)],
                spot,
                w_keep,
                w_came,
                sums,
                name="home_last",
                smem=(0,),
            )
            vectors = [v.reshape(-1) for v in vectors]

        def do_relay():
            nonlocal far_att
            far_att = call(
                copy_kernel, [shaped(far_att[0].shape, BF16)], far_att[0], name="relay", after=tuple(near_att[1:])
            )

        steps = {
            "pack": do_pack,
            "mask": do_mask,
            "trade": do_trade,
            "join_down": do_join_down,
            "settle": do_settle,
            "bundle": do_bundle,
            "split": do_split,
            "stack": do_stack,
            "vectors": do_vectors,
            "join_up": do_join_up,
            "attend": do_attend,
            "unpair": do_unpair,
            "rows_own": do_rows_own,
            "stack_far": do_stack_far,
            "rows_far": do_rows_far,
            "forward": do_forward,
            "fold_norm": do_fold_norm,
            "gradients": do_gradients,
            "turn": do_turn,
            "pick": do_pick,
            "outer": do_outer,
            "out_fold": do_out_fold,
            "o0": do_o0,
            "assemble": do_assemble,
            "planes": do_planes,
            "attend_back": do_attend_back,
            "top_pair": do_top_pair,
            "input": do_input,
            "lr": do_lr,
            "dn1": do_dn1,
            "o1": do_o1,
            "layer": do_layer,
            "top": do_top,
            "add": do_add,
            "o2": do_o2,
            "d_down": do_d_down,
            "home0": do_home0,
            "o3": do_o3,
            "last": do_last,
            "home1": do_home1,
            "home_last": do_home_last,
            "relay": do_relay,
        }
        for name in PLAN:
            lay.order.step = name
            known = {
                "near": near,
                "far": far,
                "downs_came": downs_came,
                "ups_came": ups_came,
                "rows_came": rows_came,
                "pair_came": pair_came,
                "down_m": down_m,
                "down_c": down_c,
                "near_att": near_att,
                "far_att": far_att,
                "att_c": att_c,
                "outs_c": outs_c,
                "up_far_came": up_far_came,
                "down_far_came": down_far_came,
                "up_came": up_came,
                "down_came": down_came,
                "out_came": out_came,
                "o_came": o_came,
                "far_came": far_came,
                "sums_came": sums_came,
                "in_came": in_came,
            }
            lay.order.waits = tuple(
                v for w in WAITS.get(name, ()) for v in jax.tree.leaves(known[w])
            )
            steps[name]()
        return (
            layer_out[None],
            input_gradient[None],
            vectors[0],
            vectors[1],
            d_in,
            vectors[2],
            vectors[3],
            d_out,
            vectors[4],
            vectors[5],
            vectors[6],
            d_up,
            vectors[8],
            d_down,
            vectors[7],
        )

    vector, matrix = P(AXES), P(AXES, None)
    tokens = P("batch", "blk", None)
    return jax.shard_map(
        local,
        mesh=mesh,
        in_specs=(
            tokens,
            P("batch", None),
            P("batch"),
            vector,
            vector,
            matrix,
            vector,
            vector,
            matrix,
            vector,
            vector,
            vector,
            matrix,
            vector,
            matrix,
            vector,
            tokens,
        ),
        out_specs=(
            tokens,
            tokens,
            vector,
            vector,
            matrix,
            vector,
            vector,
            matrix,
            vector,
            vector,
            vector,
            matrix,
            vector,
            matrix,
            vector,
        ),
        check_vma=False,
    )
```

```python
import functools

import jax
import jax.numpy as jnp
from jax import lax
from jax.experimental import pallas as pl
from jax.experimental.pallas import tpu as pltpu
from jax.sharding import PartitionSpec as P

HEADS = 16
EPSILON = 1e-05
SCORE_SCALE = 0.125
MASKED = -1e30
LANES = 128
AXES = ("blk", "batch")
F32 = jnp.float32
BF16 = jnp.bfloat16

NT = (((1,), (1,)), ((), ()))
NN = (((1,), (0,)), ((), ()))
TN = (((0,), (0,)), ((), ()))


def dot(a, b, dims=NN):
    return lax.dot_general(a, b, dims, preferred_element_type=F32)


def bits_of(size):
    return size.bit_length() - 1


def key_mask_terms(rows):
    key = lax.broadcasted_iota(jnp.int32, (rows, rows), 0)
    query = lax.broadcasted_iota(jnp.int32, (rows, rows), 1)
    return key < query, key == query


def centre(values):
    average = jnp.mean(values, axis=-1, keepdims=True)
    centred = values - average
    variance = jnp.mean(centred * centred, axis=-1, keepdims=True)
    scale = lax.rsqrt(variance + EPSILON)
    return centred * scale, scale


def norm_back(slope, normal, scale, gain):
    weighted = slope * gain
    return scale * (
        weighted
        - jnp.mean(weighted, axis=-1, keepdims=True)
        - normal * jnp.mean(weighted * normal, axis=-1, keepdims=True)
    )


GELU_A = 0.7978845608028654
GELU_B = 0.044715


def gelu_terms(pre):
    square = pre * pre
    bend = jnp.tanh(GELU_A * pre * (1.0 + GELU_B * square))
    half = 0.5 * (1.0 + bend)
    slope = half + 0.5 * pre * (1.0 - bend * bend) * (GELU_A * (1.0 + 3.0 * GELU_B * square))
    return pre * half, slope


EXTRA = 16


WEIGHTS = {'pack': 10000000000, 'unpair': 10000000000, 'trade': 1, 'join_down': 1, 'mask': 1}
FREE = {'trade': [0]}
WAITS = {'stack_far': ['down_c'], 'pick': ['ups_came'], 'd_down': ['down_came']}
GRANTS = {'o2': 32}
HEAVY = 10**11
PLAN = (
    "pack",
    "mask",
    "trade",
    "join_down",
    "settle",
    "bundle",
    "split",
    "stack",
    "vectors",
    "join_up",
    "attend",
    "unpair",
    "stack_far",
    "relay",
    "rows_own",
    "rows_far",
    "forward",
    "fold_norm",
    "gradients",
    "turn",
    "outer",
    "pick",
    "o0",
    "out_fold",
    "assemble",
    "planes",
    "attend_back",
    "top_pair",
    "input",
    "lr",
    "dn1",
    "o1",
    "top",
    "o2",
    "add",
    "d_down",
    "home0",
    "layer",
    "o3",
    "last",
    "home1",
    "home_last",
)


def shaped(shape, kind):
    return jax.ShapeDtypeStruct(shape, kind)


class Order:
    def __init__(self):
        self.ticket = ()
        self.step = ""
        self.waits = ()


def kernel_call(order, body, outs, *args, name, smem=(), away=(), scratch=(), vmem=8, after=()):
    weight = WEIGHTS.get(order.step, HEAVY)
    after = tuple(v for i, v in enumerate(after) if i not in FREE.get(order.step, ()))
    after, order.waits = after + order.waits, ()
    count, given, held = len(args), len(outs), len(order.ticket)
    inner = body

    def body(*refs):
        ins, rest = refs[:count], refs[count + len(after) :]
        before, rest = rest[:held], rest[held:]
        results, ticket = rest[:given], rest[given]
        ticket[...] = before[0][...] if held else jnp.zeros_like(ticket)
        inner(*ins, *results, *rest[given + 1 :])

    away = tuple(away) + tuple(range(count, count + len(after)))
    args = args + tuple(after) + order.ticket
    outs = list(outs) + [shaped((8, LANES), F32)]

    def spec(i, places):
        if i in places:
            return pl.BlockSpec(memory_space=pl.ANY)
        return pl.BlockSpec(memory_space=pltpu.VMEM)

    ins = [
        pl.BlockSpec(memory_space=pltpu.SMEM) if i in smem else spec(i, away)
        for i in range(len(args))
    ]
    moved = sum(v.size * v.dtype.itemsize for v in args + tuple(outs))
    *results, ticket = pl.pallas_call(
        body,
        in_specs=ins,
        out_specs=[spec(i, ()) for i in range(len(outs))],
        out_shape=list(outs),
        scratch_shapes=list(scratch),
        compiler_params=pltpu.CompilerParams(vmem_limit_bytes=GRANTS.get(order.step, vmem) * 2**20),
        cost_estimate=pl.CostEstimate(flops=weight, bytes_accessed=1, transcendentals=0),
        name=name,
    )(*args)
    order.ticket = (ticket,)
    return results


def iota(shape, dim):
    return lax.broadcasted_iota(jnp.int32, shape, dim)


class Layout:
    def __init__(self, nb, nt, rows, width, ff, length):
        self.nb, self.nt, self.rows, self.width, self.ff, self.length = nb, nt, rows, width, ff, length
        self.devices = nb * nt
        self.size = nb // 2
        self.planes = nt // 2
        self.members = 2 * self.size
        self.each = width // self.devices
        self.piece = ff // self.devices
        self.share = width // self.members
        self.ff_share = ff // self.members
        self.small = 8 * self.each + self.piece
        self.valid_at = -(-self.small // 512) * 512
        self.head = width // HEADS
        self.order = Order()


def each_way(flag, write):
    pl.when(flag == 0)(lambda: write(0))
    pl.when(flag == 1)(lambda: write(1))


def write_half(lay, side, count, in_from, up_from, in_start, up_start, give, keep, n):
    hw, pc = lay.share, lay.piece
    tail = lay.planes * pc if count > 0 else pc
    spans = []
    if count == 0:
        for q in range(3 * lay.size):
            spans.append((in_from, in_start + 2 * q * hw, hw))
        for q in range(2 * lay.size * lay.planes):
            spans.append((up_from, up_start + 2 * q * pc, pc))
    else:
        for q in range(3 * count // 2):
            spans.append((in_from, in_start + 2 * q * hw, hw))
        for q in range(count):
            spans.append((up_from, up_start + 2 * q * tail, tail))
    at = 0
    for source, start, span in spans:
        mine = source[0:n, start + side * span : start + (side + 1) * span]
        other = source[0:n, start + (1 - side) * span : start + (2 - side) * span]
        keep[0:n, at : at + span] = mine
        give[0:n, at : at + span] = other
        at += span


def load_all(pairs, sems):
    copies = [pltpu.make_async_copy(a, b, sems.at[i]) for i, (a, b) in enumerate(pairs)]
    for copy in copies:
        copy.start()
    return copies


def wait_all(copies):
    for copy in copies:
        copy.wait()


def pack_kernel(lay, spot, lengths, *refs):
    sources, (give, keep), targets, sems = refs[:13], refs[13:15], refs[15:28], refs[28]
    wait_all(load_all(list(zip(sources, targets, strict=True)), sems))
    w_in, w_up, mask, w_out = targets[:4]
    smalls = targets[4:]
    n = lay.each
    base = max(n, 16)
    if base > n:
        for ref in (give, keep):
            ref[0:base, :] = jnp.zeros((base, ref.shape[1]), BF16)
    each_way(spot[2], lambda side: write_half(lay, side, 0, w_in, w_up, 0, 0, give, keep, n))
    half = lay.width // 2
    last = give.shape[1] - half

    def write_out(side):
        keep[0:n, last:] = w_out[:, side * half : (side + 1) * half]
        give[0:n, last:] = w_out[:, (1 - side) * half : (2 - side) * half]

    each_way(spot[2], write_out)
    line = jnp.zeros((1, lay.small), F32)
    at = 0
    for ref in smalls:
        span = ref.shape[1]
        where = iota((span, lay.small), 1) == iota((span, lay.small), 0) + at
        line = line + dot(ref[...], where.astype(F32).astype(BF16))
        at += span
    row = iota((EXTRA, lay.small), 0) == spot[5]
    extra = jnp.where(row, line, 0.0).astype(BF16)
    live = (mask[...] > 0) & (iota(mask.shape, 1) < lengths[0])
    valid = jnp.where(live, 1.0, 0.0) * jnp.ones((EXTRA, 1), F32)
    for ref in (give, keep):
        ref[base : base + EXTRA, :] = jnp.zeros((EXTRA, ref.shape[1]), BF16)
        ref[base : base + EXTRA, 0 : lay.small] = extra
        ref[base : base + EXTRA, lay.valid_at : lay.valid_at + lay.length] = valid.astype(BF16)


def merge_rows(keep, came, side, n, out):
    if n < 16:
        mine, theirs = keep[0:16, :].astype(F32)[0:n], came[0:16, :].astype(F32)[0:n]
        first = jnp.where(side == 0, mine, theirs)
        second = jnp.where(side == 0, theirs, mine)
        out[...] = jnp.concatenate([first, second], axis=0).astype(BF16)
        return
    out[pl.ds(pl.multiple_of(side * n, n), n), :] = keep[0:n, :]
    out[pl.ds(pl.multiple_of((1 - side) * n, n), n), :] = came[0:n, :]


def merge_extra(lay, keep, came, n):
    n = max(n, 16)
    total = keep[n : n + EXTRA, 0 : lay.small].astype(F32) + came[n : n + EXTRA, 0 : lay.small].astype(F32)
    return total.astype(BF16)


def trade_kernel(lay, step, count, spot, keep, came, give, hold, valid, both):
    n = (1 << step) * lay.each
    merge_rows(keep, came, spot[2] if step == 0 else (spot[4] >> (step - 1)) & 1, n, both)
    start = 3 * count * lay.share
    each_way(
        (spot[4] >> step) & 1,
        lambda side: write_half(lay, side, count, both, both, 0, start, give, hold, 2 * n),
    )
    half = lay.width // 2
    for ref in (give, hold):
        ref[0 : 2 * n, ref.shape[1] - half :] = both[:, both.shape[1] - half :]
    extra = merge_extra(lay, keep, came, n)
    for ref in (give, hold):
        ref[2 * n : 2 * n + EXTRA, :] = jnp.zeros((EXTRA, ref.shape[1]), BF16)
        ref[2 * n : 2 * n + EXTRA, 0 : lay.small] = extra
    if step == 0:
        place = slice(lay.valid_at, lay.valid_at + lay.length)
        base = max(n, 16)
        mine, theirs = (ref[base : base + 16, place].astype(F32)[0:8] for ref in (keep, came))
        valid[...] = jnp.where(spot[6] == 1, mine, theirs)
    else:
        valid[...] = jnp.zeros_like(valid)


def settle_kernel(
    lay, step, spot, keep, came, far, down, in_block, up_block, far_out, pair, both
):
    far_out[...] = far[...]
    n = (1 << step) * lay.each
    merge_rows(keep, came, (spot[4] >> (step - 1)) & 1, n, both)
    cut = 3 * lay.share
    in_block[0 : 2 * n, :] = both[:, 0:cut]
    last = cut + lay.ff_share
    tall, half = 2 * n, lay.width // 2
    chunks = lay.ff_share // half
    part = tall // chunks
    targets = [up_block.at[0]] + ([pair] if pair.shape[0] > 8 else [])
    for ref in targets:
        ref[0:tall, :] = both[:, cut:last]
        for i in range(chunks):
            rows = both[i * part : (i + 1) * part, last:]
            ref[tall : tall + part, i * half : (i + 1) * half] = rows
    if pair.shape[0] > 8:
        pair[tall + part :, :] = down[...]
    in_block[2 * n : 2 * n + EXTRA, :] = jnp.zeros((EXTRA, cut), BF16)
    in_block[2 * n : 2 * n + EXTRA, 0 : lay.small] = merge_extra(lay, keep, came, n)


def split_kernel(cut, mine, came, pair, grad, left, right, pair_out, grad_out):
    pair_out[...] = pair[...]
    grad_out[...] = grad[...]
    left[0], left[1] = mine[:, 0:cut], came[:, 0:cut]
    right[0], right[1] = mine[:, cut:], came[:, cut:]


def stack_kernel(one, one_came, two, two_came, one_out, two_out):
    n = one.shape[0]
    one_out[0:n], one_out[n : 2 * n] = one[...], one_came[...]
    two_out[0:n], two_out[n : 2 * n] = two[...], two_came[...]


def stack(lay, one, one_came, two, two_came, *after):
    outs = [shaped((2 * v.shape[0],) + v.shape[1:], BF16) for v in (one, two)]
    return kernel_call(
        lay.order, stack_kernel, outs, one, one_came, two, two_came, name="stack", after=after
    )


def unpair_kernel(pair, up, down):
    n = up.shape[1]
    up[0], down[0] = pair[0:n, :], pair[n:, :]


def bundle_kernel(g, spot, *refs):
    near, far, out = refs[:g], refs[g : 2 * g], refs[2 * g]
    rows = near[0].shape[0]

    def write(home):
        parts = list(near) if home else list(far) + list(near)
        for i, ref in enumerate(parts):
            out[i * rows : (i + 1) * rows, :] = ref[...]

    each_way(spot[6], write)


def copy_kernel(value, out):
    out[...] = value[...]


def out_kernel_rows(mine, came, out):
    count, tall, half = out.shape
    chunks = mine.shape[2] // half
    part = tall // chunks
    for k in range(count):
        source = (mine if k < count // 2 else came).at[k % (count // 2)]
        for i in range(chunks):
            rows = source[tall : tall + part, i * half : (i + 1) * half]
            out[k, i * part : (i + 1) * part, :] = rows


def join_kernel(one, one_came, out):
    n = one.shape[0]
    out[0:n], out[n : 2 * n] = one[...], one_came[...]


def join(lay, one, one_came, *after):
    out = shaped((2 * one.shape[0],) + one.shape[1:], BF16)
    return kernel_call(lay.order, join_kernel, [out], one, one_came, name="join", after=after)[0]


def block_spot(lay, spot, k, flipped):
    bits = bits_of(lay.planes)
    top = (spot[3] ^ k) & 1
    order = range(bits - 1, -1, -1) if flipped else range(bits)
    plane = spot[1] >> 1
    for position, b in enumerate(order):
        plane = plane ^ (((k >> (position + 1)) & 1) << b)
    return top, plane


def vector_kernel(lay, spot, first, second, out, rows, sems):
    n, count, wide = lay.members * lay.each, 2 * lay.planes, rows.shape[1]
    copies = []
    for k in range(count):
        source = first if k < count // 2 else second
        copy = pltpu.make_async_copy(
            source.at[k % (count // 2), n : n + EXTRA, 0:wide],
            rows.at[k * EXTRA : (k + 1) * EXTRA, :],
            sems.at[k],
        )
        copy.start()
        copies.append(copy)
    for copy in copies:
        copy.wait()
    out[...] = jnp.zeros_like(out)
    tall = count * EXTRA
    line, lane = iota((tall, lay.width), 0), iota((tall, lay.width), 1)
    holder, block = jnp.zeros_like(line), jnp.zeros_like(line)
    for k in range(count):
        top, plane = block_spot(lay, spot, k, False)
        inside = line - k * EXTRA
        here = (inside >= 0) & (inside < EXTRA)
        lead = (top * lay.size + inside // 2) * lay.nt + plane * 2 + inside % 2
        holder = jnp.where(here, jnp.where(inside < lay.members, lead, -1), holder)
        block = jnp.where(here & (inside == spot[5]), top * lay.planes + plane, jnp.where(here, -1, block))
    values = rows[...]
    source, target = iota((wide, lay.width), 0), iota((wide, lay.width), 1)
    for v in range(8):
        spread = (source == v * lay.each + target % lay.each).astype(F32).astype(BF16)
        tiled = jnp.where(lane // lay.each == holder, dot(values, spread), 0.0)
        out[v : v + 1, :] = jnp.sum(tiled, axis=0, keepdims=True)
    spread = (source == 8 * lay.each + target % lay.piece).astype(F32).astype(BF16)
    tiled = jnp.where(lane // lay.piece == block, dot(values, spread), 0.0)
    out[8:9, :] = jnp.sum(tiled, axis=0, keepdims=True)
    hw = lay.share
    mine = pl.ds(pl.multiple_of(spot[5] * hw, hw), hw)
    out[9:10, 0:hw] = out[2:3, mine]
    out[9:10, 2 * hw : 3 * hw] = out[3:4, mine]


def attend_kernel(lay, spot, bias, vecs, *refs):
    g, rows, hw, length, head = lay.size, lay.rows, lay.share, lay.length, lay.head
    near, far, came = refs[:g], refs[g : 2 * g], refs[2 * g]
    near_c = far_c = [came.at[e * rows : (e + 1) * rows, :] for e in range(g)]
    weights = refs[2 * g + 1 : 2 * g + 5]
    near_att, far_att, joint, wide, lse, normed, x, w, x_sems, w_sems = refs[2 * g + 5 :]
    group, place = spot[3], spot[4]
    pending = []
    for e in range(g):
        for side, (at_home, at_away) in enumerate(((near[e], near_c[e]), (far_c[e], far[e]))):
            spot_here = (place if side == 0 else g - 1 - place) ^ e
            spot_here = (group if side == 0 else 1 - group) * g + spot_here
            target = x.at[pl.ds(pl.multiple_of(spot_here * rows, rows), rows), :]
            sem = x_sems.at[side * g + e]
            home = pltpu.make_async_copy(at_home, target, sem)
            visit = pltpu.make_async_copy(at_away, target, sem)
            pl.when(spot[6] == 1)(home.start)
            pl.when(spot[6] == 0)(visit.start)
            pending.append(home)
    count = 2 * lay.planes
    span = 2 * lay.each
    cut = weights[0].shape[-1]
    loads = []
    for k in range(count):
        for side in range(2):
            source = weights[2 * side + (k >= count // 2)]
            top, plane = block_spot(lay, spot, k, side == 1)
            for q in range(g):
                start = ((top * g + q) * lay.planes + plane) * span
                copy = pltpu.make_async_copy(
                    source.at[k % (count // 2), q * span : (q + 1) * span, :],
                    w.at[pl.ds(pl.multiple_of(start, span), span), 0:cut]
                    if side == 0
                    else w.at[pl.ds(pl.multiple_of(start, span), span), cut:],
                    w_sems.at[(k * 2 + side) * g + q],
                )
                copy.start()
                loads.append(copy)
    for copy in pending:
        copy.wait()
    for j in range(length // rows):
        here = slice(j * rows, (j + 1) * rows)
        normal, _ = centre(x[here, :].astype(F32))
        normed[here, :] = (normal * vecs[0:1, :] + vecs[1:2, :]).astype(BF16)
    for copy in loads:
        copy.wait()
    for j in range(length // rows):
        here = slice(j * rows, (j + 1) * rows)
        joint[here, :] = (dot(normed[here, :], w[...]) + vecs[9:10, 0 : 3 * hw]).astype(BF16)
    earlier, same = key_mask_terms(rows)
    lane = iota((rows, LANES), 1)
    for p in range(hw // LANES):
        q_at, k_at, v_at = (slice(i * hw + p * LANES, i * hw + (p + 1) * LANES) for i in range(3))
        value_t = joint[:, v_at].astype(F32).T.astype(BF16)
        for j in range(length // rows):
            here, past = slice(j * rows, (j + 1) * rows), slice(0, j * rows)
            bias_here = bias[here, :]
            for h in range(LANES // head):
                mine = (lane >= h * head) & (lane < (h + 1) * head)
                query = jnp.where(mine, joint[here, q_at].astype(F32) * SCORE_SCALE, 0.0).astype(BF16)
                inner = dot(joint[here, k_at], query, NT)
                inner = jnp.where(same, inner, jnp.where(earlier, inner + bias_here, MASKED))
                top = jnp.max(inner, axis=0, keepdims=True)
                if j:
                    outer = dot(joint[past, k_at], query, NT) + bias[past, :]
                    top = jnp.maximum(top, jnp.max(outer, axis=0, keepdims=True))
                inner = jnp.exp(inner - top)
                total = jnp.sum(inner, axis=0, keepdims=True)
                if j:
                    outer = jnp.exp(outer - top)
                    total = total + jnp.sum(outer, axis=0, keepdims=True)
                share = 1.0 / total
                value_h = value_t[h * head : (h + 1) * head]
                out = dot(value_h[:, here], (inner * share).astype(BF16))
                if j:
                    out = out + dot(value_h[:, past], (outer * share).astype(BF16))
                at = p * LANES + h * head
                wide[at : at + head, here] = out
                lse[p, h : h + 1, here] = top + jnp.log(total)
    for i in range(g):
        here = slice(i * rows, (i + 1) * rows)
        for out_ref, first in ((near_att, group * g + i), (far_att, (1 - group) * g + i)):
            part = wide[:, pl.ds(pl.multiple_of(first * rows, rows), rows)]
            out_ref[here, :] = part.T.astype(BF16)


def attend(lay, spot, bias, vecs, hidden, weights):
    d, hw, length, g = lay.width, lay.share, lay.length, lay.size
    outs = [
        shaped((g * lay.rows, hw), BF16),
        shaped((g * lay.rows, hw), BF16),
        shaped((length, 3 * hw), BF16),
        shaped((hw, length), F32),
        shaped((hw // LANES, 8, length), F32),
        shaped((length, d), BF16),
        shaped((length, d), BF16),
        shaped((d, 3 * hw), BF16),
    ]
    copies = 2 * lay.planes * 2 * g
    args = (spot, bias, vecs) + tuple(hidden) + tuple(weights)
    return kernel_call(
        lay.order,
        functools.partial(attend_kernel, lay),
        outs,
        *args,
        name="attend",
        smem=(0,),
        away=tuple(range(3, len(args))),
        scratch=[
            pltpu.SemaphoreType.DMA((2 * g,)),
            pltpu.SemaphoreType.DMA((copies,)),
        ],
        vmem=24,
    )


def fold_kernel(slot, shift, a, b, spot, keep, came, hold, give):
    total = keep[...].astype(F32) + came[...].astype(F32)
    side = (spot[slot] >> shift) & 1
    view = total.reshape(a, 2, b, total.shape[-1])

    def write(s):
        hold[...] = view[:, s].reshape(a * b, -1).astype(BF16)
        give[...] = view[:, 1 - s].reshape(a * b, -1).astype(BF16)

    each_way(side, write)


def fold(lay, spot, slot, shift, a, keep, came):
    count, columns = keep.shape
    b = count // (2 * a)
    return kernel_call(
        lay.order,
        functools.partial(fold_kernel, slot, shift, a, b),
        [shaped((a * b, columns), BF16)] * 2,
        spot,
        keep,
        came,
        name="fold",
        smem=(0,),
    )


def mask_kernel(spot, lengths, cotangent, out):
    rows = out.shape[0]
    live = spot[0] * rows + iota((rows, 1), 0) < lengths[0]
    out[...] = jnp.where(live, cotangent[...].astype(F32), 0.0).astype(BF16)


def place_rows(lay, spot, e):
    return spot[4] ^ e


def block_of(lay, blocks, k):
    mine, came = blocks[2 * (k & 1)], blocks[2 * (k & 1) + 1]
    half = lay.planes // 2
    return (mine if k >> 1 < half else came).at[(k >> 1) % half]


def up_loads(lay, spot, blocks, w_up):
    pairs = []
    span, g = 2 * lay.each, lay.size
    for k in range(2 * lay.planes):
        source = block_of(lay, blocks, k)
        top, plane = block_spot(lay, spot, k, False)
        for q in range(g):
            start = ((top * g + q) * lay.planes + plane) * span
            pairs.append(
                (
                    source.at[q * span : (q + 1) * span, :],
                    w_up.at[pl.ds(pl.multiple_of(start, span), span), :],
                )
            )
    return pairs


def down_loads(lay, spot, blocks, w_down):
    pairs = []
    for k in range(2 * lay.planes):
        top, plane = block_spot(lay, spot, k, True)
        start = (top * lay.planes + plane) * lay.piece
        target = w_down.at[pl.ds(pl.multiple_of(start, lay.piece), lay.piece), :]
        pairs.append((block_of(lay, blocks, k), target))
    return pairs


def row_loads(lay, spot, mine, swapped, target):
    pairs = []
    g, rows = lay.size, lay.rows
    for e in range(g):
        for source, sequence in ((mine[e], spot[2]), (swapped[e], 1 - spot[2])):
            start = (sequence * g + (spot[4] ^ e)) * rows
            pairs.append((source, target.at[pl.ds(pl.multiple_of(start, rows), rows), :]))
    return pairs


def out_loads(lay, spot, blocks, target):
    pairs = []
    half, span, g = lay.width // 2, 2 * lay.each, lay.size
    for i, block in enumerate(blocks):
        column = pl.multiple_of((spot[2] ^ (i // 2)) * half, half)
        for k in range(lay.planes):
            top, plane = block_spot(lay, spot, 2 * k + i % 2, False)
            for q in range(g):
                row = pl.multiple_of(((top * g + q) * lay.planes + plane) * span, span)
                source = block.at[k, q * span : (q + 1) * span, :]
                pairs.append((source, target.at[pl.ds(row, span), pl.ds(column, half)]))
    return pairs


def forward_kernel(lay, spot, vecs, *refs):
    outs, refs = refs[:4], refs[4:]
    g, rows, hw, d = lay.size, lay.rows, lay.share, lay.width
    lists = [refs[i * g : (i + 1) * g] for i in range(7)]
    near, far, near_c, far_c, base_m, down_m, down_c = lists
    refs = refs[7 * g :]
    bundle, ups, downs = refs[0], refs[1:5], refs[5:9]
    (
        dn_keep,
        dn_give,
        middle_own,
        att_own,
        normed,
        act,
        grad_pre,
        bias_sum,
        wo,
        att,
        base,
        gd,
        w_up,
        w_down,
        sems,
    ) = refs[9:]
    core, group, place = spot[2], spot[3], spot[4]
    span = g * rows
    pairs = out_loads(lay, spot, outs, wo)
    for e in range(g):
        for source, sequence, at, side in (
            (near[e], group, place ^ e, core),
            (near_c[e], group, place ^ e, 1 - core),
            (far[e], 1 - group, (g - 1 - place) ^ e, core),
            (far_c[e], 1 - group, (g - 1 - place) ^ e, 1 - core),
        ):
            row = pl.multiple_of(sequence * span, span)
            column = pl.multiple_of((at * 2 + side) * hw, hw)
            pairs.append((source, att.at[pl.ds(row, span), pl.ds(column, hw)]))
    first_row = jnp.where(spot[6] == 1, span, 0)
    base_c = [
        bundle.at[pl.ds(pl.multiple_of(first_row + e * rows, rows), rows), :] for e in range(g)
    ]
    pairs += row_loads(lay, spot, base_m, base_c, base)
    first = len(pairs)
    pairs += up_loads(lay, spot, ups, w_up) + down_loads(lay, spot, downs, w_down)
    pairs += row_loads(lay, spot, down_m, down_c, gd)
    copies = [pltpu.make_async_copy(a, b, sems.at[i]) for i, (a, b) in enumerate(pairs)]
    for copy in copies[:first]:
        copy.start()
    wait_all(copies[:first])
    for copy in copies[first:]:
        copy.start()
    bias_out, gain, shift = vecs[4:5, :], vecs[5:6, :], vecs[6:7, :]
    bias_up = vecs[8:9, 0 : lay.ff_share]
    total = jnp.zeros((1, lay.ff_share), F32)
    for i in range(2 * g):
        here = slice(i * rows, (i + 1) * rows)
        middle = base[here, :].astype(F32) + (dot(att[here, :], wo[...]) + bias_out)
        normal, _ = centre(middle)
        normed[here, :] = (normal * gain + shift).astype(BF16)

        @pl.when((core == i // g) & (place == i % g))
        def _():
            middle_own[...] = middle
            att_own[...] = att[here, :]

    wait_all(copies[first:])
    for i in range(2 * g):
        here = slice(i * rows, (i + 1) * rows)
        pre = dot(normed[here, :], w_up[...]) + bias_up
        value, slope = gelu_terms(pre)
        act[here, :] = value.astype(BF16)
        grad = (dot(gd[here, :], w_down[...], NT) * slope).astype(BF16)
        grad_pre[here, :] = grad
        total = total + jnp.sum(grad.astype(F32), axis=0, keepdims=True)
        back = dot(grad, w_up[...], NT).astype(BF16)
        at = slice((i % g) * rows, (i % g + 1) * rows)

        @pl.when(core == i // g)
        def _():
            dn_keep[at, :] = back

        @pl.when(core != i // g)
        def _():
            dn_give[at, :] = back

    bias_sum[...] = total


def forward_call(lay, spot, vecs, outs_w, lists, blocks):
    d, f, rows, g = lay.width, lay.ff_share, lay.rows, lay.size
    tokens = 2 * g * rows
    outs = [
        shaped((g * rows, d), BF16),
        shaped((g * rows, d), BF16),
        shaped((rows, d), F32),
        shaped((rows, d), BF16),
        shaped((tokens, d), BF16),
        shaped((tokens, f), BF16),
        shaped((tokens, f), BF16),
        shaped((1, f), F32),
        shaped((d, d), BF16),
    ]
    args = (spot, vecs) + tuple(outs_w) + tuple(lists) + tuple(blocks)
    copies = 4 * lay.planes * g + 8 * g + 2 * lay.planes * (g + 1)
    return kernel_call(
        lay.order,
        functools.partial(forward_kernel, lay),
        outs,
        *args,
        name="feed_forward",
        smem=(0,),
        away=tuple(range(2, len(args))),
        scratch=[
            pltpu.VMEM((tokens, d), BF16),
            pltpu.VMEM((tokens, d), BF16),
            pltpu.VMEM((tokens, d), BF16),
            pltpu.VMEM((d, f), BF16),
            pltpu.VMEM((f, d), BF16),
            pltpu.SemaphoreType.DMA((copies,)),
        ],
        vmem=24,
    )


def cut_rows(value, side, a, b, keep, give):
    for i in range(a):
        for ref, s in ((keep, side), (give, 1 - side)):
            start = pl.multiple_of((2 * i + s) * b, b)
            ref[i * b : (i + 1) * b, :] = value[pl.ds(start, b), :]


def gradient_kernel(lay, spot, normed, act, grad_pre, *refs):
    g, rows, d, f = lay.size, lay.rows, lay.width, lay.ff_share
    down_m, down_c, blocks = refs[:g], refs[g : 2 * g], refs[2 * g : 2 * g + 4]
    up_keep, up_give, down_keep, down_give, out_keep, out_give, gd, w_down, full, sems = refs[
        2 * g + 4 :
    ]
    pairs = row_loads(lay, spot, down_m, down_c, gd)
    pairs += down_loads(lay, spot, blocks, w_down)
    copies = load_all(pairs, sems)
    tile = 256
    for i in range(d // tile):
        here = slice(i * tile, (i + 1) * tile)
        full[here, 0:f] = dot(normed[:, here], grad_pre[...], TN).astype(BF16)
    plane_bits = bits_of(lay.planes)
    side = (spot[1] >> plane_bits) & 1
    cut_rows(full.at[0:d, 0:f], side, 2 * g, d // (4 * g), up_keep, up_give)
    wait_all(copies)
    tile = min(256, f)
    for i in range(f // tile):
        here = slice(i * tile, (i + 1) * tile)
        full[here, 0:d] = dot(act[:, here], gd[...], TN).astype(BF16)
    side = (spot[1] >> 1) & 1
    cut_rows(full.at[0:f, 0:d], side, lay.planes, lay.piece, down_keep, down_give)
    for i in range(2 * g):
        here = slice(i * rows, (i + 1) * rows)
        at = slice((i % g) * rows, (i % g + 1) * rows)
        part = dot(act[here, :], w_down[...]).astype(BF16)

        @pl.when(spot[2] == i // g)
        def _():
            out_keep[at, :] = part

        @pl.when(spot[2] != i // g)
        def _():
            out_give[at, :] = part


def gradient_call(lay, spot, normed, act, grad_pre, down_m, down_c, blocks):
    d, f, rows, g = lay.width, lay.ff_share, lay.rows, lay.size
    tokens = 2 * g * rows
    outs = [shaped((d // 2, f), BF16)] * 2 + [shaped((f // 2, d), BF16)] * 2
    outs += [shaped((g * rows, d), BF16)] * 2
    args = (spot, normed, act, grad_pre) + tuple(down_m) + tuple(down_c) + tuple(blocks)
    return kernel_call(
        lay.order,
        functools.partial(gradient_kernel, lay),
        outs,
        *args,
        name="gradients",
        smem=(0,),
        away=tuple(range(4, len(args))),
        scratch=[
            pltpu.VMEM((tokens, d), BF16),
            pltpu.VMEM((f, d), BF16),
            pltpu.VMEM((d, d), BF16),
            pltpu.SemaphoreType.DMA((2 * g + 2 * lay.planes,)),
        ],
        vmem=24,
    )


def turn_kernel(lay, spot, vecs, keep, came, middle, grad_low, w_out, *refs):
    keep_out, give_out, grad_middle, grad_branch, sums, wo, att_grad, sems = refs
    copies = load_all([(w_out, wo)], sems)
    normal, scale = centre(middle[...])
    slope = keep[...].astype(F32) + came[...].astype(F32)
    total = grad_low[...].astype(F32) + norm_back(slope, normal, scale, vecs[5:6, :])
    grad_middle[...] = total
    branch = total.astype(BF16)
    grad_branch[...] = branch
    sums[...] = jnp.zeros_like(sums)
    add = lambda value: jnp.sum(value, axis=0, keepdims=True)
    sums[0:1, :] = add(branch.astype(F32))
    sums[1:2, :] = add(slope * normal)
    sums[2:3, :] = add(slope)
    sums[3:4, :] = add(grad_low[...].astype(F32))
    wait_all(copies)
    att_grad[...] = dot(branch, wo[...], NT).astype(BF16)
    hw = lay.share
    for i in range(lay.size):
        for ref, side in ((keep_out, spot[2]), (give_out, 1 - spot[2])):
            start = pl.multiple_of((2 * i + side) * hw, hw)
            ref[:, i * hw : (i + 1) * hw] = att_grad[:, pl.ds(start, hw)]


def outer_kernel(spot, att, branch, keep, give):
    tile, half = 256, keep.shape[1]

    def write(side):
        for i in range(keep.shape[0] // tile):
            here = slice(i * tile, (i + 1) * tile)
            value = dot(att[:, here], branch[...], TN).astype(BF16)
            keep[here, :] = value[:, side * half : (side + 1) * half]
            give[here, :] = value[:, (1 - side) * half : (2 - side) * half]

    each_way(spot[2], write)


def pick_kernel(lay, spot, mine, came, *pieces):
    hw = lay.share
    for r in range(lay.members):
        chip = spot[0] ^ r
        column = pl.ds(pl.multiple_of(chip % lay.size * hw, hw), hw)
        own = chip // lay.size == spot[2]

        @pl.when(own)
        def _(r=r, column=column):
            pieces[r][...] = mine[:, column]

        @pl.when(jnp.logical_not(own))
        def _(r=r, column=column):
            pieces[r][...] = came[:, column]


def turn_call(lay, spot, vecs, keep, came, middle, grad_low, w_out):
    d, rows = lay.width, lay.rows
    outs = [shaped((rows, d // 2), BF16)] * 2
    outs += [shaped((rows, d), F32), shaped((rows, d), BF16), shaped((8, d), F32)]
    return kernel_call(
        lay.order,
        functools.partial(turn_kernel, lay),
        outs,
        spot,
        vecs,
        keep,
        came,
        middle,
        grad_low,
        w_out,
        name="turn",
        smem=(0,),
        away=(6,),
        scratch=[
            pltpu.VMEM((d, d), BF16),
            pltpu.VMEM((rows, d), BF16),
            pltpu.SemaphoreType.DMA((1,)),
        ],
        vmem=24,
    )


def assemble_kernel(lay, spot, *refs):
    out = refs[-1]
    for r in range(lay.members):
        start = pl.multiple_of((spot[0] ^ r) * lay.rows, lay.rows)
        out[pl.ds(start, lay.rows), :] = refs[r][...]


def attend_back_kernel(lay, spot, bias, joint, wide, lse, normed, slope_all, *refs):
    rows, hw, length, head, d = lay.rows, lay.share, lay.length, lay.head, lay.width
    (
        grads_out,
        left_keep,
        left_give,
        right_keep,
        right_give,
        sums,
        key_sum,
        value_sum,
        query_t,
        full,
    ) = refs
    earlier, same = key_mask_terms(rows)
    lane = iota((rows, LANES), 1)
    for p in range(hw // LANES):
        q_at, k_at, v_at = (slice(i * hw + p * LANES, i * hw + (p + 1) * LANES) for i in range(3))
        s_at = slice(p * LANES, (p + 1) * LANES)
        key_t = joint[:, k_at].astype(F32).T.astype(BF16)
        product = slope_all[:, s_at].astype(F32).T * wide[s_at, :]
        key_sum[...] = jnp.zeros_like(key_sum)
        value_sum[...] = jnp.zeros_like(value_sum)
        for j in range(length // rows):
            here = slice(j * rows, (j + 1) * rows)
            for h in range(LANES // head):
                mine = (lane >= h * head) & (lane < (h + 1) * head)
                query = jnp.where(mine, joint[here, q_at].astype(F32) * SCORE_SCALE, 0.0).astype(BF16)
                slope = jnp.where(mine, slope_all[here, s_at].astype(F32), 0.0).astype(BF16)
                top = lse[p, h : h + 1, here]
                delta = jnp.sum(product[h * head : (h + 1) * head, here], axis=0, keepdims=True)
                key_h = key_t[h * head : (h + 1) * head]
                back = None
                for part in (slice(0, j * rows), here) if j else (here,):
                    scores = dot(joint[part, k_at], query, NT)
                    if part is here:
                        scores = jnp.where(
                            same, scores, jnp.where(earlier, scores + bias[part, :], MASKED)
                        )
                    else:
                        scores = scores + bias[part, :]
                    chances = jnp.exp(scores - top)
                    slopes = dot(joint[part, v_at], slope, NT)
                    grads = (chances * (slopes - delta)).astype(BF16)
                    value_sum[part, :] += dot(chances.astype(BF16), slope)
                    key_sum[part, :] += dot(grads, query)
                    term = dot(key_h[:, part], grads)
                    back = term if back is None else back + term
                query_t[h * head : (h + 1) * head, here] = back * SCORE_SCALE
        grads_out[:, q_at] = query_t[...].T.astype(BF16)
        grads_out[:, k_at] = key_sum[...].astype(BF16)
        grads_out[:, v_at] = value_sum[...].astype(BF16)
    sums[...] = jnp.sum(grads_out[...].astype(F32), axis=0, keepdims=True)
    tile = 256
    for i in range(d // tile):
        here = slice(i * tile, (i + 1) * tile)
        full[here, :] = dot(normed[:, here], grads_out[...], TN).astype(BF16)
    cut = left_keep.shape[1]
    g = lay.size
    side = (spot[1] >> bits_of(lay.planes)) & 1
    cut_rows(full.at[:, 0:cut], side, 2 * g, d // (4 * g), left_keep, left_give)
    side = (spot[1] >> 1) & 1
    cut_rows(full.at[:, cut:], side, g * lay.planes, 2 * lay.each, right_keep, right_give)


def attend_back(lay, spot, bias, joint, wide, lse, normed, slope, cut):
    d, hw, length = lay.width, lay.share, lay.length
    outs = [shaped((length, 3 * hw), BF16)]
    outs += [shaped((d // 2, cut), BF16)] * 2 + [shaped((d // 2, 3 * hw - cut), BF16)] * 2
    outs += [shaped((1, 3 * hw), F32)]
    return kernel_call(
        lay.order,
        functools.partial(attend_back_kernel, lay),
        outs,
        spot,
        bias,
        joint,
        wide,
        lse,
        normed,
        slope,
        name="attend_back",
        smem=(0,),
        scratch=[
            pltpu.VMEM((length, LANES), F32),
            pltpu.VMEM((length, LANES), F32),
            pltpu.VMEM((LANES, length), F32),
            pltpu.VMEM((d, 3 * hw), BF16),
        ],
        vmem=24,
    )


def input_kernel(
    lay, spot, grads, w, x, sums_two, joint_sum, bias_up_sum, keep, give, sums, sums_low
):
    rows, g, hw = lay.rows, lay.size, lay.share
    gain = jnp.zeros((1, lay.width), F32)
    shift = jnp.zeros((1, lay.width), F32)
    for i in range(2 * g):
        here = slice(i * rows, (i + 1) * rows)
        part = dot(grads[here, :], w[...], NT)
        normal, _ = centre(x[here, :].astype(F32))
        gain = gain + jnp.sum(part * normal, axis=0, keepdims=True)
        shift = shift + jnp.sum(part, axis=0, keepdims=True)
        low = part.astype(BF16)
        at = slice((i % g) * rows, (i % g + 1) * rows)

        @pl.when(spot[8] == i // g)
        def _():
            keep[at, :] = low

        @pl.when(spot[8] != i // g)
        def _():
            give[at, :] = low

    sums[...] = jnp.zeros_like(sums)
    sums[0:1, :] = gain
    sums[1:2, :] = shift
    mine = pl.ds(pl.multiple_of(spot[5] * hw, hw), hw)
    sums[2:3, mine] = joint_sum[:, 0:hw]
    sums[3:4, mine] = joint_sum[:, 2 * hw :]
    sums[4:8, :] = sums_two[0:4, :]
    piece = lay.piece

    def write(m):
        for b in range(2 * lay.planes):
            at = up_column(lay, b, m)
            line, column = 8 + at // lay.width, at % lay.width
            sums[line : line + 1, column : column + piece] = bias_up_sum[:, b * piece : (b + 1) * piece]

    for m in range(lay.members):
        pl.when(spot[5] == m)(functools.partial(write, m))
    sums_low[...] = sums[...].astype(BF16)


SUM_ROWS = 16


def up_column(lay, b, member):
    top, plane = b // lay.planes, b % lay.planes
    chip = top * lay.size + member // 2
    return ((chip * lay.planes + plane) * 2 + member % 2) * lay.piece


def sum_rows(width, columns):
    return -(-width // columns) * SUM_ROWS


def put_sums(ref, base, total):
    width, columns = total.shape[1], ref.shape[1]
    for k in range(-(-width // columns)):
        part = total[:, k * columns : min(width, (k + 1) * columns)]
        at = slice(base + k * SUM_ROWS, base + (k + 1) * SUM_ROWS)
        if part.shape[1] < columns:
            ref[at, :] = jnp.zeros((SUM_ROWS, columns), BF16)
        ref[at, 0 : part.shape[1]] = part.astype(BF16)


def take_sums(ref, base, width):
    columns = ref.shape[1]
    parts = []
    for k in range(-(-width // columns)):
        at = slice(base + k * SUM_ROWS, base + (k + 1) * SUM_ROWS)
        parts.append(ref[at, 0 : min(columns, width - k * columns)].astype(F32))
    return parts[0] if len(parts) == 1 else jnp.concatenate(parts, axis=1)


def input_call(lay, spot, grads, w, x, sums_two, joint_sum, bias_up_sum):
    d, rows, g = lay.width, lay.rows, lay.size
    small = (SUM_ROWS, d)
    return kernel_call(
        lay.order,
        functools.partial(input_kernel, lay),
        [shaped((g * rows, d), BF16)] * 2 + [shaped(small, F32), shaped(small, BF16)],
        spot,
        grads,
        w,
        x,
        sums_two,
        joint_sum,
        bias_up_sum,
        name="input_slope",
        smem=(0,),
        vmem=24,
    )


def fold_into(spot, cut, keep, came, hold, give, rows=None):
    slot, shift, a = cut
    count = keep.shape[0]
    b = count // (2 * a)
    side = (spot[slot] >> shift) & 1
    half = a * b

    def write(s):
        for i in range(a):
            for ref, t in ((hold, s), (give, 1 - s)):
                at = slice((2 * i + t) * b, (2 * i + t + 1) * b)
                value = keep[at, :].astype(F32) + came[at, :].astype(F32)
                ref[i * b : (i + 1) * b, :] = value.astype(BF16)

    each_way(side, write)


def two_fold_kernel(cuts, spot, one, one_came, two, two_came, one_keep, one_give, two_keep, two_give):
    fold_into(spot, cuts[0], one, one_came, one_keep, one_give)
    fold_into(spot, cuts[1], two, two_came, two_keep, two_give)


def two_fold(lay, spot, cuts, one, one_came, two, two_came):
    outs = []
    for v in (one, two):
        outs += [shaped((v.shape[0] // 2, v.shape[1]), BF16)] * 2
    return kernel_call(
        lay.order,
        functools.partial(two_fold_kernel, cuts),
        outs,
        spot,
        one,
        one_came,
        two,
        two_came,
        name="two_fold",
        smem=(0,),
    )


def sums_fold_kernel(
    cuts, spot, one, one_came, two, two_came, sums, sums_came, one_keep, one_give, two_keep, two_give, sums_out
):
    n, half, width = one.shape[0], one_keep.shape[0], sums.shape[1]
    if one_came.shape[0] > n:
        came = take_sums(one_came, n, width)
    else:
        came = sums_came[...].astype(F32)
    total = sums[...] + came
    sums_out[...] = total
    fold_into(spot, cuts[0], one, one_came, one_keep, one_give)
    put_sums(one_give, half, total)
    fold_into(spot, cuts[1], two, two_came, two_keep, two_give)


def sums_fold(lay, spot, cuts, one, one_came, two, two_came, sums, sums_came):
    half, other = one.shape[0] // 2, two.shape[0] // 2
    outs = [
        shaped((half, one.shape[1]), BF16),
        shaped((half + sum_rows(sums.shape[1], one.shape[1]), one.shape[1]), BF16),
        shaped((other, two.shape[1]), BF16),
        shaped((other, two.shape[1]), BF16),
        shaped(sums.shape, F32),
    ]
    args = (spot, one, one_came, two, two_came, sums, sums_came)
    return kernel_call(
        lay.order, functools.partial(sums_fold_kernel, cuts), outs, *args, name="sums_fold", smem=(0,)
    )


def top_fold_kernel(shift, spot, one, one_came, two, two_came, sums, keep, give, sums_out):
    n, cut = one.shape
    half = n // 2
    total = sums[...] + take_sums(one_came, n, sums.shape[1])
    sums_out[...] = total
    put_sums(give, half, total)

    def write(s):
        for here, x, y in ((slice(0, cut), one, one_came), (slice(cut, None), two, two_came)):
            for ref, t in ((keep, s), (give, 1 - s)):
                at = slice(t * half, (t + 1) * half)
                value = x[at, :].astype(F32) + y[at, :].astype(F32)
                ref[0:half, here] = value.astype(BF16)

    each_way((spot[0] >> shift) & 1, write)


def top_pair_kernel(shift, spot, one, one_came, two, two_came, one_keep, two_keep, give):
    half = one_keep.shape[0]

    def write(s):
        for i, (x, y, keep) in enumerate(((one, one_came, one_keep), (two, two_came, two_keep))):
            for ref, t in ((keep, s), (give.at[i], 1 - s)):
                at = slice(t * half, (t + 1) * half)
                ref[...] = (x[at, :].astype(F32) + y[at, :].astype(F32)).astype(BF16)

    each_way((spot[0] >> shift) & 1, write)


def home_first_kernel(slot, shift, spot, w_in, w_in_came, w_up, w_up_came, sums, keep, give, sums_out):
    n, cut = w_in.shape
    half = n // 2
    w_up_came = w_up_came.at[0] if len(w_up_came.shape) > len(w_up.shape) else w_up_came
    total = sums[...] + take_sums(w_in_came, n, sums.shape[1])
    sums_out[...] = total
    put_sums(give, half, total)

    def write(s):
        for here, x, y in ((slice(0, cut), w_in, w_in_came), (slice(cut, None), w_up, w_up_came)):
            for ref, t in ((keep, s), (give, 1 - s)):
                at = slice(t * half, (t + 1) * half)
                value = x[at, :].astype(F32) + y[at, :].astype(F32)
                ref[0:half, here] = value.astype(BF16)

    each_way((spot[slot] >> shift) & 1, write)


def home_next_kernel(slot, shift, spot, mine, came, sums, *refs):
    keep, give, sums_out = refs[-3:]
    n, columns = mine.shape
    half = n // 2
    total = sums[...] + take_sums(came, max(n, 16), sums.shape[1])
    sums_out[...] = total
    put_sums(give, max(half, 16), total)

    def write(s):
        for here, x in ((slice(0, columns), mine), (slice(columns, 2 * columns), came)):
            for ref, t in ((keep, s), (give, 1 - s)):
                put_rows(ref, here, x, t * half, half)
        if len(refs) > 3:
            total = (refs[0][...].astype(F32) + refs[1][...].astype(F32)).astype(BF16)
            for ref, t in ((keep, s), (give, 1 - s)):
                put_rows(ref, slice(2 * columns, None), total, t * half, half)

    each_way((spot[slot] >> shift) & 1, write)


def put_rows(ref, columns, source, start, count):
    if count >= 16:
        ref[0:count, columns] = source[start : start + count, :]
        return
    value = source[0:16, :].astype(F32)[start : start + count]
    value = jnp.concatenate([value, jnp.zeros((16 - count, value.shape[1]), F32)], axis=0)
    ref[0:16, columns] = value.astype(BF16)


def home_last_kernel(lay, spot, mine, came, sums, w_in, w_up, w_out, *refs):
    n = lay.each
    hw, piece, cut = lay.share, lay.piece, 3 * lay.share
    span = cut + lay.ff_share
    for f, ref in enumerate((mine, came)):
        for e in range(lay.size):
            place = 0
            for k in range(bits_of(lay.size)):
                place |= ((e >> k) & 1) << (bits_of(lay.size) - 1 - k)
            member = (spot[4] ^ place) * 2 + (spot[2] ^ f)

            def write(m, ref=ref, e=e):
                for i in range(3):
                    at = i * lay.width + m * hw
                    start = e * span + i * hw
                    w_in[:, at : at + hw] = ref[0 : max(n, 16), start : start + hw].astype(F32)[0:n]
                for b in range(2 * lay.planes):
                    at = up_column(lay, b, m)
                    start = e * span + cut + b * piece
                    value = ref[0 : max(n, 16), start : start + piece].astype(F32)
                    w_up[:, at : at + piece] = value[0:n]

            for m in range(lay.members):
                pl.when(member == m)(functools.partial(write, m))
    half = lay.width // 2

    def write_out(side):
        for ref, s in ((mine, side), (came, 1 - side)):
            at = ref.shape[1] - half
            w_out[:, s * half : (s + 1) * half] = ref[0 : max(n, 16), at:].astype(F32)[0:n]

    each_way(spot[2], write_out)
    vectors, held = refs[:9], refs[9]
    held[...] = sums[...] + take_sums(came, max(n, 16), lay.width)

    def part_of(start, count):
        block = held[:, pl.ds(pl.multiple_of(start // LANES * LANES, LANES), LANES)]
        part = jnp.zeros((SUM_ROWS, count), F32)
        for i in range(LANES // count):
            here = start % LANES == i * count
            part = part + jnp.where(here, block[:, i * count : (i + 1) * count], 0.0)
        return part

    own = part_of(spot[7] * n, n)
    for v in range(8):
        vectors[v][...] = own[v : v + 1, :]
    first = spot[7] * piece
    own = part_of(first % lay.width, piece)
    line = iota(own.shape, 0) == 8 + first // lay.width
    vectors[8][...] = jnp.sum(jnp.where(line, own, 0.0), axis=0, keepdims=True)


def add_kernel(one, two, out):
    other = two[1] if len(two.shape) > len(one.shape) else two[...]
    out[...] = (one[...].astype(F32) + other.astype(F32)).astype(out.dtype)


def last_kernel(spot, vecs, keep, came, sent, own, grad_middle, out):
    total = keep[...].astype(F32) + came[...].astype(F32)
    slope = jnp.where(spot[6] == 1, total, sent[...].astype(F32))
    normal, scale = centre(own[...].astype(F32))
    out[...] = (grad_middle[...] + norm_back(slope, normal, scale, vecs[0:1, :])).astype(BF16)


def out_kernel(vecs, middle, keep, came, out):
    total = keep[...].astype(F32) + came[...].astype(F32)
    out[...] = (middle[...] + (total + vecs[7:8, :])).astype(BF16)


def solution(mesh):
    nb, nt = mesh.shape["blk"], mesh.shape["batch"]
    devices = nb * nt
    group_size = nb // 2
    total_bits = bits_of(devices)
    plane_bits = list(range(1, bits_of(nt)))
    group_bits = list(range(bits_of(nt), bits_of(nt) + bits_of(group_size)))
    top_bit = total_bits - 1
    members = 2 * group_size

    def at_home(i):
        return (i // nt) // group_size == i % 2

    def send(value, route):
        return lax.ppermute(value, AXES, route)

    def flip(value, bit, who=None):
        return send(value, [(i, i ^ (1 << bit)) for i in range(devices) if who is None or who(i)])

    def mirror(i):
        return (nb - 1 - i // nt) * nt + i % nt

    def local(
        hidden_in,
        key_mask,
        lengths,
        first_gain,
        first_shift,
        input_weight,
        query_bias,
        value_bias,
        output_weight,
        output_bias,
        second_gain,
        second_shift,
        up_weight,
        up_bias,
        down_weight,
        down_bias,
        cotangent,
    ):
        rows, width = hidden_in.shape[1:]
        length = key_mask.shape[1]
        head = width // HEADS
        blk, lane_id = lax.axis_index("blk"), lax.axis_index("batch")
        index = blk * nt + lane_id
        core = lane_id % 2
        group, place = blk // group_size, blk % group_size
        member = place * 2 + core
        home = group == core
        share = width // members
        ff = up_weight.shape[1]
        piece = ff // devices

        def bit(b):
            return (index >> b) & 1

        def ordered(mine, theirs, side, axis):
            return jnp.where(
                side == 0,
                jnp.concatenate([mine, theirs], axis),
                jnp.concatenate([theirs, mine], axis),
            )

        def side_of(value, side, axis):
            lo, hi = jnp.split(value, 2, axis)
            return jnp.where(side == 0, lo, hi)

        lay = Layout(nb, nt, rows, width, ff, length)
        each = lay.each
        own = hidden_in[0]
        kept_group = jnp.where(home, group, 1 - group)
        kept_place = jnp.where(home, place, group_size - 1 - place)
        spot = jnp.stack(
            [blk, lane_id, core, group, place, member, home.astype(jnp.int32), index]
            + [kept_group, kept_place]
        )
        away = lambda i: not at_home(i)
        across = [(i, mirror(i) ^ 1) for i in range(devices) if away(i)]
        mirrored = [(i, mirror(i)) for i in range(devices)]

        call = functools.partial(kernel_call, lay.order)
        wide_in = 3 * group_size * share + 2 * group_size * lay.planes * piece
        row = lambda value: value.reshape(1, -1)
        vectors = [
            row(v)
            for v in (
                first_gain,
                first_shift,
                query_bias,
                value_bias,
                output_bias,
                second_gain,
                second_shift,
                down_bias,
                up_bias,
            )
        ]

        def spread_group(values, who=None):
            for b in group_bits:
                values = values + [flip(v, b, who) for v in values]
            return values

        act = None
        after = None
        att_c = None
        att_own = None
        b = None
        base = None
        bundle = None
        c = None
        came_w = None
        columns = None
        count = None
        cut = None
        cuts_of = None
        d_bias_up = None
        d_down = None
        d_in = None
        d_out = None
        d_up = None
        dn_came = None
        dn_give = None
        dn_keep = None
        down_blocks = None
        down_c = None
        down_came = None
        down_cuts = None
        down_far = None
        down_far_came = None
        down_give = None
        down_keep = None
        down_m = None
        downs = None
        downs_came = None
        far = None
        far_att = None
        far_came = None
        far_later = None
        final = None
        give = None
        grad_branch = None
        grad_joint = None
        grad_later = None
        grad_low = None
        grad_middle = None
        grad_pre = None
        half = None
        home_outs = None
        home_steps = None
        in_block = None
        in_came = None
        in_give = None
        in_keep = None
        in_pieces = None
        in_sum = None
        input_gradient = None
        joint = None
        joint_sum = None
        k = None
        keep = None
        key_bias = None
        layer_out = None
        left = None
        left_came = None
        left_cuts = None
        left_give = None
        left_keep = None
        lse = None
        middle = None
        near = None
        near_att = None
        next_out = None
        next_planes = None
        normed_one = None
        normed_two = None
        o_came = None
        o_give = None
        o_keep = None
        out_bits = None
        out_blocks = None
        out_came = None
        out_cuts = None
        out_give = None
        out_keep = None
        out_shape = None
        out_steps = None
        outs = None
        outs_c = None
        outs_far = None
        outs_w = None
        pair = None
        pair_came = None
        paired = None
        parts = None
        pieces = None
        planes_down = None
        r = None
        ready = None
        reduce_group = None
        right = None
        right_came = None
        right_cuts = None
        right_give = None
        right_keep = None
        rows_came = None
        sent = None
        shape = None
        shift = None
        slope = None
        slope_give = None
        slope_keep = None
        slot = None
        small = None
        start = None
        step = None
        sums = None
        sums_came = None
        sums_give = None
        sums_two = None
        tall = None
        top_shift = None
        up_blocks = None
        up_came = None
        up_cuts = None
        up_far = None
        up_far_came = None
        up_give = None
        up_keep = None
        up_tall = None
        ups = None
        ups_came = None
        ups_first = None
        valid = None
        vecs = None
        w_came = None
        w_give = None
        w_in = None
        w_keep = None
        w_out = None
        wide = None
        x_all = None
        def do_pack():
            nonlocal base, came_w, downs, downs_came, far, give, half, keep, near, start
            start = [input_weight, up_weight, key_mask, output_weight] + vectors
            half = width // 2
            base = max(each, 16)
            give, keep = call(
                functools.partial(pack_kernel, lay),
                [shaped((base + EXTRA, wide_in + half), BF16)] * 2,
                spot,
                lengths,
                *start,
                name="pack",
                smem=(0, 1),
                away=tuple(range(2, 15)),
                vmem=60,
                scratch=[pltpu.VMEM(v.shape, v.dtype) for v in start] + [pltpu.SemaphoreType.DMA((13,))],
            )
            came_w = flip(give, 0)
            far = [send(own, across)]
            near = spread_group([own])
            downs = down_weight[None]
            downs_came = flip(downs, plane_bits[-1])

        def do_mask():
            nonlocal grad_low
            grad_low = call(
                mask_kernel,
                [shaped((rows, width), BF16)],
                spot,
                lengths,
                cotangent[0],
                name="mask",
                smem=(0, 1),
            )[0]

        def do_trade():
            nonlocal b, came_w, columns, count, give, keep, ready, step, tall, valid
            count = group_size
            for step, b in enumerate(group_bits):
                tall = (2 << step) * each
                columns = wide_in >> (step + 1)
                give, keep, ready = call(
                    functools.partial(trade_kernel, lay, step, count),
                    [shaped((tall + EXTRA, columns + half), BF16)] * 2 + [shaped((8, length), F32)],
                    spot,
                    keep,
                    came_w,
                    name="trade",
                    smem=(0,),
                    scratch=[pltpu.VMEM((tall, 2 * columns + half), BF16)],
                    after=(far[0], *near[1:], downs_came) if step == 0 else (),
                )
                valid = ready if step == 0 else valid
                came_w = flip(give, b)
                count //= 2

        def do_join_down():
            nonlocal b, downs, downs_came
            for b in reversed(plane_bits[:-1]):
                downs = join(lay, downs, downs_came)
                downs_came = flip(downs, b)

        def do_settle():
            nonlocal far, far_later, in_block, pair, paired, tall, up_tall, ups, ups_came, ups_first
            tall = members * each
            paired = ff // members == width
            up_tall = tall + tall * half // (ff // members)
            in_block, ups, far_later, pair = call(
                functools.partial(settle_kernel, lay, len(group_bits)),
                [
                    shaped((tall + EXTRA, 3 * share), BF16),
                    shaped((1, up_tall, ff // members), BF16),
                    shaped(own.shape, BF16),
                    shaped((up_tall + piece, width) if paired else (8, LANES), BF16),
                ],
                spot,
                keep,
                came_w,
                far[0],
                down_weight,
                name="settle",
                smem=(0,),
                scratch=[pltpu.VMEM((tall, 3 * share + ff // members + half), BF16)],
            )
            far = far + spread_group([far_later], away)[1:]
            ups_first = ups
            ups_came = flip(ups, plane_bits[0])

        def do_bundle():
            nonlocal bundle, cut, rows_came
            bundle = call(
                functools.partial(bundle_kernel, group_size),
                [shaped((2 * group_size * rows, width), BF16)],
                spot,
                *near,
                *far,
                name="bundle",
                smem=(0,),
                after=(downs_came,),
            )[0]
            rows_came = flip(bundle, 0)
            cut = max(LANES, 3 * share // 2 // LANES * LANES)

        def do_split():
            nonlocal down_far, down_m, grad_later, left, left_came, pair, pair_came, right, right_came, up_far
            left, right, pair, grad_later = call(
                functools.partial(split_kernel, cut),
                [
                    shaped((2, tall + EXTRA, cut), BF16),
                    shaped((2, tall + EXTRA, 3 * share - cut), BF16),
                    shaped(pair.shape, BF16),
                    shaped(grad_low.shape, BF16),
                ],
                in_block,
                flip(in_block, top_bit),
                pair,
                grad_low,
                name="split",
                after=(ups_came,),
            )
            left_came, right_came = flip(left, plane_bits[0]), flip(right, plane_bits[-1])
            if paired:
                pair_came = flip(pair, top_bit)
            else:
                up_far, down_far = flip(ups_first, top_bit), flip(down_weight, top_bit)[None]
            down_m = [grad_low] + spread_group([grad_later])[1:]

        def do_stack():
            nonlocal after, b, c, k, left, left_came, right, right_came
            for k, (b, c) in list(enumerate(zip(plane_bits, reversed(plane_bits), strict=True)))[1:]:
                after = (rows_came,) if k == 1 else ()
                left, right = stack(lay, left, left_came, right, right_came, *after)
                left_came, right_came = flip(left, b), flip(right, c)

        def do_vectors():
            nonlocal in_pieces, vecs
            in_pieces = (left, left_came, right, right_came)
            vecs = call(
                functools.partial(vector_kernel, lay),
                [shaped((16, width), F32)],
                spot,
                left,
                left_came,
                name="vectors",
                smem=(0,),
                away=(1, 2),
                scratch=[
                    pltpu.VMEM((2 * lay.planes * EXTRA, -(-lay.small // LANES) * LANES), BF16),
                    pltpu.SemaphoreType.DMA((2 * lay.planes,)),
                ],
            )[0]

        def do_join_up():
            nonlocal b, ups, ups_came
            for b in plane_bits[1:]:
                ups = join(lay, ups, ups_came)
                ups_came = flip(ups, b)

        def do_attend():
            nonlocal att_c, far_att, joint, key_bias, lse, near_att, normed_one, w_in, wide, x_all
            key_bias = jnp.where(valid[0] > 0.5, 0.0, MASKED).astype(F32).reshape(length, 1)
            near_att, far_att, joint, wide, lse, normed_one, x_all, w_in = attend(
                lay, spot, key_bias, vecs, near + far + [rows_came], in_pieces
            )
            far_att = [send(far_att, mirrored)]
            near_att = spread_group([near_att])
            att_c = [flip(near_att[0], 0)]

        def do_unpair():
            nonlocal down_far, down_far_came, up_far, up_far_came
            if paired:
                up_far, down_far = call(
                    unpair_kernel,
                    [shaped((1, up_tall, width), BF16), shaped((1, piece, width), BF16)],
                    pair_came,
                    name="unpair",
                    after=(ups_came, *down_m[1:]),
                )
            up_far_came, down_far_came = flip(up_far, plane_bits[0]), flip(down_far, plane_bits[-1])

        def do_rows_own():
            nonlocal out_shape, outs_c, outs_w
            out_shape = [shaped((lay.planes, tall, half), BF16)]
            outs_w = call(out_kernel_rows, out_shape, ups, ups_came, name="out_rows")
            outs_c = flip(outs_w[0], 0)

        def do_stack_far():
            nonlocal b, c, down_far, down_far_came, k, up_far, up_far_came
            for k, (b, c) in list(enumerate(zip(plane_bits, reversed(plane_bits), strict=True)))[1:]:
                up_far, down_far = stack(lay, up_far, up_far_came, down_far, down_far_came, att_c[0])
                up_far_came, down_far_came = flip(up_far, b), flip(down_far, c)

        def do_rows_far():
            nonlocal att_c, down_blocks, down_c, far_att, out_blocks, outs_far, up_blocks
            down_c = [flip(v, 0) for v in down_m]
            far_att = spread_group(far_att)
            att_c = att_c[:1] + [flip(v, 0) for v in near_att[1:] + far_att]
            outs_far = call(out_kernel_rows, out_shape, up_far, up_far_came, name="out_rows", after=(outs_c,))[0]
            out_blocks = (*outs_w, outs_far, outs_c, flip(outs_far, 0))
            up_blocks = (ups, ups_came, up_far, up_far_came)
            down_blocks = (downs, downs_came, down_far, down_far_came)

        def do_forward():
            nonlocal act, att_own, cuts_of, d_bias_up, dn_give, dn_keep, grad_pre, middle, normed_two, planes_down, reduce_group, top_shift, w_out
            (
                dn_keep,
                dn_give,
                middle,
                att_own,
                normed_two,
                act,
                grad_pre,
                d_bias_up,
                w_out,
            ) = forward_call(
                lay,
                spot,
                vecs,
                out_blocks,
                near_att + far_att + att_c + near + down_m + down_c + [rows_came],
                up_blocks + down_blocks,
            )

            def reduce_group(keep, came, slot):
                for k in reversed(range(len(group_bits))):
                    keep, give = fold(lay, spot, slot, k, 1, keep, came)
                    came = flip(give, group_bits[k])
                return keep, came

            planes_down = list(reversed(plane_bits))
            top_shift = bits_of(group_size)

            def cuts_of(lead, order):
                here, cuts = list(planes_down), []
                for b in order:
                    cuts.append((1, b, lead << here.index(b)))
                    here.remove(b)
                return cuts

        def do_fold_norm():
            nonlocal dn_came, dn_keep
            dn_keep, dn_came = reduce_group(dn_keep, flip(dn_give, 0), 4)

        def do_gradients():
            nonlocal down_came, down_give, down_keep, out_came, out_give, out_keep, up_came, up_give, up_keep
            up_keep, up_give, down_keep, down_give, out_keep, out_give = gradient_call(
                lay, spot, normed_two, act, grad_pre, down_m, down_c, down_blocks
            )
            up_came, down_came = flip(up_give, planes_down[0]), flip(down_give, plane_bits[0])
            out_came = flip(out_give, 0)

        def do_turn():
            nonlocal grad_branch, grad_middle, slope_give, slope_keep, sums_two
            slope_keep, slope_give, grad_middle, grad_branch, sums_two = turn_call(
                lay, spot, vecs, dn_keep, dn_came, middle, grad_low, w_out
            )

        def do_pick():
            nonlocal parts, pieces, r
            pieces = call(
                functools.partial(pick_kernel, lay),
                [shaped((rows, share), BF16)] * members,
                spot,
                slope_keep,
                flip(slope_give, 0),
                name="pick",
                smem=(0,),
            )
            parts = [pieces[0]]
            for r in range(1, members):
                parts.append(send(pieces[r], [(i, i ^ (r * nt)) for i in range(devices)]))

        def do_outer():
            nonlocal o_came, o_give, o_keep
            o_keep, o_give = call(
                outer_kernel,
                [shaped((width, width // 2), BF16)] * 2,
                spot,
                att_own,
                grad_branch,
                name="output_gradient",
                smem=(0,),
            )
            o_came = flip(o_give, 0)

        def do_out_fold():
            nonlocal out_came, out_keep
            out_keep, out_came = reduce_group(out_keep, out_came, 4)

        def do_o0():
            nonlocal next_out, o_came, o_keep, out_bits, out_cuts, out_steps
            out_cuts = [(4, k, 2) for k in reversed(range(len(group_bits)))]
            out_cuts += cuts_of(2, planes_down) + [(0, top_shift, 1)]
            out_bits = list(reversed(group_bits)) + planes_down + [top_bit]
            out_steps = iter(range(len(out_bits)))

            def next_out(keep, came, count=1):
                for _ in range(count):
                    k = next(out_steps)
                    keep, give = fold(lay, spot, *out_cuts[k], keep, came)
                    came = flip(give, out_bits[k])
                return keep, came

            o_keep, o_came = next_out(o_keep, o_came)

        def do_assemble():
            nonlocal slope
            slope = call(
                functools.partial(assemble_kernel, lay),
                [shaped((length, share), BF16)],
                spot,
                *parts,
                name="assemble",
                smem=(0,),
            )[0]

        def do_planes():
            nonlocal down_came, down_cuts, down_keep, k, next_planes, up_came, up_cuts, up_keep
            up_cuts, down_cuts = cuts_of(members, planes_down), cuts_of(2, plane_bits)

            def next_planes(k, up_keep, up_came, down_keep, down_came):
                up_keep, up_give, down_keep, down_give = two_fold(
                    lay, spot, (up_cuts[k], down_cuts[k]), up_keep, up_came, down_keep, down_came
                )
                return up_keep, flip(up_give, planes_down[k]), down_keep, flip(down_give, plane_bits[k])

            for k in range(1, len(plane_bits)):
                up_keep, up_came, down_keep, down_came = next_planes(
                    k, up_keep, up_came, down_keep, down_came
                )

        def do_attend_back():
            nonlocal grad_joint, joint_sum, left_came, left_give, left_keep, right_came, right_give, right_keep
            grad_joint, left_keep, left_give, right_keep, right_give, joint_sum = attend_back(
                lay, spot, key_bias, joint, wide, lse, normed_one, slope, cut
            )
            left_came, right_came = flip(left_give, planes_down[0]), flip(right_give, plane_bits[0])

        def do_top_pair():
            nonlocal down_give, down_keep, far_came, give, shape, up_give, up_keep
            if paired:
                shape = (up_keep.shape[0] // 2, up_keep.shape[1])
                up_keep, down_keep, give = call(
                    functools.partial(top_pair_kernel, top_shift),
                    [shaped(shape, BF16), shaped(shape, BF16), shaped((2,) + shape, BF16)],
                    spot,
                    up_keep,
                    up_came,
                    down_keep,
                    down_came,
                    name="top_pair",
                    smem=(0,),
                    after=(o_came,),
                )
                far_came = flip(give, top_bit)
            else:
                up_keep, up_give, down_keep, down_give = two_fold(
                    lay, spot, ((0, top_shift, 1),) * 2, up_keep, up_came, down_keep, down_came
                )
                far_came = (flip(up_give, top_bit), flip(down_give, top_bit))

        def do_input():
            nonlocal in_came, in_give, in_keep, sums, sums_came, sums_give
            in_keep, in_give, sums, sums_give = input_call(
                lay, spot, grad_joint, w_in, x_all, sums_two, joint_sum, d_bias_up
            )
            sums_came = flip(sums_give, planes_down[0])
            in_came = flip(in_give, 0)

        def do_lr():
            nonlocal k, left_came, left_cuts, left_give, left_keep, right_came, right_cuts, right_give, right_keep, sums
            left_cuts, right_cuts = cuts_of(members, planes_down), cuts_of(members, plane_bits)
            for k in range(1, len(plane_bits)):
                left_keep, left_give, right_keep, right_give, sums = sums_fold(
                    lay,
                    spot,
                    (left_cuts[k], right_cuts[k]),
                    left_keep,
                    left_came,
                    right_keep,
                    right_came,
                    sums,
                    sums_came,
                )
                left_came, right_came = flip(left_give, planes_down[k]), flip(right_give, plane_bits[k])

        def do_dn1():
            nonlocal in_came, in_keep
            in_keep, in_came = reduce_group(in_keep, in_came, 9)

        def do_o1():
            nonlocal o_came, o_keep
            o_keep, o_came = next_out(o_keep, o_came, len(group_bits))

        def do_layer():
            nonlocal layer_out
            layer_out = call(
                out_kernel,
                [shaped((rows, width), BF16)],
                vecs,
                middle,
                out_keep,
                out_came,
                name="layer_out",
            )[0]

        def do_top():
            nonlocal small, sums, tall, w_came, w_give, w_keep
            small = (SUM_ROWS, width)
            tall = left_keep.shape[0] // 2
            w_keep, w_give, sums = call(
                functools.partial(top_fold_kernel, top_shift),
                [
                    shaped((tall, 3 * share), BF16),
                    shaped((tall + sum_rows(width, 3 * share), 3 * share), BF16),
                    shaped(small, F32),
                ],
                spot,
                left_keep,
                left_came,
                right_keep,
                right_came,
                sums,
                name="top_fold",
                smem=(0,),
            )
            w_came = flip(w_give, top_bit)

        def do_add():
            nonlocal in_sum, sent
            in_sum = call(add_kernel, [shaped((rows, width), BF16)], in_keep, in_came, name="add")[0]
            sent = send(in_sum, across)

        def do_o2():
            nonlocal o_came, o_keep
            o_keep, o_came = next_out(o_keep, o_came, len(plane_bits) - 1)

        def do_d_down():
            nonlocal d_down
            d_down = call(
                add_kernel,
                [shaped((piece, width), F32)],
                down_keep,
                far_came if paired else far_came[1],
                name="add",
            )[0]

        def do_home0():
            nonlocal columns, down_came, home_outs, home_steps, sums, tall, up_came, w_came, w_give, w_keep
            up_came, down_came = (far_came, far_came) if paired else far_came
            columns = 3 * share + ff // members
            home_steps = [(4, k, b) for k, b in reversed(list(enumerate(group_bits)))] + [(2, 0, 0)]

            def home_outs():
                rows_here = max(tall, 16)
                return [
                    shaped((rows_here, columns), BF16),
                    shaped((rows_here + sum_rows(width, columns), columns), BF16),
                    shaped(small, F32),
                ]

            tall //= 2
            w_keep, w_give, sums = call(
                functools.partial(home_first_kernel, *home_steps[0][:2]),
                home_outs(),
                spot,
                w_keep,
                w_came,
                up_keep,
                up_came,
                sums,
                name="home_first",
                smem=(0,),
            )
            w_came = flip(w_give, home_steps[0][2])

        def do_o3():
            nonlocal o_came, o_keep
            o_keep, o_came = next_out(o_keep, o_came)

        def do_last():
            nonlocal input_gradient
            input_gradient = call(
                last_kernel,
                [shaped((rows, width), BF16)],
                spot,
                vecs,
                in_keep,
                in_came,
                sent,
                own,
                grad_middle,
                name="input_gradient",
                smem=(0,),
            )[0]

        def do_home1():
            nonlocal b, columns, final, outs, shift, slot, sums, tall, w_came, w_give, w_keep
            for slot, shift, b in home_steps[1:]:
                tall //= 2
                columns *= 2
                outs = home_outs()
                final = (o_keep, o_came) if b == 0 else ()
                if final:
                    outs = [shaped((v.shape[0], columns + width // 2), BF16) for v in outs[:2]] + outs[2:]
                w_keep, w_give, sums = call(
                    functools.partial(home_next_kernel, slot, shift),
                    outs,
                    spot,
                    w_keep,
                    w_came,
                    sums,
                    *final,
                    name="home_next",
                    smem=(0,),
                )
                w_came = flip(w_give, b)

        def do_home_last():
            nonlocal d_in, d_out, d_up, vectors
            d_in, d_up, d_out, *vectors = call(
                functools.partial(home_last_kernel, lay),
                [shaped((each, 3 * width), F32), shaped((each, ff), F32), shaped((each, width), F32)]
                + [shaped((1, each), F32)] * 8
                + [shaped((1, piece), F32)],
                spot,
                w_keep,
                w_came,
                sums,
                name="home_last",
                smem=(0,),
                scratch=[pltpu.VMEM((SUM_ROWS, width), F32)],
            )
            vectors = [v.reshape(-1) for v in vectors]

        def do_relay():
            nonlocal far_att
            far_att = call(
                copy_kernel, [shaped(far_att[0].shape, BF16)], far_att[0], name="relay", after=tuple(near_att[1:])
            )

        steps = {
            "pack": do_pack,
            "mask": do_mask,
            "trade": do_trade,
            "join_down": do_join_down,
            "settle": do_settle,
            "bundle": do_bundle,
            "split": do_split,
            "stack": do_stack,
            "vectors": do_vectors,
            "join_up": do_join_up,
            "attend": do_attend,
            "unpair": do_unpair,
            "rows_own": do_rows_own,
            "stack_far": do_stack_far,
            "rows_far": do_rows_far,
            "forward": do_forward,
            "fold_norm": do_fold_norm,
            "gradients": do_gradients,
            "turn": do_turn,
            "pick": do_pick,
            "outer": do_outer,
            "out_fold": do_out_fold,
            "o0": do_o0,
            "assemble": do_assemble,
            "planes": do_planes,
            "attend_back": do_attend_back,
            "top_pair": do_top_pair,
            "input": do_input,
            "lr": do_lr,
            "dn1": do_dn1,
            "o1": do_o1,
            "layer": do_layer,
            "top": do_top,
            "add": do_add,
            "o2": do_o2,
            "d_down": do_d_down,
            "home0": do_home0,
            "o3": do_o3,
            "last": do_last,
            "home1": do_home1,
            "home_last": do_home_last,
            "relay": do_relay,
        }
        for name in PLAN:
            lay.order.step = name
            known = {
                "near": near,
                "far": far,
                "downs_came": downs_came,
                "ups_came": ups_came,
                "rows_came": rows_came,
                "pair_came": pair_came,
                "down_m": down_m,
                "down_c": down_c,
                "near_att": near_att,
                "far_att": far_att,
                "att_c": att_c,
                "outs_c": outs_c,
                "up_far_came": up_far_came,
                "down_far_came": down_far_came,
                "up_came": up_came,
                "down_came": down_came,
                "out_came": out_came,
                "o_came": o_came,
                "far_came": far_came,
                "sums_came": sums_came,
                "in_came": in_came,
            }
            lay.order.waits = tuple(
                v for w in WAITS.get(name, ()) for v in jax.tree.leaves(known[w])
            )
            steps[name]()
        return (
            layer_out[None],
            input_gradient[None],
            vectors[0],
            vectors[1],
            d_in,
            vectors[2],
            vectors[3],
            d_out,
            vectors[4],
            vectors[5],
            vectors[6],
            d_up,
            vectors[8],
            d_down,
            vectors[7],
        )

    vector, matrix = P(AXES), P(AXES, None)
    tokens = P("batch", "blk", None)
    return jax.shard_map(
        local,
        mesh=mesh,
        in_specs=(
            tokens,
            P("batch", None),
            P("batch"),
            vector,
            vector,
            matrix,
            vector,
            vector,
            matrix,
            vector,
            vector,
            vector,
            matrix,
            vector,
            matrix,
            vector,
            tokens,
        ),
        out_specs=(
            tokens,
            tokens,
            vector,
            vector,
            matrix,
            vector,
            vector,
            matrix,
            vector,
            vector,
            vector,
            matrix,
            vector,
            matrix,
            vector,
        ),
        check_vma=False,
    )
```
